128 devices in a mesh: row: 16 (over y, z), col: 8 (over x, core).
Axes of the slice: x: 4, y: 4, z: 4, core: 2. Of those that a mesh axis runs over, the one named last changes fastest.
Arguments:
- frontal: float32 [16384, 24576], P('row', 'col'), may hold values from -0.0390625 to 0.0390625
- sketch: float32 [24576, 512], P(('col', 'row')), may hold values from -6 to 6
- leaf_ranks: int32 [128], replicated, may hold values from 48 to 96, as said below
- leaf_pivots: int32 [128, 128], replicated, may hold values from 0 to 127, each once within a row
- mid_ranks: int32 [64], replicated, may hold values from 48 to 96, as said below
- mid_pivots: int32 [64, 192], replicated, may hold values from 0 to 191, as said below
- top_ranks: int32 [32], replicated, may hold values from 48 to 96, as said below
- top_pivots: int32 [32, 192], replicated, may hold values from 0 to 191, as said below
Outputs:
- leaf_interp: float32 [128, 96, 128], P(('row', 'col'))
- mid_interp: float32 [128, 96, 192], P(('row', 'col'))
- top_interp: float32 [128, 96, 192], P(('row', 'col'))
- top_rows: float32 [128, 96, 512], P(('row', 'col'))
The draws below stay inside these ranges and needn't reach their ends.
Inputs may be any that keep to these rules, and one draw needn't show every extreme that they name: `leaf_ranks`: some leaf has rank exactly 96. `mid_ranks`: some parent has rank exactly 96. `top_ranks`: some grandparent has rank exactly 96. `mid_pivots`: each row is a permutation of the slots; slot s < 96 holds row s of the left child's skeleton and slot 96 + s row s of the right child's; the first mid_ranks[j] entries of row j name only slots below the children's ranks. `top_pivots`: each row is a permutation of the slots, built like mid_pivots over the two parents' skeletons with top_ranks.
All inputs are finite; a program needn't handle non-finite values.
Results may differ from the reference program's by a relative error of at most 0.0003.
Values sent between devices are 32-bit elements; how exact they have to be, the bound alone decides.
No kernel may reach another device: no remote copies, remote signals or barrier semaphores. Data moves between devices by JAX's collectives and lax.ppermute only.
A program may use at most 64 MiB of HBM per device.

```python
import jax
import jax.numpy as jnp
from jax import lax

ORDER = 24576
SAMPLES = 512
LEAF = 128
KMAX = 96
KMIN = 48
ROWS = 16384
LEAVES = 128


def rank_table(key):
    tables = []
    for level_tag, node_count in ((11, LEAVES), (12, LEAVES // 2), (13, LEAVES // 4)):
        subkey = jax.random.fold_in(key, level_tag)
        values = jax.random.randint(jax.random.fold_in(subkey, 1), (node_count,), KMIN, KMAX + 1)
        top_place = jax.random.randint(jax.random.fold_in(subkey, 2), (), 0, node_count)
        values = values.at[top_place].set(KMAX)
        tables.append(values.astype(jnp.int32))
    return tables


def shuffle_one(subkey):
    return jax.random.permutation(subkey, 2 * KMAX).astype(jnp.int32)


def parent_pivots(key, child_ranks):
    node_count = child_ranks.shape[0] // 2
    left_ranks = child_ranks[0::2][:, None]
    right_ranks = child_ranks[1::2][:, None]
    slot_ids = jnp.arange(2 * KMAX, dtype=jnp.int32)[None, :]
    usable = jnp.where(slot_ids < KMAX, slot_ids < left_ranks, slot_ids - KMAX < right_ranks)
    key_list = jax.random.split(key, node_count)
    shuffled = jax.vmap(shuffle_one)(key_list)
    order_score = shuffled + jnp.where(usable, 0, 2 * KMAX).astype(jnp.int32)
    return jnp.argsort(order_score, axis=1, stable=True).astype(jnp.int32)


def draw_leaf_ranks(key, part):
    tables = rank_table(key)
    return tables[0]


def draw_mid_ranks(key, part):
    tables = rank_table(key)
    return tables[1]


def draw_top_ranks(key, part):
    tables = rank_table(key)
    return tables[2]


def draw_mid_pivots(key, part):
    tables = rank_table(key)
    key = jax.random.fold_in(key, 6)
    return parent_pivots(key, tables[0])


def draw_top_pivots(key, part):
    tables = rank_table(key)
    key = jax.random.fold_in(key, 7)
    return parent_pivots(key, tables[1])


def levels(own_key, extent, shards, least, high):
    def one(position, shards_of):
        heights = jax.random.uniform(jax.random.fold_in(jax.random.fold_in(own_key, 6), position), (shards_of,), jnp.float32, least / len(shards), high / len(shards))
        return jnp.repeat(jnp.exp(heights), extent[position] // shards_of).reshape((-1,) + (1,) * (len(extent) - position - 1))

    gain = one(*shards[0])
    for cut in shards[1:]:
        gain = gain * one(*cut)
    return gain


def centred(key, extent, deviation, reach, shards=(), kind=jnp.bfloat16):
    array = jax.random.normal(key, extent, jnp.float32) * deviation
    if len(shards) > 0:
        array = levels(key, extent, shards, -0.22, 0.18) * array
    return jnp.clip(array, min=-reach, max=reach).astype(kind)


def setup_inputs(seed: int = 0) -> dict:
    key_of = jax.random.split(jax.random.key(seed), 9)
    return {
        "frontal": centred(key_of[0], (ROWS, ORDER), ORDER ** -0.5, 0.0390625, ((0, 16), (1, 8)), jnp.float32),
        "sketch": centred(key_of[1], (ORDER, SAMPLES), 1.0, 6.0, ((0, 128),), jnp.float32),
        "leaf_ranks": draw_leaf_ranks(jax.random.fold_in(key_of[8], 71), 0),
        "leaf_pivots": jax.vmap(lambda own: jax.random.permutation(own, LEAF))(jax.random.split(key_of[3], LEAVES)).reshape((LEAVES, LEAF)).astype(jnp.int32),
        "mid_ranks": draw_mid_ranks(jax.random.fold_in(key_of[8], 71), 0),
        "mid_pivots": draw_mid_pivots(jax.random.fold_in(key_of[8], 71), 0),
        "top_ranks": draw_top_ranks(jax.random.fold_in(key_of[8], 71), 0),
        "top_pivots": draw_top_pivots(jax.random.fold_in(key_of[8], 71), 0),
    }


def interpolate(candidates, pivots, skeleton_rank):
    slot_ids = jnp.arange(KMAX)
    keep_mask = (slot_ids < skeleton_rank).astype(candidates.dtype)
    skeleton = jnp.take(candidates, pivots[:KMAX], axis=0) * keep_mask[:, None]
    gram_matrix = jnp.dot(skeleton, skeleton.T, precision=lax.Precision.HIGHEST) / SAMPLES
    gram_matrix = gram_matrix + jnp.diag(1.0 - keep_mask)
    cross_terms = jnp.dot(skeleton, candidates.T, precision=lax.Precision.HIGHEST) / SAMPLES
    factor = jnp.linalg.cholesky(gram_matrix)
    solved = jax.scipy.linalg.cho_solve((factor, True), cross_terms)
    return (solved, skeleton)

def reference(frontal, sketch, leaf_ranks, leaf_pivots, mid_ranks, mid_pivots, top_ranks, top_pivots):
    samples_all = jnp.dot(frontal, sketch, precision=lax.Precision.HIGHEST)
    leaf_rows = samples_all.reshape(LEAVES, LEAF, SAMPLES)
    leaf_solved, leaf_skeleton = jax.vmap(interpolate)(leaf_rows, leaf_pivots, leaf_ranks)
    mid_rows = leaf_skeleton.reshape(LEAVES // 2, 2 * KMAX, SAMPLES)
    mid_solved, mid_skeleton = jax.vmap(interpolate)(mid_rows, mid_pivots, mid_ranks)
    top_rows_in = mid_skeleton.reshape(LEAVES // 4, 2 * KMAX, SAMPLES)
    top_solved, top_skeleton = jax.vmap(interpolate)(top_rows_in, top_pivots, top_ranks)
    return (leaf_solved, jnp.repeat(mid_solved, 2, axis=0), jnp.repeat(top_solved, 4, axis=0), jnp.repeat(top_skeleton, 4, axis=0))
```

```python
import functools

import jax
import jax.numpy as jnp
from jax import lax
from jax.experimental import pallas as pl
from jax.experimental.pallas import tpu as pltpu
from jax.sharding import PartitionSpec as P

SAMPLES = 512
KMAX = 96
SIDE = 4
LEAF = 128
CHUNKS = 2
K_STEPS = 4


def from_partner(value, axis, apart):
    mask = 2**apart
    pairs = [(source, source ^ mask) for source in range(lax.axis_size(axis))]
    return lax.ppermute(value, axis, pairs)


def pick_entry(table, position):
    return lax.dynamic_index_in_dim(table, position, 0, keepdims=False)


def shift_x(value, dx):
    pairs = []
    for x in range(SIDE):
        for core in range(2):
            pairs.append((x * 2 + core, (x + dx) % SIDE * 2 + core))
    return lax.ppermute(value, "col", pairs)


FIRST, SECOND = 1, 3
ROUTES = (
    (("y", FIRST), ("y", SECOND), ("z", FIRST), ("z", SECOND)),
    (("y", SECOND), ("y", FIRST), ("z", SECOND), ("z", FIRST)),
    (("z", FIRST), ("z", SECOND), ("y", FIRST), ("y", SECOND)),
    (("z", SECOND), ("z", FIRST), ("y", SECOND), ("y", FIRST)),
)


def row_mask(step):
    axis, mask = step
    return mask * SIDE if axis == "y" else mask


def from_row(value, step):
    mask = row_mask(step)
    return lax.ppermute(value, "row", [(source, source ^ mask) for source in range(SIDE * SIDE)])


def origins(route):
    masks = [0]
    for step in route:
        masks += [mask ^ row_mask(step) for mask in masks]
    return masks


def gather_parts(sketch):
    depth = sketch.shape[0] // len(ROUTES)
    stacks = [sketch[None, part * depth : (part + 1) * depth] for part in range(len(ROUTES))]
    for at in range(3):
        received = [from_row(stack, route[at]) for stack, route in zip(stacks, ROUTES)]
        stacks = [jnp.concatenate(pair, 0) for pair in zip(stacks, received)]
    width = SAMPLES // CHUNKS
    halves = []
    for chunk in range(CHUNKS):
        own = [stack[:, :, chunk * width : (chunk + 1) * width] for stack in stacks]
        halves.append(own + [from_row(value, route[3]) for value, route in zip(own, ROUTES)])
    return halves


def split_kernel(value_ref, high_ref, low_ref):
    value = value_ref[...]
    high = value.astype(jnp.bfloat16)
    high_ref[...] = high
    low_ref[...] = (value - high.astype(jnp.float32)).astype(jnp.bfloat16)


def split(value):
    rows, order = value.shape
    block = pl.BlockSpec((LEAF, order), lambda i: (i, 0))
    return pl.pallas_call(
        split_kernel,
        out_shape=[jax.ShapeDtypeStruct(value.shape, jnp.bfloat16)] * 2,
        grid=(rows // LEAF,),
        in_specs=[block],
        out_specs=[block] * 2,
        compiler_params=pltpu.CompilerParams(vmem_limit_bytes=16 * 2**20),
        cost_estimate=pl.CostEstimate(
            flops=4 * rows * order, bytes_accessed=8 * rows * order, transcendentals=0
        ),
        name="split",
    )(value)


def product_kernel(place_ref, a_high, a_low, *refs):
    parts = len(ROUTES)
    pieces = refs[: 2 * parts]
    other_ref, own_ref, high, low, total = refs[2 * parts :]
    step = pl.program_id(0)

    @pl.when(step == 0)
    def _():
        depth = pieces[0].shape[1]
        for part, route in enumerate(ROUTES):
            masks = origins(route)
            for at, mask in enumerate(masks):
                source = pieces[part + parts * (at // 8)]
                block = jnp.bitwise_xor(place_ref[1], mask)
                start = pl.multiple_of((block * parts + part) * depth, depth)
                value = source[at % 8]
                top = value.astype(jnp.bfloat16)
                high[pl.ds(start, depth), :] = top
                low[pl.ds(start, depth), :] = (value - top.astype(jnp.float32)).astype(
                    jnp.bfloat16
                )

    k_rows = a_high.shape[-1]
    rows = pl.ds(pl.multiple_of(step * k_rows, 256), k_rows)
    left, right = a_high[...], high[rows, :]
    result = jnp.dot(
        jnp.concatenate([left, left, a_low[...]], 1),
        jnp.concatenate([right, low[rows, :], right], 0),
        preferred_element_type=jnp.float32,
    )

    @pl.when(step == 0)
    def _():
        total[...] = result.reshape(total.shape)

    @pl.when(step > 0)
    def _():
        total[...] += result.reshape(total.shape)

    @pl.when(step == K_STEPS - 1)
    def _():
        core, x = place_ref[0], place_ref[2]
        for away in range(SIDE):
            chip = lax.rem(x + away, SIDE)
            own_ref[away] = total[chip * 2 + core]
            other_ref[away] = total[chip * 2 + 1 - core]


def chunk_product(high, low, pieces, place):
    rows, order = high.shape
    width = pieces[0].shape[-1]
    k_rows = order // K_STEPS
    leaves = rows // LEAF // 2
    left = pl.BlockSpec((rows, k_rows), lambda k, place: (0, k))
    out = jax.ShapeDtypeStruct((leaves, LEAF, width), jnp.float32)
    return pl.pallas_call(
        product_kernel,
        out_shape=[out] * 2,
        grid_spec=pltpu.PrefetchScalarGridSpec(
            num_scalar_prefetch=1,
            grid=(K_STEPS,),
            in_specs=[left] * 2 + [pl.BlockSpec(memory_space=pltpu.VMEM)] * len(pieces),
            out_specs=[pl.BlockSpec(memory_space=pltpu.VMEM)] * 2,
            scratch_shapes=[
                pltpu.VMEM((order, width), jnp.bfloat16),
                pltpu.VMEM((order, width), jnp.bfloat16),
                pltpu.VMEM((2 * leaves, LEAF, width), jnp.float32),
            ],
        ),
        compiler_params=pltpu.CompilerParams(vmem_limit_bytes=36 * 2**20),
        cost_estimate=pl.CostEstimate(
            flops=6 * rows * order * width,
            bytes_accessed=4 * (rows * order + order * width + rows * width),
            transcendentals=0,
        ),
        name="chunk_product",
    )(place, high, low, *pieces)


def sum_over_col(other, own):
    core_sum = own + from_partner(other, "col", 0)
    return [core_sum[0]] + [shift_x(core_sum[step % SIDE], step) for step in (1, -1, 2)]


BLOCK = 8
NODES = 3


def lane_of(value, lane):
    return jnp.broadcast_to(value[:, lane : lane + 1], value.shape)


def invert_pivot(entry):
    def at(i, j):
        return entry[max(i, j)][min(i, j)]

    def put(i, j, value):
        entry[max(i, j)][min(i, j)] = value

    for p in range(0, BLOCK, 2):
        q = p + 1
        a, b, c = at(p, p), at(q, p), at(q, q)
        scale = 1.0 / (a * c - b * b)
        w_pp, w_pq, w_qq = c * scale, -b * scale, a * scale
        rest = [i for i in range(BLOCK) if i not in (p, q)]
        first = {i: at(i, p) for i in rest}
        second = {i: at(i, q) for i in rest}
        left = {i: w_pp * first[i] + w_pq * second[i] for i in rest}
        right = {i: w_pq * first[i] + w_qq * second[i] for i in rest}
        for i in rest:
            for j in rest:
                if j <= i:
                    put(i, j, at(i, j) - (left[i] * first[j] + right[i] * second[j]))
        for i in rest:
            put(i, p, left[i])
            put(i, q, right[i])
        put(p, p, -w_pp)
        put(q, p, -w_pq)
        put(q, q, -w_qq)
    return at


def sweep(tiles, rows_scratch, new_scratch):
    lanes = lax.broadcasted_iota(jnp.int32, (BLOCK, 128), 1)
    count = KMAX // BLOCK
    for block in range(count):
        at_lane = block * BLOCK
        slot = block % 2
        inside = (lanes >= at_lane) & (lanes < at_lane + BLOCK)
        for node in range(NODES):
            rows_scratch[slot, node * BLOCK : (node + 1) * BLOCK, :] = tiles[node][block]
        rows = [rows_scratch[slot, pl.ds(k, BLOCK, stride=BLOCK), :] for k in range(BLOCK)]
        entry = [[lane_of(rows[k], at_lane + i) for i in range(k + 1)] for k in range(BLOCK)]
        at = invert_pivot(entry)
        wide = [
            jnp.where(lanes == at_lane + k, 1.0, jnp.where(inside, 0.0, -rows[k]))
            for k in range(BLOCK)
        ]
        for k in range(BLOCK):
            total = at(k, 0) * wide[0]
            for i in range(1, BLOCK):
                total = total + at(k, i) * wide[i]
            new_scratch[slot, pl.ds(k, BLOCK, stride=BLOCK), :] = total
        for node in range(NODES):
            new_rows = [
                jnp.broadcast_to(
                    new_scratch[slot, node * BLOCK + k : node * BLOCK + k + 1, :], (BLOCK, 128)
                )
                for k in range(BLOCK)
            ]
            for t in range(count):
                if t == block:
                    continue
                old = tiles[node][t]
                value = jnp.where(inside, 0.0, old)
                for k in range(BLOCK):
                    value = value - lane_of(old, at_lane + k) * new_rows[k]
                tiles[node][t] = value
            tiles[node][block] = new_scratch[slot, node * BLOCK : (node + 1) * BLOCK, :]
    return tiles


def invert_all(matrices, rows_scratch, new_scratch):
    count = KMAX // BLOCK
    lanes = lax.broadcasted_iota(jnp.int32, (BLOCK, 128), 1)
    sublanes = lax.broadcasted_iota(jnp.int32, (BLOCK, 128), 0)
    rows_scratch[...] = jnp.zeros_like(rows_scratch)
    all_tiles, all_down, all_across = [], [], []
    for matrix in matrices:
        wide = jnp.concatenate([matrix, jnp.zeros((KMAX, 128 - KMAX), jnp.float32)], 1)
        tiles = [wide[t * BLOCK : (t + 1) * BLOCK] for t in range(count)]
        on_diagonal = [
            jnp.where(lanes == sublanes + t * BLOCK, tiles[t], 0.0) for t in range(count)
        ]
        down = [lax.rsqrt(jnp.sum(part, axis=1, keepdims=True)) for part in on_diagonal]
        line = functools.reduce(jnp.add, on_diagonal)
        line = jnp.sum(line, axis=0, keepdims=True)
        across = lax.rsqrt(jnp.where(lanes[:1] < KMAX, line, 1.0))
        all_tiles.append([tiles[t] * down[t] * across for t in range(count)])
        all_down.append(down)
        all_across.append(across)
    all_tiles = sweep(all_tiles, rows_scratch, new_scratch)
    inverses = []
    for tiles, down, across in zip(all_tiles, all_down, all_across):
        scaled = [-(tiles[t] * down[t] * across) for t in range(count)]
        inverses.append(jnp.concatenate(scaled, 0)[:, :KMAX])
    return inverses


def select_rows(source, pivots_ref, node, rank, target, target_at):
    for row in range(KMAX):
        picked = source[pl.ds(pivots_ref[node, row], 1), :]
        target[target_at + row : target_at + row + 1, :] = jnp.where(row < rank, picked, 0.0)


def leaf_kernel(info_ref, pivots_ref, *refs):
    parts, (rows_ref, skeleton_ref) = refs[:-2], refs[-2:]
    each = len(parts) // CHUNKS
    wide = SAMPLES // CHUNKS
    for chunk in range(CHUNKS):
        group = parts[chunk * each : (chunk + 1) * each]
        total = functools.reduce(jnp.add, [part[...] for part in group])
        rows_ref[:, chunk * wide : (chunk + 1) * wide] = total
    select_rows(rows_ref, pivots_ref, 0, info_ref[2], skeleton_ref, 0)


def mid_kernel(info_ref, pivots_ref, own_ref, other_ref, rows_ref, skeleton_ref):
    own_at = pl.multiple_of(info_ref[0] * KMAX, KMAX)
    other_at = pl.multiple_of((1 - info_ref[0]) * KMAX, KMAX)
    rows_ref[pl.ds(own_at, KMAX), :] = own_ref[...]
    rows_ref[pl.ds(other_at, KMAX), :] = other_ref[...]
    select_rows(rows_ref, pivots_ref, 1, info_ref[3], skeleton_ref, 0)


def top_kernel(
    info_ref, pivots_ref, leaf_rows, leaf_skeleton, mid_rows, mid_skeleton, cousin_ref,
    leaf_out, mid_out, top_out, rows_out, top_rows, rows_scratch, new_scratch,
):
    own_at = pl.multiple_of(info_ref[1] * KMAX, KMAX)
    other_at = pl.multiple_of((1 - info_ref[1]) * KMAX, KMAX)
    top_rows[pl.ds(own_at, KMAX), :] = mid_skeleton[...]
    top_rows[pl.ds(other_at, KMAX), :] = cousin_ref[...]
    select_rows(top_rows, pivots_ref, 2, info_ref[4], rows_out, 0)
    row_ids = lax.broadcasted_iota(jnp.int32, (KMAX, KMAX), 0)
    column_ids = lax.broadcasted_iota(jnp.int32, (KMAX, KMAX), 1)
    dot = functools.partial(
        lax.dot_general,
        dimension_numbers=(((1,), (1,)), ((), ())),
        precision=lax.Precision.HIGHEST,
        preferred_element_type=jnp.float32,
    )
    grams, crosses = [], []
    for node, (rows, skeleton) in enumerate(
        ((leaf_rows, leaf_skeleton), (mid_rows, mid_skeleton), (top_rows, rows_out))
    ):
        chosen = skeleton[...]
        gram = dot(chosen, chosen) * (1.0 / SAMPLES)
        empty = (row_ids == column_ids) & (row_ids >= info_ref[2 + node])
        grams.append(gram + jnp.where(empty, 1.0, 0.0))
        crosses.append(dot(rows[...], chosen) * (1.0 / SAMPLES))
    inverses = invert_all(grams, rows_scratch, new_scratch)
    for inverse, cross, out in zip(inverses, crosses, (leaf_out, mid_out, top_out)):
        out[...] = dot(inverse, cross)


def vmem_call(kernel, outs, scratch, name):
    in_vmem = pl.BlockSpec(memory_space=pltpu.VMEM)

    def call(info, pivots, *arrays):
        return pl.pallas_call(
            kernel,
            out_shape=[jax.ShapeDtypeStruct(shape, jnp.float32) for shape in outs],
            in_specs=[pl.BlockSpec(memory_space=pltpu.SMEM)] * 2 + [in_vmem] * len(arrays),
            out_specs=[in_vmem] * len(outs),
            scratch_shapes=scratch,
            compiler_params=pltpu.CompilerParams(vmem_limit_bytes=32 * 2**20),
            name=name,
        )(info, pivots, *arrays)

    return call


def on_device(
    frontal, sketch, leaf_ranks, leaf_pivots, mid_ranks, mid_pivots, top_ranks, top_pivots
):
    col_count = lax.axis_size("col")
    col_index = lax.axis_index("col")
    row_index = lax.axis_index("row")
    leaf_index = row_index * col_count + col_index
    place = jnp.stack([col_index % 2, row_index, col_index // 2]).astype(jnp.int32)
    nodes = (leaf_index, leaf_index // 2, leaf_index // 4)
    ranks = [
        pick_entry(table, node)
        for table, node in zip((leaf_ranks, mid_ranks, top_ranks), nodes)
    ]
    info = jnp.stack([col_index % 2, col_index // 2 % 2] + ranks).astype(jnp.int32)
    pivots = jnp.stack(
        [
            pick_entry(table, node)[:KMAX]
            for table, node in zip((leaf_pivots, mid_pivots, top_pivots), nodes)
        ]
    )
    high, low = split(frontal)
    high, low, info, pivots = lax.optimization_barrier((high, low, info, pivots))
    parts = []
    for pieces in gather_parts(sketch):
        parts += sum_over_col(*chunk_product(high, low, pieces, place))
    skeleton_shape, pair_shape = (KMAX, SAMPLES), (2 * KMAX, SAMPLES)
    leaf_rows, leaf_skeleton = vmem_call(
        leaf_kernel, [(LEAF, SAMPLES), skeleton_shape], [], "leaf_rows"
    )(info, pivots, *parts)
    sibling = from_partner(leaf_skeleton, "col", 0)
    mid_rows, mid_skeleton = vmem_call(
        mid_kernel, [pair_shape, skeleton_shape], [], "mid_rows"
    )(info, pivots, leaf_skeleton, sibling)
    cousin = from_partner(mid_skeleton, "col", 1)
    scratch = [pltpu.VMEM(pair_shape, jnp.float32)]
    scratch += [pltpu.VMEM((2, BLOCK * BLOCK, 128), jnp.float32)] * 2
    outs = vmem_call(
        top_kernel,
        [(KMAX, LEAF), (KMAX, 2 * KMAX), (KMAX, 2 * KMAX), skeleton_shape],
        scratch,
        "interpolation",
    )(info, pivots, leaf_rows, leaf_skeleton, mid_rows, mid_skeleton, cousin)
    return tuple(out[None] for out in outs)


def solution(mesh):
    return jax.shard_map(
        on_device,
        mesh=mesh,
        in_specs=(P("row", "col"), P(("col", "row"), None), P(), P(), P(), P(), P(), P()),
        out_specs=(
            P(("row", "col"), None, None),
            P(("row", "col"), None, None),
            P(("row", "col"), None, None),
            P(("row", "col"), None, None),
        ),
        check_vma=False,
    )
```

```python
import functools

import jax
import jax.numpy as jnp
from jax import lax
from jax.experimental import pallas as pl
from jax.experimental.pallas import tpu as pltpu
from jax.sharding import PartitionSpec as P

SAMPLES = 512
KMAX = 96
SIDE = 4
LEAF = 128
WIDTHS = (256, 256)
K_STEPS = 4


def from_partner(value, axis, apart):
    mask = 2**apart
    pairs = [(source, source ^ mask) for source in range(lax.axis_size(axis))]
    return lax.ppermute(value, axis, pairs)


def pick_entry(table, position):
    return lax.dynamic_index_in_dim(table, position, 0, keepdims=False)


FIRST, SECOND = 1, 3
ROUTES = (
    (("y", FIRST), ("y", SECOND), ("z", FIRST), ("z", SECOND)),
    (("y", SECOND), ("y", FIRST), ("z", SECOND), ("z", FIRST)),
    (("z", FIRST), ("z", SECOND), ("y", FIRST), ("y", SECOND)),
    (("z", SECOND), ("z", FIRST), ("y", SECOND), ("y", FIRST)),
)


def row_mask(step):
    axis, mask = step
    return mask * SIDE if axis == "y" else mask


def from_row(value, step):
    mask = row_mask(step)
    return lax.ppermute(value, "row", [(source, source ^ mask) for source in range(SIDE * SIDE)])


def origins(route):
    masks = [0]
    for step in route:
        masks += [mask ^ row_mask(step) for mask in masks]
    return masks


def gather_parts(sketch, ready):
    depth = sketch.shape[0] // len(ROUTES)
    stacks = [sketch[None, part * depth : (part + 1) * depth] for part in range(len(ROUTES))]
    for at in range(3):
        received = [from_row(stack, route[at]) for stack, route in zip(stacks, ROUTES)]
        if at == 0:
            received = lax.optimization_barrier(received)
        stacks = [jnp.concatenate(pair, 0) for pair in zip(stacks, received)]
    stacks, ready = lax.optimization_barrier((stacks, ready))
    chunks, start = [], 0
    for width in WIDTHS:
        own = [stack[:, :, start : start + width] for stack in stacks]
        chunks.append(own + [from_row(value, route[3]) for value, route in zip(own, ROUTES)])
        start += width
    return chunks, ready


def split_kernel(value_ref, high_ref, low_ref):
    value = value_ref[...]
    high = value.astype(jnp.bfloat16)
    high_ref[...] = high
    low_ref[...] = (value - high.astype(jnp.float32)).astype(jnp.bfloat16)


def split(value):
    rows, order = value.shape
    block = pl.BlockSpec((LEAF, order), lambda i: (i, 0))
    return pl.pallas_call(
        split_kernel,
        out_shape=[jax.ShapeDtypeStruct(value.shape, jnp.bfloat16)] * 2,
        grid=(rows // LEAF,),
        in_specs=[block],
        out_specs=[block] * 2,
        compiler_params=pltpu.CompilerParams(vmem_limit_bytes=16 * 2**20),
        cost_estimate=pl.CostEstimate(
            flops=4 * rows * order, bytes_accessed=8 * rows * order, transcendentals=0
        ),
        name="split",
    )(value)


def product_kernel(place_ref, a_high, a_low, *refs):
    parts = len(ROUTES)
    pieces = refs[: 2 * parts]
    other_ref, own_ref, high, low, total = refs[2 * parts :]
    step = pl.program_id(0)

    @pl.when(step == 0)
    def _():
        depth = pieces[0].shape[1]
        for part, route in enumerate(ROUTES):
            masks = origins(route)
            for at, mask in enumerate(masks):
                source = pieces[part + parts * (at // 8)]
                block = jnp.bitwise_xor(place_ref[1], mask)
                start = pl.multiple_of((block * parts + part) * depth, depth)
                value = source[at % 8]
                top = value.astype(jnp.bfloat16)
                high[pl.ds(start, depth), :] = top
                low[pl.ds(start, depth), :] = (value - top.astype(jnp.float32)).astype(
                    jnp.bfloat16
                )

    k_rows = a_high.shape[-1]
    rows = pl.ds(pl.multiple_of(step * k_rows, 256), k_rows)
    left, right = a_high[...], high[rows, :]
    result = jnp.dot(
        jnp.concatenate([left, left, a_low[...]], 1),
        jnp.concatenate([right, low[rows, :], right], 0),
        preferred_element_type=jnp.float32,
    )

    @pl.when(step == 0)
    def _():
        total[...] = result.reshape(total.shape)

    @pl.when(step > 0)
    def _():
        total[...] += result.reshape(total.shape)

    @pl.when(step == K_STEPS - 1)
    def _():
        core, x = place_ref[0], place_ref[2]
        for away in range(SIDE):
            chip = jnp.bitwise_xor(x, away)
            own_ref[away] = total[chip * 2 + core]
            other_ref[away] = total[chip * 2 + 1 - core]


def chunk_product(high, low, pieces, place):
    rows, order = high.shape
    width = pieces[0].shape[-1]
    k_rows = order // K_STEPS
    leaves = rows // LEAF // 2
    left = pl.BlockSpec((rows, k_rows), lambda k, place: (0, k))
    out = jax.ShapeDtypeStruct((leaves, LEAF, width), jnp.float32)
    return pl.pallas_call(
        product_kernel,
        out_shape=[out] * 2,
        grid_spec=pltpu.PrefetchScalarGridSpec(
            num_scalar_prefetch=1,
            grid=(K_STEPS,),
            in_specs=[left] * 2 + [pl.BlockSpec(memory_space=pltpu.VMEM)] * len(pieces),
            out_specs=[pl.BlockSpec(memory_space=pltpu.VMEM)] * 2,
            scratch_shapes=[
                pltpu.VMEM((order, width), jnp.bfloat16),
                pltpu.VMEM((order, width), jnp.bfloat16),
                pltpu.VMEM((2 * leaves, LEAF, width), jnp.float32),
            ],
        ),
        compiler_params=pltpu.CompilerParams(vmem_limit_bytes=36 * 2**20),
        name="chunk_product",
    )(place, high, low, *pieces)


X_ROUTES = ((FIRST, SECOND), (SECOND, FIRST))


def from_x(value, mask):
    pairs = [(source, source ^ (2 * mask)) for source in range(2 * SIDE)]
    return lax.ppermute(value, "col", pairs)


def sum_over_col(other, own, route):
    near, far = route
    core_sum = own + from_partner(other, "col", 0)
    kept = from_x(jnp.stack([core_sum[near], core_sum[near ^ far]]), near)
    return [core_sum[0], kept[0], from_x(core_sum[far] + kept[1], far)]


BLOCK = 8
NODES = 3


def lane_of(value, lane):
    return jnp.broadcast_to(value[:, lane : lane + 1], value.shape)


def invert_pivot(entry):
    def at(i, j):
        return entry[max(i, j)][min(i, j)]

    def put(i, j, value):
        entry[max(i, j)][min(i, j)] = value

    for p in range(0, BLOCK, 2):
        q = p + 1
        a, b, c = at(p, p), at(q, p), at(q, q)
        scale = 1.0 / (a * c - b * b)
        w_pp, w_pq, w_qq = c * scale, -b * scale, a * scale
        rest = [i for i in range(BLOCK) if i not in (p, q)]
        first = {i: at(i, p) for i in rest}
        second = {i: at(i, q) for i in rest}
        left = {i: w_pp * first[i] + w_pq * second[i] for i in rest}
        right = {i: w_pq * first[i] + w_qq * second[i] for i in rest}
        for i in rest:
            for j in rest:
                if j <= i:
                    put(i, j, at(i, j) - (left[i] * first[j] + right[i] * second[j]))
        for i in rest:
            put(i, p, left[i])
            put(i, q, right[i])
        put(p, p, -w_pp)
        put(q, p, -w_pq)
        put(q, q, -w_qq)
    return at


def sweep(tiles, rows_scratch, new_scratch):
    lanes = lax.broadcasted_iota(jnp.int32, (BLOCK, 128), 1)
    count = KMAX // BLOCK
    for block in range(count):
        at_lane = block * BLOCK
        slot = block % 2
        inside = (lanes >= at_lane) & (lanes < at_lane + BLOCK)
        for node in range(NODES):
            rows_scratch[slot, node * BLOCK : (node + 1) * BLOCK, :] = tiles[node][block]
        rows = [rows_scratch[slot, pl.ds(k, BLOCK, stride=BLOCK), :] for k in range(BLOCK)]
        entry = [[lane_of(rows[k], at_lane + i) for i in range(k + 1)] for k in range(BLOCK)]
        at = invert_pivot(entry)
        wide = [
            jnp.where(lanes == at_lane + k, 1.0, jnp.where(inside, 0.0, -rows[k]))
            for k in range(BLOCK)
        ]
        for k in range(BLOCK):
            total = at(k, 0) * wide[0]
            for i in range(1, BLOCK):
                total = total + at(k, i) * wide[i]
            new_scratch[slot, pl.ds(k, BLOCK, stride=BLOCK), :] = total
        for node in range(NODES):
            new_rows = [
                jnp.broadcast_to(
                    new_scratch[slot, node * BLOCK + k : node * BLOCK + k + 1, :], (BLOCK, 128)
                )
                for k in range(BLOCK)
            ]
            for t in range(count):
                if t == block:
                    continue
                old = tiles[node][t]
                value = jnp.where(inside, 0.0, old)
                for k in range(BLOCK):
                    value = value - lane_of(old, at_lane + k) * new_rows[k]
                tiles[node][t] = value
            tiles[node][block] = new_scratch[slot, node * BLOCK : (node + 1) * BLOCK, :]
    return tiles


def invert_all(matrices, rows_scratch, new_scratch):
    count = KMAX // BLOCK
    lanes = lax.broadcasted_iota(jnp.int32, (BLOCK, 128), 1)
    sublanes = lax.broadcasted_iota(jnp.int32, (BLOCK, 128), 0)
    rows_scratch[...] = jnp.zeros_like(rows_scratch)
    all_tiles, all_down, all_across = [], [], []
    for matrix in matrices:
        wide = jnp.concatenate([matrix, jnp.zeros((KMAX, 128 - KMAX), jnp.float32)], 1)
        tiles = [wide[t * BLOCK : (t + 1) * BLOCK] for t in range(count)]
        on_diagonal = [
            jnp.where(lanes == sublanes + t * BLOCK, tiles[t], 0.0) for t in range(count)
        ]
        down = [lax.rsqrt(jnp.sum(part, axis=1, keepdims=True)) for part in on_diagonal]
        line = functools.reduce(jnp.add, on_diagonal)
        line = jnp.sum(line, axis=0, keepdims=True)
        across = lax.rsqrt(jnp.where(lanes[:1] < KMAX, line, 1.0))
        all_tiles.append([tiles[t] * down[t] * across for t in range(count)])
        all_down.append(down)
        all_across.append(across)
    all_tiles = sweep(all_tiles, rows_scratch, new_scratch)
    inverses = []
    for tiles, down, across in zip(all_tiles, all_down, all_across):
        scaled = [-(tiles[t] * down[t] * across) for t in range(count)]
        inverses.append(jnp.concatenate(scaled, 0)[:, :KMAX])
    return inverses


def select_rows(source, pivots_ref, node, rank, target, target_at):
    for row in range(KMAX):
        picked = source[pl.ds(pivots_ref[node, row], 1), :]
        target[target_at + row : target_at + row + 1, :] = jnp.where(row < rank, picked, 0.0)


def leaf_kernel(info_ref, pivots_ref, *refs):
    parts, (rows_ref, skeleton_ref) = refs[:-2], refs[-2:]
    rows_ref[...] = functools.reduce(jnp.add, [part[...] for part in parts])
    select_rows(rows_ref, pivots_ref, 0, info_ref[2], skeleton_ref, 0)


def mid_kernel(info_ref, pivots_ref, own_ref, other_ref, rows_ref, skeleton_ref):
    own_at = pl.multiple_of(info_ref[0] * KMAX, KMAX)
    other_at = pl.multiple_of((1 - info_ref[0]) * KMAX, KMAX)
    rows_ref[pl.ds(own_at, KMAX), :] = own_ref[...]
    rows_ref[pl.ds(other_at, KMAX), :] = other_ref[...]
    select_rows(rows_ref, pivots_ref, 1, info_ref[3], skeleton_ref, 0)


def top_kernel(info_ref, pivots_ref, *refs):
    chunks = len(WIDTHS)
    groups = [refs[5 * chunk : 5 * chunk + 5] for chunk in range(chunks)]
    leaf_out, mid_out, top_out, rows_out = refs[5 * chunks : 5 * chunks + 4]
    scratch = refs[5 * chunks + 4 :]
    tops, chosen, (rows_scratch, new_scratch) = (
        scratch[:chunks], scratch[chunks : 2 * chunks], scratch[2 * chunks :]
    )
    own_at = pl.multiple_of(info_ref[1] * KMAX, KMAX)
    other_at = pl.multiple_of((1 - info_ref[1]) * KMAX, KMAX)
    start = 0
    for group, top, skeleton in zip(groups, tops, chosen):
        top[pl.ds(own_at, KMAX), :] = group[3][...]
        top[pl.ds(other_at, KMAX), :] = group[4][...]
        select_rows(top, pivots_ref, 2, info_ref[4], skeleton, 0)
        width = skeleton.shape[-1]
        rows_out[:, start : start + width] = skeleton[...]
        start += width
    row_ids = lax.broadcasted_iota(jnp.int32, (KMAX, KMAX), 0)
    column_ids = lax.broadcasted_iota(jnp.int32, (KMAX, KMAX), 1)
    dot = functools.partial(
        lax.dot_general,
        dimension_numbers=(((1,), (1,)), ((), ())),
        precision=lax.Precision.HIGHEST,
        preferred_element_type=jnp.float32,
    )
    levels = (
        ([group[0] for group in groups], [group[1] for group in groups]),
        ([group[2] for group in groups], [group[3] for group in groups]),
        (tops, chosen),
    )
    grams, crosses = [], []
    for node, (rows, skeletons) in enumerate(levels):
        gram = functools.reduce(jnp.add, [dot(part[...], part[...]) for part in skeletons])
        cross = functools.reduce(
            jnp.add, [dot(row[...], part[...]) for row, part in zip(rows, skeletons)]
        )
        empty = (row_ids == column_ids) & (row_ids >= info_ref[2 + node])
        grams.append(gram * (1.0 / SAMPLES) + jnp.where(empty, 1.0, 0.0))
        crosses.append(cross * (1.0 / SAMPLES))
    inverses = invert_all(grams, rows_scratch, new_scratch)
    for inverse, cross, out in zip(inverses, crosses, (leaf_out, mid_out, top_out)):
        out[...] = dot(inverse, cross)


def vmem_call(kernel, outs, scratch, name):
    in_vmem = pl.BlockSpec(memory_space=pltpu.VMEM)

    def call(info, pivots, *arrays):
        return pl.pallas_call(
            kernel,
            out_shape=[jax.ShapeDtypeStruct(shape, jnp.float32) for shape in outs],
            in_specs=[pl.BlockSpec(memory_space=pltpu.SMEM)] * 2 + [in_vmem] * len(arrays),
            out_specs=[in_vmem] * len(outs),
            scratch_shapes=scratch,
            compiler_params=pltpu.CompilerParams(vmem_limit_bytes=32 * 2**20),
            name=name,
        )(info, pivots, *arrays)

    return call


def on_device(
    frontal, sketch, leaf_ranks, leaf_pivots, mid_ranks, mid_pivots, top_ranks, top_pivots
):
    col_count = lax.axis_size("col")
    col_index = lax.axis_index("col")
    row_index = lax.axis_index("row")
    leaf_index = row_index * col_count + col_index
    place = jnp.stack([col_index % 2, row_index, col_index // 2]).astype(jnp.int32)
    nodes = (leaf_index, leaf_index // 2, leaf_index // 4)
    ranks = [
        pick_entry(table, node)
        for table, node in zip((leaf_ranks, mid_ranks, top_ranks), nodes)
    ]
    info = jnp.stack([col_index % 2, col_index // 2 % 2] + ranks).astype(jnp.int32)
    pivots = jnp.stack(
        [
            pick_entry(table, node)[:KMAX]
            for table, node in zip((leaf_pivots, mid_pivots, top_pivots), nodes)
        ]
    )
    chunks, (high, low, info, pivots) = gather_parts(sketch, (*split(frontal), info, pivots))
    groups = [
        sum_over_col(*chunk_product(high, low, pieces, place), route)
        for pieces, route in zip(chunks, X_ROUTES)
    ]
    arrays = []
    for group, width in zip(groups, WIDTHS):
        skeleton_shape, pair_shape = (KMAX, width), (2 * KMAX, width)
        rows, skeleton = vmem_call(
            leaf_kernel, [(LEAF, width), skeleton_shape], [], "leaf_rows"
        )(info, pivots, *group)
        mid_rows, mid_skeleton = vmem_call(
            mid_kernel, [pair_shape, skeleton_shape], [], "mid_rows"
        )(info, pivots, skeleton, from_partner(skeleton, "col", 0))
        arrays += [rows, skeleton, mid_rows, mid_skeleton, from_partner(mid_skeleton, "col", 1)]
    scratch = [pltpu.VMEM((2 * KMAX, width), jnp.float32) for width in WIDTHS]
    scratch += [pltpu.VMEM((KMAX, width), jnp.float32) for width in WIDTHS]
    scratch += [pltpu.VMEM((2, BLOCK * BLOCK, 128), jnp.float32)] * 2
    outs = vmem_call(
        top_kernel,
        [(KMAX, LEAF), (KMAX, 2 * KMAX), (KMAX, 2 * KMAX), (KMAX, SAMPLES)],
        scratch,
        "interpolation",
    )(info, pivots, *arrays)
    return tuple(out[None] for out in outs)


def solution(mesh):
    return jax.shard_map(
        on_device,
        mesh=mesh,
        in_specs=(P("row", "col"), P(("col", "row"), None), P(), P(), P(), P(), P(), P()),
        out_specs=(
            P(("row", "col"), None, None),
            P(("row", "col"), None, None),
            P(("row", "col"), None, None),
            P(("row", "col"), None, None),
        ),
        check_vma=False,
    )
```

```python
import functools

import jax
import jax.numpy as jnp
from jax import lax
from jax.experimental import pallas as pl
from jax.experimental.pallas import tpu as pltpu
from jax.sharding import PartitionSpec as P

SAMPLES = 512
KMAX = 96
SIDE = 4
LEAF = 128
LEAVES = 128
WIDTHS = (256, 256)
K_STEPS = 4


def from_partner(value, axis, apart):
    mask = 2**apart
    pairs = [(source, source ^ mask) for source in range(lax.axis_size(axis))]
    return lax.ppermute(value, axis, pairs)


def pick_entry(table, position):
    return lax.dynamic_index_in_dim(table, position, 0, keepdims=False)


FIRST, SECOND = 1, 3
ORDERS = ((FIRST, SECOND), (SECOND, FIRST))


def row_mask(core, step, masks):
    along_y = (step < 2) == (core == 0)
    return masks[step % 2] * SIDE if along_y else masks[step % 2]


def from_row(value, step, masks):
    columns = 2 * SIDE
    pairs = []
    for row in range(SIDE * SIDE):
        for column in range(columns):
            partner = row ^ row_mask(column % 2, step, masks)
            pairs.append((row * columns + column, partner * columns + column))
    return lax.ppermute(value, ("row", "col"), pairs)


def origins(core, masks):
    found = [0]
    for step in range(4):
        found += [mask ^ row_mask(core, step, masks) for mask in found]
    return found


def gather_parts(sketch, before, after):
    depth = sketch.shape[0] // len(ORDERS)
    stacks = [sketch[None, part * depth : (part + 1) * depth] for part in range(len(ORDERS))]
    for step in range(3):
        received = [from_row(stack, step, masks) for stack, masks in zip(stacks, ORDERS)]
        if step == 1:
            received, before = lax.optimization_barrier((received, before))
        stacks = [jnp.concatenate(pair, 0) for pair in zip(stacks, received)]
    stacks, ready = lax.optimization_barrier((stacks, after(*before)))
    chunks, start = [], 0
    for width in WIDTHS:
        own = [stack[:, :, start : start + width] for stack in stacks]
        chunks.append(own + [from_row(value, 3, masks) for value, masks in zip(own, ORDERS)])
        start += width
    return chunks, ready


def split_kernel(value_ref, high_ref, low_ref):
    value = value_ref[...]
    high = value.astype(jnp.bfloat16)
    high_ref[...] = high
    low_ref[...] = (value - high.astype(jnp.float32)).astype(jnp.bfloat16)


def split(value):
    rows, order = value.shape
    block = pl.BlockSpec((LEAF, order), lambda i: (i, 0))
    return pl.pallas_call(
        split_kernel,
        out_shape=[jax.ShapeDtypeStruct(value.shape, jnp.bfloat16)] * 2,
        grid=(rows // LEAF,),
        in_specs=[block],
        out_specs=[block] * 2,
        compiler_params=pltpu.CompilerParams(vmem_limit_bytes=8 * 2**20),
        cost_estimate=pl.CostEstimate(
            flops=4 * rows * order, bytes_accessed=8 * rows * order, transcendentals=0
        ),
        name="split",
    )(value)


def product_kernel(place_ref, a_high, a_low, *refs):
    parts = len(ORDERS)
    pieces = refs[: 2 * parts]
    own_ref, other_ref, high, low, total = refs[2 * parts :]
    step = pl.program_id(0)

    @pl.when(step == 0)
    def _():
        depth = pieces[0].shape[1]
        for part, masks in enumerate(ORDERS):
            for at, (mask_0, mask_1) in enumerate(zip(origins(0, masks), origins(1, masks))):
                source = pieces[part + parts * (at // 8)]
                mask = jnp.where(place_ref[2] == 0, mask_0, mask_1)
                block = jnp.bitwise_xor(place_ref[0], mask)
                start = pl.multiple_of((block * parts + part) * depth, depth)
                value = source[at % 8]
                top = value.astype(jnp.bfloat16)
                high[pl.ds(start, depth), :] = top
                low[pl.ds(start, depth), :] = (value - top.astype(jnp.float32)).astype(
                    jnp.bfloat16
                )

    k_rows = a_high.shape[-1] // K_STEPS
    rows = pl.ds(pl.multiple_of(step * k_rows, 256), k_rows)
    left, right = a_high[:, rows], high[rows, :]
    result = jnp.dot(
        jnp.concatenate([left, left, a_low[:, rows]], 1),
        jnp.concatenate([right, low[rows, :], right], 0),
        preferred_element_type=jnp.float32,
    )

    @pl.when(step == 0)
    def _():
        total[...] = result.reshape(total.shape)

    @pl.when(step > 0)
    def _():
        total[...] += result.reshape(total.shape)

    @pl.when(step == K_STEPS - 1)
    def _():
        for at, masks in enumerate(zip((0, SECOND, FIRST, FIRST ^ SECOND), (0, FIRST, SECOND, FIRST ^ SECOND))):
            for out_ref, core in ((own_ref, place_ref[2]), (other_ref, 1 - place_ref[2])):
                chip = jnp.bitwise_xor(place_ref[1], jnp.where(core == 0, *masks))
                out_ref[at] = total[chip * 2 + core]


def chunk_product(high, low, pieces, place):
    rows, order = high.shape
    width = pieces[0].shape[-1]
    leaves = rows // LEAF // 2
    in_vmem = pl.BlockSpec(memory_space=pltpu.VMEM)
    out = jax.ShapeDtypeStruct((leaves, LEAF, width), jnp.float32)
    return pl.pallas_call(
        product_kernel,
        out_shape=[out] * 2,
        grid_spec=pltpu.PrefetchScalarGridSpec(
            num_scalar_prefetch=1,
            grid=(K_STEPS,),
            in_specs=[in_vmem] * (2 + len(pieces)),
            out_specs=[in_vmem] * 2,
            scratch_shapes=[
                pltpu.VMEM((order, width), jnp.bfloat16),
                pltpu.VMEM((order, width), jnp.bfloat16),
                pltpu.VMEM((2 * leaves, LEAF, width), jnp.float32),
            ],
        ),
        compiler_params=pltpu.CompilerParams(vmem_limit_bytes=24 * 2**20),
        name="chunk_product",
    )(place, high, low, *pieces)


def from_x(value, step):
    pairs = []
    for column in range(2 * SIDE):
        mask = ORDERS[column % 2][step]
        pairs.append((column, column ^ (2 * mask)))
    return lax.ppermute(value, "col", pairs)


def sum_over_col(own, other):
    core_sum = own + from_partner(other, "col", 0)
    kept = from_x(core_sum[2:], 0)
    return [core_sum[0], kept[0], from_x(core_sum[1] + kept[1], 1)]


BLOCK = 8
NODES = 3


def lane_of(value, lane):
    return jnp.broadcast_to(value[:, lane : lane + 1], value.shape)


def invert_pivot(entry):
    def at(i, j):
        return entry[max(i, j)][min(i, j)]

    def put(i, j, value):
        entry[max(i, j)][min(i, j)] = value

    for p in range(0, BLOCK, 2):
        q = p + 1
        a, b, c = at(p, p), at(q, p), at(q, q)
        scale = 1.0 / (a * c - b * b)
        w_pp, w_pq, w_qq = c * scale, -b * scale, a * scale
        rest = [i for i in range(BLOCK) if i not in (p, q)]
        first = {i: at(i, p) for i in rest}
        second = {i: at(i, q) for i in rest}
        left = {i: w_pp * first[i] + w_pq * second[i] for i in rest}
        right = {i: w_pq * first[i] + w_qq * second[i] for i in rest}
        for i in rest:
            for j in rest:
                if j <= i:
                    put(i, j, at(i, j) - (left[i] * first[j] + right[i] * second[j]))
        for i in rest:
            put(i, p, left[i])
            put(i, q, right[i])
        put(p, p, -w_pp)
        put(q, p, -w_pq)
        put(q, q, -w_qq)
    return at


def sweep(tiles, rows_scratch, new_scratch):
    lanes = lax.broadcasted_iota(jnp.int32, (BLOCK, 128), 1)
    count = KMAX // BLOCK
    for block in range(count):
        at_lane = block * BLOCK
        slot = block % 2
        inside = (lanes >= at_lane) & (lanes < at_lane + BLOCK)
        for node in range(NODES):
            rows_scratch[slot, node * BLOCK : (node + 1) * BLOCK, :] = tiles[node][block]
        rows = [rows_scratch[slot, pl.ds(k, BLOCK, stride=BLOCK), :] for k in range(BLOCK)]
        entry = [[lane_of(rows[k], at_lane + i) for i in range(k + 1)] for k in range(BLOCK)]
        at = invert_pivot(entry)
        wide = [
            jnp.where(lanes == at_lane + k, 1.0, jnp.where(inside, 0.0, -rows[k]))
            for k in range(BLOCK)
        ]
        for k in range(BLOCK):
            total = at(k, 0) * wide[0]
            for i in range(1, BLOCK):
                total = total + at(k, i) * wide[i]
            new_scratch[slot, pl.ds(k, BLOCK, stride=BLOCK), :] = total
        for node in range(NODES):
            new_rows = [
                jnp.broadcast_to(
                    new_scratch[slot, node * BLOCK + k : node * BLOCK + k + 1, :], (BLOCK, 128)
                )
                for k in range(BLOCK)
            ]
            for t in range(count):
                if t == block:
                    continue
                old = tiles[node][t]
                value = jnp.where(inside, 0.0, old)
                for k in range(BLOCK):
                    value = value - lane_of(old, at_lane + k) * new_rows[k]
                tiles[node][t] = value
            tiles[node][block] = new_scratch[slot, node * BLOCK : (node + 1) * BLOCK, :]
    return tiles


def invert_all(matrices, rows_scratch, new_scratch):
    count = KMAX // BLOCK
    lanes = lax.broadcasted_iota(jnp.int32, (BLOCK, 128), 1)
    sublanes = lax.broadcasted_iota(jnp.int32, (BLOCK, 128), 0)
    rows_scratch[...] = jnp.zeros_like(rows_scratch)
    all_tiles, all_down, all_across = [], [], []
    for matrix in matrices:
        wide = jnp.concatenate([matrix, jnp.zeros((KMAX, 128 - KMAX), jnp.float32)], 1)
        tiles = [wide[t * BLOCK : (t + 1) * BLOCK] for t in range(count)]
        on_diagonal = [
            jnp.where(lanes == sublanes + t * BLOCK, tiles[t], 0.0) for t in range(count)
        ]
        down = [lax.rsqrt(jnp.sum(part, axis=1, keepdims=True)) for part in on_diagonal]
        line = functools.reduce(jnp.add, on_diagonal)
        line = jnp.sum(line, axis=0, keepdims=True)
        across = lax.rsqrt(jnp.where(lanes[:1] < KMAX, line, 1.0))
        all_tiles.append([tiles[t] * down[t] * across for t in range(count)])
        all_down.append(down)
        all_across.append(across)
    all_tiles = sweep(all_tiles, rows_scratch, new_scratch)
    inverses = []
    for tiles, down, across in zip(all_tiles, all_down, all_across):
        scaled = [-(tiles[t] * down[t] * across) for t in range(count)]
        inverses.append(jnp.concatenate(scaled, 0)[:, :KMAX])
    return inverses


def select_rows(source, pivots_ref, node, rank, target, target_at):
    for row in range(KMAX):
        picked = source[pl.ds(pivots_ref[node, row], 1), :]
        target[target_at + row : target_at + row + 1, :] = jnp.where(row < rank, picked, 0.0)


def rank_of(info_ref, ranks_ref, level):
    place = info_ref[0] // 2**level
    starts = [0, LEAVES, LEAVES + LEAVES // 2]
    return ranks_ref[starts[level] + place]


def leaf_kernel(info_ref, ranks_ref, pivots_ref, *refs):
    parts, (rows_ref, skeleton_ref) = refs[:-2], refs[-2:]
    rows_ref[...] = functools.reduce(jnp.add, [part[...] for part in parts])
    select_rows(rows_ref, pivots_ref, 0, rank_of(info_ref, ranks_ref, 0), skeleton_ref, 0)


def mid_kernel(info_ref, ranks_ref, pivots_ref, own_ref, other_ref, rows_ref, skeleton_ref):
    own_at = pl.multiple_of((info_ref[0] % 2) * KMAX, KMAX)
    other_at = pl.multiple_of((1 - info_ref[0] % 2) * KMAX, KMAX)
    rows_ref[pl.ds(own_at, KMAX), :] = own_ref[...]
    rows_ref[pl.ds(other_at, KMAX), :] = other_ref[...]
    select_rows(rows_ref, pivots_ref, 1, rank_of(info_ref, ranks_ref, 1), skeleton_ref, 0)


def top_kernel(info_ref, ranks_ref, pivots_ref, *refs):
    chunks = len(WIDTHS)
    groups = [refs[5 * chunk : 5 * chunk + 5] for chunk in range(chunks)]
    leaf_out, mid_out, top_out, rows_out = refs[5 * chunks : 5 * chunks + 4]
    scratch = refs[5 * chunks + 4 :]
    tops, chosen, (rows_scratch, new_scratch) = (
        scratch[:chunks], scratch[chunks : 2 * chunks], scratch[2 * chunks :]
    )
    own_at = pl.multiple_of((info_ref[0] // 2 % 2) * KMAX, KMAX)
    other_at = pl.multiple_of((1 - info_ref[0] // 2 % 2) * KMAX, KMAX)
    start = 0
    for group, top, skeleton in zip(groups, tops, chosen):
        top[pl.ds(own_at, KMAX), :] = group[3][...]
        top[pl.ds(other_at, KMAX), :] = group[4][...]
        select_rows(top, pivots_ref, 2, rank_of(info_ref, ranks_ref, 2), skeleton, 0)
        width = skeleton.shape[-1]
        rows_out[:, start : start + width] = skeleton[...]
        start += width
    row_ids = lax.broadcasted_iota(jnp.int32, (KMAX, KMAX), 0)
    column_ids = lax.broadcasted_iota(jnp.int32, (KMAX, KMAX), 1)
    dot = functools.partial(
        lax.dot_general,
        dimension_numbers=(((1,), (1,)), ((), ())),
        precision=lax.Precision.HIGHEST,
        preferred_element_type=jnp.float32,
    )
    levels = (
        ([group[0] for group in groups], [group[1] for group in groups]),
        ([group[2] for group in groups], [group[3] for group in groups]),
        (tops, chosen),
    )
    grams, crosses = [], []
    for node, (rows, skeletons) in enumerate(levels):
        gram = functools.reduce(jnp.add, [dot(part[...], part[...]) for part in skeletons])
        cross = functools.reduce(
            jnp.add, [dot(row[...], part[...]) for row, part in zip(rows, skeletons)]
        )
        empty = (row_ids == column_ids) & (row_ids >= rank_of(info_ref, ranks_ref, node))
        grams.append(gram * (1.0 / SAMPLES) + jnp.where(empty, 1.0, 0.0))
        crosses.append(cross * (1.0 / SAMPLES))
    inverses = invert_all(grams, rows_scratch, new_scratch)
    for inverse, cross, out in zip(inverses, crosses, (leaf_out, mid_out, top_out)):
        out[...] = dot(inverse, cross)


def vmem_call(kernel, outs, scratch, name):
    in_vmem = pl.BlockSpec(memory_space=pltpu.VMEM)

    def call(info, ranks, pivots, *arrays):
        return pl.pallas_call(
            kernel,
            out_shape=[jax.ShapeDtypeStruct(shape, jnp.float32) for shape in outs],
            in_specs=[pl.BlockSpec(memory_space=pltpu.SMEM)] * 3 + [in_vmem] * len(arrays),
            out_specs=[in_vmem] * len(outs),
            scratch_shapes=scratch,
            compiler_params=pltpu.CompilerParams(vmem_limit_bytes=8 * 2**20),
            name=name,
        )(info, ranks, pivots, *arrays)

    return call


def on_device(
    frontal, sketch, leaf_ranks, leaf_pivots, mid_ranks, mid_pivots, top_ranks, top_pivots
):
    col_count = lax.axis_size("col")
    col_index = lax.axis_index("col")
    row_index = lax.axis_index("row")
    leaf_index = row_index * col_count + col_index
    place = jnp.stack([row_index, col_index // 2, col_index % 2]).astype(jnp.int32)
    nodes = (leaf_index, leaf_index // 2, leaf_index // 4)

    def prepare(frontal, *tables):
        ranks = jnp.concatenate(tables[:3])
        pivots = [pick_entry(table, node)[:KMAX] for table, node in zip(tables[3:], nodes)]
        return (*split(frontal), ranks, jnp.stack(pivots))

    tables = (leaf_ranks, mid_ranks, top_ranks, leaf_pivots, mid_pivots, top_pivots)
    chunks, (high, low, ranks, pivots) = gather_parts(sketch, (frontal, *tables), prepare)
    info = jnp.stack([leaf_index]).astype(jnp.int32)
    groups = [sum_over_col(*chunk_product(high, low, pieces, place)) for pieces in chunks]
    arrays = []
    for group, width in zip(groups, WIDTHS):
        skeleton_shape, pair_shape = (KMAX, width), (2 * KMAX, width)
        rows, skeleton = vmem_call(
            leaf_kernel, [(LEAF, width), skeleton_shape], [], "leaf_rows"
        )(info, ranks, pivots, *group)
        mid_rows, mid_skeleton = vmem_call(
            mid_kernel, [pair_shape, skeleton_shape], [], "mid_rows"
        )(info, ranks, pivots, skeleton, from_partner(skeleton, "col", 0))
        arrays += [rows, skeleton, mid_rows, mid_skeleton, from_partner(mid_skeleton, "col", 1)]
    scratch = [pltpu.VMEM((2 * KMAX, width), jnp.float32) for width in WIDTHS]
    scratch += [pltpu.VMEM((KMAX, width), jnp.float32) for width in WIDTHS]
    scratch += [pltpu.VMEM((2, BLOCK * BLOCK, 128), jnp.float32)] * 2
    outs = vmem_call(
        top_kernel,
        [(KMAX, LEAF), (KMAX, 2 * KMAX), (KMAX, 2 * KMAX), (KMAX, SAMPLES)],
        scratch,
        "interpolation",
    )(info, ranks, pivots, *arrays)
    return tuple(out[None] for out in outs)


def solution(mesh):
    return jax.shard_map(
        on_device,
        mesh=mesh,
        in_specs=(P("row", "col"), P(("col", "row"), None), P(), P(), P(), P(), P(), P()),
        out_specs=(
            P(("row", "col"), None, None),
            P(("row", "col"), None, None),
            P(("row", "col"), None, None),
            P(("row", "col"), None, None),
        ),
        check_vma=False,
    )
```

```python
import functools

import jax
import jax.numpy as jnp
from jax import lax
from jax.experimental import pallas as pl
from jax.experimental.pallas import tpu as pltpu
from jax.sharding import PartitionSpec as P

SAMPLES = 512
KMAX = 96
SIDE = 4
LEAF = 128
LEAVES = 128
WIDTHS = (256, 256)


def from_partner(value, axis, apart):
    mask = 2**apart
    pairs = [(source, source ^ mask) for source in range(lax.axis_size(axis))]
    return lax.ppermute(value, axis, pairs)


def pick_entry(table, position):
    return lax.dynamic_index_in_dim(table, position, 0, keepdims=False)


FIRST, SECOND = 1, 3
ORDERS = ((FIRST, SECOND), (SECOND, FIRST))


def row_mask(core, step, masks):
    along_y = (step < 2) == (core == 0)
    return masks[step % 2] * SIDE if along_y else masks[step % 2]


def from_row(value, step, masks):
    columns = 2 * SIDE
    pairs = []
    for row in range(SIDE * SIDE):
        for column in range(columns):
            partner = row ^ row_mask(column % 2, step, masks)
            pairs.append((row * columns + column, partner * columns + column))
    return lax.ppermute(value, ("row", "col"), pairs)


def origins(core, masks):
    found = [0]
    for step in range(4):
        found += [mask ^ row_mask(core, step, masks) for mask in found]
    return found


def gather_parts(sketch, before, after):
    depth = sketch.shape[0] // len(ORDERS)
    stacks = [sketch[None, part * depth : (part + 1) * depth] for part in range(len(ORDERS))]
    for step in range(3):
        received = [from_row(stack, step, masks) for stack, masks in zip(stacks, ORDERS)]
        if step == 1:
            received, before = lax.optimization_barrier((received, before))
        if step < 2:
            stacks = [jnp.concatenate(pair, 0) for pair in zip(stacks, received)]
    stacks, received, ready = lax.optimization_barrier((stacks, received, after(*before)))
    chunks, start = [], 0
    for width in WIDTHS:
        columns = slice(start, start + width)
        own = [
            jnp.concatenate([stack[:, :, columns], other[:, :, columns]], 0)
            for stack, other in zip(stacks, received)
        ]
        chunks.append(own + [from_row(value, 3, masks) for value, masks in zip(own, ORDERS)])
        start += width
    return chunks, ready


def split_kernel(value_ref, high_ref, low_ref):
    value = value_ref[...]
    rows = pl.ds(pl.multiple_of(pl.program_id(0) * LEAF, LEAF), LEAF)
    high = value.astype(jnp.bfloat16)
    high_ref[rows, :] = high
    low_ref[rows, :] = (value - high.astype(jnp.float32)).astype(jnp.bfloat16)


def split(value):
    rows, order = value.shape
    return pl.pallas_call(
        split_kernel,
        out_shape=[pltpu.VMEM(value.shape, jnp.bfloat16)] * 2,
        grid=(rows // LEAF,),
        in_specs=[pl.BlockSpec((LEAF, order), lambda i: (i, 0))],
        out_specs=[pl.BlockSpec(memory_space=pltpu.VMEM)] * 2,
        compiler_params=pltpu.CompilerParams(vmem_limit_bytes=8 * 2**20),
        cost_estimate=pl.CostEstimate(
            flops=4 * rows * order, bytes_accessed=8 * rows * order, transcendentals=0
        ),
        name="split",
    )(pltpu.with_memory_space_constraint(value, pltpu.HBM))


def convert(place_ref, pieces, high, low):
    parts = len(ORDERS)
    depth = pieces[0].shape[1]
    for part, masks in enumerate(ORDERS):
        for at, (mask_0, mask_1) in enumerate(zip(origins(0, masks), origins(1, masks))):
            source = pieces[part + parts * (at // 8)]
            mask = jnp.where(place_ref[2] == 0, mask_0, mask_1)
            block = jnp.bitwise_xor(place_ref[0], mask)
            start = pl.multiple_of((block * parts + part) * depth, depth)
            value = source[at % 8]
            top = value.astype(jnp.bfloat16)
            high[pl.ds(start, depth), :] = top
            low[pl.ds(start, depth), :] = (value - top.astype(jnp.float32)).astype(jnp.bfloat16)


def multiply(place_ref, core, a_high, a_low, high, low, total, out_ref):
    left = a_high[:, core].reshape(-1, high.shape[0])
    low_left = a_low[:, core].reshape(-1, high.shape[0])
    right = high[...]
    total[...] = jnp.dot(
        jnp.concatenate([left, left, low_left], 1),
        jnp.concatenate([right, low[...], right], 0),
        preferred_element_type=jnp.float32,
    ).reshape(total.shape)
    orders = zip((0, SECOND, FIRST, FIRST ^ SECOND), (0, FIRST, SECOND, FIRST ^ SECOND))
    for at, masks in enumerate(orders):
        chip = jnp.bitwise_xor(place_ref[1], jnp.where(core == 0, *masks))
        out_ref[at] = total[chip]


def other_kernel(place_ref, a_high, a_low, *refs):
    pieces = refs[: 2 * len(ORDERS)]
    out_ref, high, low, total = refs[2 * len(ORDERS) :]
    convert(place_ref, pieces, high, low)
    multiply(place_ref, 1 - place_ref[2], a_high, a_low, high, low, total, out_ref)


def own_kernel(place_ref, a_high, a_low, high, low, out_ref, total):
    multiply(place_ref, place_ref[2], a_high, a_low, high, low, total, out_ref)


def product(kernel, place, halves, arrays, outs, cost, name):
    in_vmem = pl.BlockSpec(memory_space=pltpu.VMEM)
    halves = [pltpu.with_memory_space_constraint(half, pltpu.VMEM) for half in halves]
    return pl.pallas_call(
        kernel,
        out_shape=outs,
        in_specs=[pl.BlockSpec(memory_space=pltpu.SMEM)] + [in_vmem] * (2 + len(arrays)),
        out_specs=[in_vmem] * len(outs),
        scratch_shapes=[pltpu.VMEM(outs[0].shape, jnp.float32)],
        compiler_params=pltpu.CompilerParams(vmem_limit_bytes=24 * 2**20),
        cost_estimate=pl.CostEstimate(flops=cost, bytes_accessed=cost // 400, transcendentals=0),
        name=name,
    )(place, *halves, *arrays)


def product_other(halves, pieces, place):
    leaves, _, leaf, order = halves[0].shape
    width = pieces[0].shape[-1]
    outs = [jax.ShapeDtypeStruct((leaves, leaf, width), jnp.float32)]
    outs += [jax.ShapeDtypeStruct((order, width), jnp.bfloat16)] * 2
    return product(other_kernel, place, halves, pieces, outs, 1, "product_other")


def product_own(halves, sketch, place, last):
    leaves, _, leaf, order = halves[0].shape
    width = sketch[0].shape[-1]
    outs = [jax.ShapeDtypeStruct((leaves, leaf, width), jnp.float32)]
    cost = 6 * leaves * leaf * order * width if last else 1
    return product(own_kernel, place, halves, sketch, outs, cost, "product_own")[0]


def from_x(value, step):
    pairs = []
    for column in range(2 * SIDE):
        mask = ORDERS[column % 2][step]
        pairs.append((column, column ^ (2 * mask)))
    return lax.ppermute(value, "col", pairs)


def sum_over_x(core_sum):
    kept = from_x(core_sum[2:], 0)
    return [core_sum[0], kept[0], from_x(core_sum[1] + kept[1], 1)]


BLOCK = 8
NODES = 3


def lane_of(value, lane):
    return jnp.broadcast_to(value[:, lane : lane + 1], value.shape)


def invert_pivot(entry):
    def at(i, j):
        return entry[max(i, j)][min(i, j)]

    def put(i, j, value):
        entry[max(i, j)][min(i, j)] = value

    for p in range(0, BLOCK, 2):
        q = p + 1
        a, b, c = at(p, p), at(q, p), at(q, q)
        scale = 1.0 / (a * c - b * b)
        w_pp, w_pq, w_qq = c * scale, -b * scale, a * scale
        rest = [i for i in range(BLOCK) if i not in (p, q)]
        first = {i: at(i, p) for i in rest}
        second = {i: at(i, q) for i in rest}
        left = {i: w_pp * first[i] + w_pq * second[i] for i in rest}
        right = {i: w_pq * first[i] + w_qq * second[i] for i in rest}
        for i in rest:
            for j in rest:
                if j <= i:
                    put(i, j, at(i, j) - (left[i] * first[j] + right[i] * second[j]))
        for i in rest:
            put(i, p, left[i])
            put(i, q, right[i])
        put(p, p, -w_pp)
        put(q, p, -w_pq)
        put(q, q, -w_qq)
    return at


def sweep(tiles, rows_scratch, new_scratch):
    lanes = lax.broadcasted_iota(jnp.int32, (BLOCK, 128), 1)
    count = KMAX // BLOCK
    for block in range(count):
        at_lane = block * BLOCK
        slot = block % 2
        inside = (lanes >= at_lane) & (lanes < at_lane + BLOCK)
        for node in range(NODES):
            rows_scratch[slot, node * BLOCK : (node + 1) * BLOCK, :] = tiles[node][block]
        rows = [rows_scratch[slot, pl.ds(k, BLOCK, stride=BLOCK), :] for k in range(BLOCK)]
        entry = [[lane_of(rows[k], at_lane + i) for i in range(k + 1)] for k in range(BLOCK)]
        at = invert_pivot(entry)
        wide = [
            jnp.where(lanes == at_lane + k, 1.0, jnp.where(inside, 0.0, -rows[k]))
            for k in range(BLOCK)
        ]
        for k in range(BLOCK):
            total = at(k, 0) * wide[0]
            for i in range(1, BLOCK):
                total = total + at(k, i) * wide[i]
            new_scratch[slot, pl.ds(k, BLOCK, stride=BLOCK), :] = total
        for node in range(NODES):
            new_rows = [
                jnp.broadcast_to(
                    new_scratch[slot, node * BLOCK + k : node * BLOCK + k + 1, :], (BLOCK, 128)
                )
                for k in range(BLOCK)
            ]
            for t in range(count):
                if t == block:
                    continue
                old = tiles[node][t]
                value = jnp.where(inside, 0.0, old)
                for k in range(BLOCK):
                    value = value - lane_of(old, at_lane + k) * new_rows[k]
                tiles[node][t] = value
            tiles[node][block] = new_scratch[slot, node * BLOCK : (node + 1) * BLOCK, :]
    return tiles


def invert_all(matrices, rows_scratch, new_scratch):
    count = KMAX // BLOCK
    lanes = lax.broadcasted_iota(jnp.int32, (BLOCK, 128), 1)
    sublanes = lax.broadcasted_iota(jnp.int32, (BLOCK, 128), 0)
    rows_scratch[...] = jnp.zeros_like(rows_scratch)
    all_tiles, all_down, all_across = [], [], []
    for matrix in matrices:
        wide = jnp.concatenate([matrix, jnp.zeros((KMAX, 128 - KMAX), jnp.float32)], 1)
        tiles = [wide[t * BLOCK : (t + 1) * BLOCK] for t in range(count)]
        on_diagonal = [
            jnp.where(lanes == sublanes + t * BLOCK, tiles[t], 0.0) for t in range(count)
        ]
        down = [lax.rsqrt(jnp.sum(part, axis=1, keepdims=True)) for part in on_diagonal]
        line = functools.reduce(jnp.add, on_diagonal)
        line = jnp.sum(line, axis=0, keepdims=True)
        across = lax.rsqrt(jnp.where(lanes[:1] < KMAX, line, 1.0))
        all_tiles.append([tiles[t] * down[t] * across for t in range(count)])
        all_down.append(down)
        all_across.append(across)
    all_tiles = sweep(all_tiles, rows_scratch, new_scratch)
    inverses = []
    for tiles, down, across in zip(all_tiles, all_down, all_across):
        scaled = [-(tiles[t] * down[t] * across) for t in range(count)]
        inverses.append(jnp.concatenate(scaled, 0)[:, :KMAX])
    return inverses


def select_rows(source, pivots_ref, node, rank, target, target_at):
    for row in range(KMAX):
        picked = source[pl.ds(pivots_ref[node, row], 1), :]
        target[target_at + row : target_at + row + 1, :] = jnp.where(row < rank, picked, 0.0)


def rank_of(info_ref, ranks_ref, level):
    place = info_ref[0] // 2**level
    starts = [0, LEAVES, LEAVES + LEAVES // 2]
    return ranks_ref[starts[level] + place]


def leaf_kernel(info_ref, ranks_ref, pivots_ref, *refs):
    parts, (rows_ref, skeleton_ref) = refs[:-2], refs[-2:]
    rows_ref[...] = functools.reduce(jnp.add, [part[...] for part in parts])
    select_rows(rows_ref, pivots_ref, 0, rank_of(info_ref, ranks_ref, 0), skeleton_ref, 0)


def mid_kernel(info_ref, ranks_ref, pivots_ref, own_ref, other_ref, rows_ref, skeleton_ref):
    own_at = pl.multiple_of((info_ref[0] % 2) * KMAX, KMAX)
    other_at = pl.multiple_of((1 - info_ref[0] % 2) * KMAX, KMAX)
    rows_ref[pl.ds(own_at, KMAX), :] = own_ref[...]
    rows_ref[pl.ds(other_at, KMAX), :] = other_ref[...]
    select_rows(rows_ref, pivots_ref, 1, rank_of(info_ref, ranks_ref, 1), skeleton_ref, 0)


def top_kernel(info_ref, ranks_ref, pivots_ref, *refs):
    chunks = len(WIDTHS)
    groups = [refs[5 * chunk : 5 * chunk + 5] for chunk in range(chunks)]
    leaf_out, mid_out, top_out, rows_out = refs[5 * chunks : 5 * chunks + 4]
    scratch = refs[5 * chunks + 4 :]
    tops, chosen, (rows_scratch, new_scratch) = (
        scratch[:chunks], scratch[chunks : 2 * chunks], scratch[2 * chunks :]
    )
    own_at = pl.multiple_of((info_ref[0] // 2 % 2) * KMAX, KMAX)
    other_at = pl.multiple_of((1 - info_ref[0] // 2 % 2) * KMAX, KMAX)
    start = 0
    for group, top, skeleton in zip(groups, tops, chosen):
        top[pl.ds(own_at, KMAX), :] = group[3][...]
        top[pl.ds(other_at, KMAX), :] = group[4][...]
        select_rows(top, pivots_ref, 2, rank_of(info_ref, ranks_ref, 2), skeleton, 0)
        width = skeleton.shape[-1]
        rows_out[:, start : start + width] = skeleton[...]
        start += width
    row_ids = lax.broadcasted_iota(jnp.int32, (KMAX, KMAX), 0)
    column_ids = lax.broadcasted_iota(jnp.int32, (KMAX, KMAX), 1)
    dot = functools.partial(
        lax.dot_general,
        dimension_numbers=(((1,), (1,)), ((), ())),
        precision=lax.Precision.HIGHEST,
        preferred_element_type=jnp.float32,
    )
    levels = (
        ([group[0] for group in groups], [group[1] for group in groups]),
        ([group[2] for group in groups], [group[3] for group in groups]),
        (tops, chosen),
    )
    grams, crosses = [], []
    for node, (rows, skeletons) in enumerate(levels):
        gram = functools.reduce(jnp.add, [dot(part[...], part[...]) for part in skeletons])
        cross = functools.reduce(
            jnp.add, [dot(row[...], part[...]) for row, part in zip(rows, skeletons)]
        )
        empty = (row_ids == column_ids) & (row_ids >= rank_of(info_ref, ranks_ref, node))
        grams.append(gram * (1.0 / SAMPLES) + jnp.where(empty, 1.0, 0.0))
        crosses.append(cross * (1.0 / SAMPLES))
    inverses = invert_all(grams, rows_scratch, new_scratch)
    for inverse, cross, out in zip(inverses, crosses, (leaf_out, mid_out, top_out)):
        out[...] = dot(inverse, cross)


def vmem_call(kernel, outs, scratch, name):
    in_vmem = pl.BlockSpec(memory_space=pltpu.VMEM)

    def call(info, ranks, pivots, *arrays):
        return pl.pallas_call(
            kernel,
            out_shape=[jax.ShapeDtypeStruct(shape, jnp.float32) for shape in outs],
            in_specs=[pl.BlockSpec(memory_space=pltpu.SMEM)] * 3 + [in_vmem] * len(arrays),
            out_specs=[in_vmem] * len(outs),
            scratch_shapes=scratch,
            compiler_params=pltpu.CompilerParams(vmem_limit_bytes=8 * 2**20),
            name=name,
        )(info, ranks, pivots, *arrays)

    return call


def on_device(
    frontal, sketch, leaf_ranks, leaf_pivots, mid_ranks, mid_pivots, top_ranks, top_pivots
):
    col_count = lax.axis_size("col")
    col_index = lax.axis_index("col")
    row_index = lax.axis_index("row")
    leaf_index = row_index * col_count + col_index
    place = jnp.stack([row_index, col_index // 2, col_index % 2]).astype(jnp.int32)
    nodes = (leaf_index, leaf_index // 2, leaf_index // 4)

    def prepare(frontal, *tables):
        ranks = jnp.concatenate(tables[:3])
        pivots = [pick_entry(table, node)[:KMAX] for table, node in zip(tables[3:], nodes)]
        return (*split(frontal), ranks, jnp.stack(pivots))

    tables = (leaf_ranks, mid_ranks, top_ranks, leaf_pivots, mid_pivots, top_pivots)
    chunks, (high, low, ranks, pivots) = gather_parts(sketch, (frontal, *tables), prepare)
    info = jnp.stack([leaf_index]).astype(jnp.int32)
    halves = [part.reshape(SIDE, 2, LEAF, -1) for part in (high, low)]
    core_sums, own = [], ()
    for chunk, pieces in enumerate(chunks):
        place, own = lax.optimization_barrier((place, own))
        other, *parts = product_other(halves, pieces, place)
        received = from_partner(other, "col", 0)
        last = chunk == len(chunks) - 1
        if chunk > 0:
            core_sums[-1] = own + core_sums[-1]
            place, core_sums = lax.optimization_barrier((place, core_sums))
        own = product_own(halves, parts, place, last)
        core_sums.append(received)
    core_sums[-1] = own + core_sums[-1]
    groups = [sum_over_x(core_sum) for core_sum in core_sums]
    arrays = []
    for group, width in zip(groups, WIDTHS):
        skeleton_shape, pair_shape = (KMAX, width), (2 * KMAX, width)
        rows, skeleton = vmem_call(
            leaf_kernel, [(LEAF, width), skeleton_shape], [], "leaf_rows"
        )(info, ranks, pivots, *group)
        mid_rows, mid_skeleton = vmem_call(
            mid_kernel, [pair_shape, skeleton_shape], [], "mid_rows"
        )(info, ranks, pivots, skeleton, from_partner(skeleton, "col", 0))
        arrays += [rows, skeleton, mid_rows, mid_skeleton, from_partner(mid_skeleton, "col", 1)]
    scratch = [pltpu.VMEM((2 * KMAX, width), jnp.float32) for width in WIDTHS]
    scratch += [pltpu.VMEM((KMAX, width), jnp.float32) for width in WIDTHS]
    scratch += [pltpu.VMEM((2, BLOCK * BLOCK, 128), jnp.float32)] * 2
    outs = vmem_call(
        top_kernel,
        [(KMAX, LEAF), (KMAX, 2 * KMAX), (KMAX, 2 * KMAX), (KMAX, SAMPLES)],
        scratch,
        "interpolation",
    )(info, ranks, pivots, *arrays)
    return tuple(out[None] for out in outs)


def solution(mesh):
    return jax.shard_map(
        on_device,
        mesh=mesh,
        in_specs=(P("row", "col"), P(("col", "row"), None), P(), P(), P(), P(), P(), P()),
        out_specs=(
            P(("row", "col"), None, None),
            P(("row", "col"), None, None),
            P(("row", "col"), None, None),
            P(("row", "col"), None, None),
        ),
        check_vma=False,
    )
```

```python
import functools

import jax
import jax.numpy as jnp
from jax import lax
from jax.experimental import pallas as pl
from jax.experimental.pallas import tpu as pltpu
from jax.sharding import PartitionSpec as P

SAMPLES = 512
KMAX = 96
SIDE = 4
LEAF = 128
LEAVES = 128
WIDTHS = (256, 256)


def from_partner(value, axis, apart):
    mask = 2**apart
    pairs = [(source, source ^ mask) for source in range(lax.axis_size(axis))]
    return lax.ppermute(value, axis, pairs)


def pick_entry(table, position):
    return lax.dynamic_index_in_dim(table, position, 0, keepdims=False)


FIRST, SECOND = 1, 3
ORDERS = ((FIRST, SECOND), (SECOND, FIRST))


def row_mask(core, step, masks):
    along_y = (step < 2) == (core == 0)
    return masks[step % 2] * SIDE if along_y else masks[step % 2]


def from_row(value, step, masks):
    columns = 2 * SIDE
    pairs = []
    for row in range(SIDE * SIDE):
        for column in range(columns):
            partner = row ^ row_mask(column % 2, step, masks)
            pairs.append((row * columns + column, partner * columns + column))
    return lax.ppermute(value, ("row", "col"), pairs)


def origins(core, masks):
    found = [0]
    for step in range(4):
        found += [mask ^ row_mask(core, step, masks) for mask in found]
    return found


def gather_parts(sketch, before, after):
    depth = sketch.shape[0] // len(ORDERS)
    stacks = [sketch[None, part * depth : (part + 1) * depth] for part in range(len(ORDERS))]
    for step in range(3):
        received = [from_row(stack, step, masks) for stack, masks in zip(stacks, ORDERS)]
        if step == 1:
            received, before = lax.optimization_barrier((received, before))
        if step < 2:
            stacks = [jnp.concatenate(pair, 0) for pair in zip(stacks, received)]
    stacks, received, ready = lax.optimization_barrier((stacks, received, after(*before)))
    chunks, start = [], 0
    for width in WIDTHS:
        columns = slice(start, start + width)
        own = [
            jnp.concatenate([stack[:, :, columns], other[:, :, columns]], 0)
            for stack, other in zip(stacks, received)
        ]
        chunks.append(own + [from_row(value, 3, masks) for value, masks in zip(own, ORDERS)])
        start += width
    return chunks, ready


def split_kernel(value_ref, high_ref, low_ref):
    value = value_ref[...]
    rows = pl.ds(pl.multiple_of(pl.program_id(0) * LEAF, LEAF), LEAF)
    high = value.astype(jnp.bfloat16)
    high_ref[rows, :] = high
    low_ref[rows, :] = (value - high.astype(jnp.float32)).astype(jnp.bfloat16)


def split(value):
    rows, order = value.shape
    return pl.pallas_call(
        split_kernel,
        out_shape=[pltpu.VMEM(value.shape, jnp.bfloat16)] * 2,
        grid=(rows // LEAF,),
        in_specs=[pl.BlockSpec((LEAF, order), lambda i: (i, 0))],
        out_specs=[pl.BlockSpec(memory_space=pltpu.VMEM)] * 2,
        compiler_params=pltpu.CompilerParams(vmem_limit_bytes=6 * 2**20),
        cost_estimate=pl.CostEstimate(
            flops=4 * rows * order, bytes_accessed=8 * rows * order, transcendentals=0
        ),
        name="split",
    )(pltpu.with_memory_space_constraint(value, pltpu.HBM))


def convert(place_ref, pieces, high, low):
    parts = len(ORDERS)
    depth = pieces[0].shape[1]
    for part, masks in enumerate(ORDERS):
        for at, (mask_0, mask_1) in enumerate(zip(origins(0, masks), origins(1, masks))):
            source = pieces[part + parts * (at // 8)]
            mask = jnp.where(place_ref[2] == 0, mask_0, mask_1)
            block = jnp.bitwise_xor(place_ref[0], mask)
            start = pl.multiple_of((block * parts + part) * depth, depth)
            value = source[at % 8]
            top = value.astype(jnp.bfloat16)
            high[pl.ds(start, depth), :] = top
            low[pl.ds(start, depth), :] = (value - top.astype(jnp.float32)).astype(jnp.bfloat16)


def multiply(place_ref, core, a_high, a_low, high, low, total, out_ref):
    left = a_high[:, core].reshape(-1, high.shape[0])
    low_left = a_low[:, core].reshape(-1, high.shape[0])
    right = high[...]
    total[...] = jnp.dot(
        jnp.concatenate([left, left, low_left], 1),
        jnp.concatenate([right, low[...], right], 0),
        preferred_element_type=jnp.float32,
    ).reshape(total.shape)
    orders = zip((0, SECOND, FIRST, FIRST ^ SECOND), (0, FIRST, SECOND, FIRST ^ SECOND))
    for at, masks in enumerate(orders):
        chip = jnp.bitwise_xor(place_ref[1], jnp.where(core == 0, *masks))
        out_ref[at] = total[chip]


def other_kernel(place_ref, a_high, a_low, *refs):
    pieces = refs[: 2 * len(ORDERS)]
    out_ref, high, low, total = refs[2 * len(ORDERS) :]
    convert(place_ref, pieces, high, low)
    multiply(place_ref, 1 - place_ref[2], a_high, a_low, high, low, total, out_ref)


def own_kernel(place_ref, a_high, a_low, high, low, out_ref, total):
    multiply(place_ref, place_ref[2], a_high, a_low, high, low, total, out_ref)


def product(kernel, place, halves, arrays, outs, cost, name):
    in_vmem = pl.BlockSpec(memory_space=pltpu.VMEM)
    halves = [pltpu.with_memory_space_constraint(half, pltpu.VMEM) for half in halves]
    return pl.pallas_call(
        kernel,
        out_shape=outs,
        in_specs=[pl.BlockSpec(memory_space=pltpu.SMEM)] + [in_vmem] * (2 + len(arrays)),
        out_specs=[in_vmem] * len(outs),
        scratch_shapes=[pltpu.VMEM(outs[0].shape, jnp.float32)],
        compiler_params=pltpu.CompilerParams(vmem_limit_bytes=8 * 2**20),
        cost_estimate=pl.CostEstimate(flops=cost, bytes_accessed=cost // 400, transcendentals=0),
        name=name,
    )(place, *halves, *arrays)


def product_other(halves, pieces, place):
    leaves, _, leaf, order = halves[0].shape
    width = pieces[0].shape[-1]
    outs = [jax.ShapeDtypeStruct((leaves, leaf, width), jnp.float32)]
    outs += [jax.ShapeDtypeStruct((order, width), jnp.bfloat16)] * 2
    return product(other_kernel, place, halves, pieces, outs, 1, "product_other")


def product_own(halves, sketch, place, last):
    leaves, _, leaf, order = halves[0].shape
    width = sketch[0].shape[-1]
    outs = [jax.ShapeDtypeStruct((leaves, leaf, width), jnp.float32)]
    cost = 6 * leaves * leaf * order * width if last else 1
    return product(own_kernel, place, halves, sketch, outs, cost, "product_own")[0]


def from_x(value, step):
    pairs = []
    for column in range(2 * SIDE):
        mask = ORDERS[column % 2][step]
        pairs.append((column, column ^ (2 * mask)))
    return lax.ppermute(value, "col", pairs)


def sum_over_x(core_sum):
    kept = from_x(core_sum[2:], 0)
    return [core_sum[0], kept[0], from_x(core_sum[1] + kept[1], 1)]


BLOCK = 8
NODES = 3


def lane_of(value, lane):
    return jnp.broadcast_to(value[:, lane : lane + 1], value.shape)


def invert_pivot(entry):
    def at(i, j):
        return entry[max(i, j)][min(i, j)]

    def put(i, j, value):
        entry[max(i, j)][min(i, j)] = value

    for p in range(0, BLOCK, 2):
        q = p + 1
        a, b, c = at(p, p), at(q, p), at(q, q)
        scale = 1.0 / (a * c - b * b)
        w_pp, w_pq, w_qq = c * scale, -b * scale, a * scale
        rest = [i for i in range(BLOCK) if i not in (p, q)]
        first = {i: at(i, p) for i in rest}
        second = {i: at(i, q) for i in rest}
        left = {i: w_pp * first[i] + w_pq * second[i] for i in rest}
        right = {i: w_pq * first[i] + w_qq * second[i] for i in rest}
        for i in rest:
            for j in rest:
                if j <= i:
                    put(i, j, at(i, j) - (left[i] * first[j] + right[i] * second[j]))
        for i in rest:
            put(i, p, left[i])
            put(i, q, right[i])
        put(p, p, -w_pp)
        put(q, p, -w_pq)
        put(q, q, -w_qq)
    return at


def sweep(tiles, rows_scratch, new_scratch):
    lanes = lax.broadcasted_iota(jnp.int32, (BLOCK, 128), 1)
    count = KMAX // BLOCK
    for block in range(count):
        at_lane = block * BLOCK
        slot = block % 2
        inside = (lanes >= at_lane) & (lanes < at_lane + BLOCK)
        for node in range(NODES):
            rows_scratch[slot, node * BLOCK : (node + 1) * BLOCK, :] = tiles[node][block]
        rows = [rows_scratch[slot, pl.ds(k, BLOCK, stride=BLOCK), :] for k in range(BLOCK)]
        entry = [[lane_of(rows[k], at_lane + i) for i in range(k + 1)] for k in range(BLOCK)]
        at = invert_pivot(entry)
        wide = [
            jnp.where(lanes == at_lane + k, 1.0, jnp.where(inside, 0.0, -rows[k]))
            for k in range(BLOCK)
        ]
        for k in range(BLOCK):
            total = at(k, 0) * wide[0]
            for i in range(1, BLOCK):
                total = total + at(k, i) * wide[i]
            new_scratch[slot, pl.ds(k, BLOCK, stride=BLOCK), :] = total
        for node in range(NODES):
            new_rows = [
                jnp.broadcast_to(
                    new_scratch[slot, node * BLOCK + k : node * BLOCK + k + 1, :], (BLOCK, 128)
                )
                for k in range(BLOCK)
            ]
            for t in range(count):
                if t == block:
                    continue
                old = tiles[node][t]
                value = jnp.where(inside, 0.0, old)
                for k in range(BLOCK):
                    value = value - lane_of(old, at_lane + k) * new_rows[k]
                tiles[node][t] = value
            tiles[node][block] = new_scratch[slot, node * BLOCK : (node + 1) * BLOCK, :]
    return tiles


def invert_all(matrices, rows_scratch, new_scratch):
    count = KMAX // BLOCK
    lanes = lax.broadcasted_iota(jnp.int32, (BLOCK, 128), 1)
    sublanes = lax.broadcasted_iota(jnp.int32, (BLOCK, 128), 0)
    rows_scratch[...] = jnp.zeros_like(rows_scratch)
    all_tiles, all_down, all_across = [], [], []
    for matrix in matrices:
        wide = jnp.concatenate([matrix, jnp.zeros((KMAX, 128 - KMAX), jnp.float32)], 1)
        tiles = [wide[t * BLOCK : (t + 1) * BLOCK] for t in range(count)]
        on_diagonal = [
            jnp.where(lanes == sublanes + t * BLOCK, tiles[t], 0.0) for t in range(count)
        ]
        down = [lax.rsqrt(jnp.sum(part, axis=1, keepdims=True)) for part in on_diagonal]
        line = functools.reduce(jnp.add, on_diagonal)
        line = jnp.sum(line, axis=0, keepdims=True)
        across = lax.rsqrt(jnp.where(lanes[:1] < KMAX, line, 1.0))
        all_tiles.append([tiles[t] * down[t] * across for t in range(count)])
        all_down.append(down)
        all_across.append(across)
    all_tiles = sweep(all_tiles, rows_scratch, new_scratch)
    inverses = []
    for tiles, down, across in zip(all_tiles, all_down, all_across):
        scaled = [-(tiles[t] * down[t] * across) for t in range(count)]
        inverses.append(jnp.concatenate(scaled, 0)[:, :KMAX])
    return inverses


def select_rows(source, pivots_ref, node, rank, target, target_at):
    for row in range(KMAX):
        picked = source[pl.ds(pivots_ref[node, row], 1), :]
        target[target_at + row : target_at + row + 1, :] = jnp.where(row < rank, picked, 0.0)


def rank_of(info_ref, ranks_ref, level):
    place = info_ref[0] // 2**level
    starts = [0, LEAVES, LEAVES + LEAVES // 2]
    return ranks_ref[starts[level] + place]


def leaf_kernel(info_ref, ranks_ref, pivots_ref, *refs):
    parts, (rows_ref, skeleton_ref) = refs[:-2], refs[-2:]
    rows_ref[...] = functools.reduce(jnp.add, [part[...] for part in parts])
    select_rows(rows_ref, pivots_ref, 0, rank_of(info_ref, ranks_ref, 0), skeleton_ref, 0)


def mid_kernel(info_ref, ranks_ref, pivots_ref, own_ref, other_ref, rows_ref, skeleton_ref):
    own_at = pl.multiple_of((info_ref[0] % 2) * KMAX, KMAX)
    other_at = pl.multiple_of((1 - info_ref[0] % 2) * KMAX, KMAX)
    rows_ref[pl.ds(own_at, KMAX), :] = own_ref[...]
    rows_ref[pl.ds(other_at, KMAX), :] = other_ref[...]
    select_rows(rows_ref, pivots_ref, 1, rank_of(info_ref, ranks_ref, 1), skeleton_ref, 0)


def top_kernel(info_ref, ranks_ref, pivots_ref, *refs):
    chunks = len(WIDTHS)
    groups = [refs[5 * chunk : 5 * chunk + 5] for chunk in range(chunks)]
    leaf_out, mid_out, top_out, rows_out = refs[5 * chunks : 5 * chunks + 4]
    scratch = refs[5 * chunks + 4 :]
    tops, chosen, (rows_scratch, new_scratch) = (
        scratch[:chunks], scratch[chunks : 2 * chunks], scratch[2 * chunks :]
    )
    own_at = pl.multiple_of((info_ref[0] // 2 % 2) * KMAX, KMAX)
    other_at = pl.multiple_of((1 - info_ref[0] // 2 % 2) * KMAX, KMAX)
    start = 0
    for group, top, skeleton in zip(groups, tops, chosen):
        top[pl.ds(own_at, KMAX), :] = group[3][...]
        top[pl.ds(other_at, KMAX), :] = group[4][...]
        select_rows(top, pivots_ref, 2, rank_of(info_ref, ranks_ref, 2), skeleton, 0)
        width = skeleton.shape[-1]
        rows_out[:, start : start + width] = skeleton[...]
        start += width
    row_ids = lax.broadcasted_iota(jnp.int32, (KMAX, KMAX), 0)
    column_ids = lax.broadcasted_iota(jnp.int32, (KMAX, KMAX), 1)
    dot = functools.partial(
        lax.dot_general,
        dimension_numbers=(((1,), (1,)), ((), ())),
        precision=lax.Precision.HIGHEST,
        preferred_element_type=jnp.float32,
    )
    levels = (
        ([group[0] for group in groups], [group[1] for group in groups]),
        ([group[2] for group in groups], [group[3] for group in groups]),
        (tops, chosen),
    )
    grams, crosses = [], []
    for node, (rows, skeletons) in enumerate(levels):
        gram = functools.reduce(jnp.add, [dot(part[...], part[...]) for part in skeletons])
        cross = functools.reduce(
            jnp.add, [dot(row[...], part[...]) for row, part in zip(rows, skeletons)]
        )
        empty = (row_ids == column_ids) & (row_ids >= rank_of(info_ref, ranks_ref, node))
        grams.append(gram * (1.0 / SAMPLES) + jnp.where(empty, 1.0, 0.0))
        crosses.append(cross * (1.0 / SAMPLES))
    inverses = invert_all(grams, rows_scratch, new_scratch)
    for inverse, cross, out in zip(inverses, crosses, (leaf_out, mid_out, top_out)):
        out[...] = dot(inverse, cross)


def vmem_call(kernel, outs, scratch, name):
    in_vmem = pl.BlockSpec(memory_space=pltpu.VMEM)

    def call(info, ranks, pivots, *arrays):
        return pl.pallas_call(
            kernel,
            out_shape=[jax.ShapeDtypeStruct(shape, jnp.float32) for shape in outs],
            in_specs=[pl.BlockSpec(memory_space=pltpu.SMEM)] * 3 + [in_vmem] * len(arrays),
            out_specs=[in_vmem] * len(outs),
            scratch_shapes=scratch,
            compiler_params=pltpu.CompilerParams(vmem_limit_bytes=6 * 2**20),
            name=name,
        )(info, ranks, pivots, *arrays)

    return call


def on_device(
    frontal, sketch, leaf_ranks, leaf_pivots, mid_ranks, mid_pivots, top_ranks, top_pivots
):
    col_count = lax.axis_size("col")
    col_index = lax.axis_index("col")
    row_index = lax.axis_index("row")
    leaf_index = row_index * col_count + col_index
    place = jnp.stack([row_index, col_index // 2, col_index % 2]).astype(jnp.int32)
    nodes = (leaf_index, leaf_index // 2, leaf_index // 4)

    def prepare(frontal, *tables):
        ranks = jnp.concatenate(tables[:3])
        pivots = [pick_entry(table, node)[:KMAX] for table, node in zip(tables[3:], nodes)]
        return (*split(frontal), ranks, jnp.stack(pivots))

    tables = (leaf_ranks, mid_ranks, top_ranks, leaf_pivots, mid_pivots, top_pivots)
    chunks, (high, low, ranks, pivots) = gather_parts(sketch, (frontal, *tables), prepare)
    info = jnp.stack([leaf_index]).astype(jnp.int32)
    halves = [part.reshape(SIDE, 2, LEAF, -1) for part in (high, low)]
    core_sums, own = [], ()
    for chunk, pieces in enumerate(chunks):
        place, own = lax.optimization_barrier((place, own))
        other, *parts = product_other(halves, pieces, place)
        received = from_partner(other, "col", 0)
        last = chunk == len(chunks) - 1
        if chunk > 0:
            core_sums[-1] = own + core_sums[-1]
            place, core_sums = lax.optimization_barrier((place, core_sums))
        own = product_own(halves, parts, place, last)
        core_sums.append(received)
    core_sums[-1] = own + core_sums[-1]
    groups = [sum_over_x(core_sum) for core_sum in core_sums]
    arrays = []
    for group, width in zip(groups, WIDTHS):
        skeleton_shape, pair_shape = (KMAX, width), (2 * KMAX, width)
        rows, skeleton = vmem_call(
            leaf_kernel, [(LEAF, width), skeleton_shape], [], "leaf_rows"
        )(info, ranks, pivots, *group)
        mid_rows, mid_skeleton = vmem_call(
            mid_kernel, [pair_shape, skeleton_shape], [], "mid_rows"
        )(info, ranks, pivots, skeleton, from_partner(skeleton, "col", 0))
        arrays += [rows, skeleton, mid_rows, mid_skeleton, from_partner(mid_skeleton, "col", 1)]
    scratch = [pltpu.VMEM((2 * KMAX, width), jnp.float32) for width in WIDTHS]
    scratch += [pltpu.VMEM((KMAX, width), jnp.float32) for width in WIDTHS]
    scratch += [pltpu.VMEM((2, BLOCK * BLOCK, 128), jnp.float32)] * 2
    outs = vmem_call(
        top_kernel,
        [(KMAX, LEAF), (KMAX, 2 * KMAX), (KMAX, 2 * KMAX), (KMAX, SAMPLES)],
        scratch,
        "interpolation",
    )(info, ranks, pivots, *arrays)
    return tuple(out[None] for out in outs)


def solution(mesh):
    return jax.shard_map(
        on_device,
        mesh=mesh,
        in_specs=(P("row", "col"), P(("col", "row"), None), P(), P(), P(), P(), P(), P()),
        out_specs=(
            P(("row", "col"), None, None),
            P(("row", "col"), None, None),
            P(("row", "col"), None, None),
            P(("row", "col"), None, None),
        ),
        check_vma=False,
    )
```

```python
import functools

import jax
import jax.numpy as jnp
from jax import lax
from jax.experimental import pallas as pl
from jax.experimental.pallas import tpu as pltpu
from jax.sharding import PartitionSpec as P

SAMPLES = 512
KMAX = 96
SIDE = 4
LEAF = 128
LEAVES = 128
WIDTHS = (256, 256)


def from_partner(value, axis, apart):
    mask = 2**apart
    pairs = [(source, source ^ mask) for source in range(lax.axis_size(axis))]
    return lax.ppermute(value, axis, pairs)


def pick_entry(table, position):
    return lax.dynamic_index_in_dim(table, position, 0, keepdims=False)


FIRST, SECOND = 1, 3
ORDERS = ((FIRST, SECOND), (SECOND, FIRST))


def row_mask(core, step, masks):
    along_y = (step < 2) == (core == 0)
    return masks[step % 2] * SIDE if along_y else masks[step % 2]


def from_row(value, step, masks):
    columns = 2 * SIDE
    pairs = []
    for row in range(SIDE * SIDE):
        for column in range(columns):
            partner = row ^ row_mask(column % 2, step, masks)
            pairs.append((row * columns + column, partner * columns + column))
    return lax.ppermute(value, ("row", "col"), pairs)


def origins(core, masks):
    found = [0]
    for step in range(4):
        found += [mask ^ row_mask(core, step, masks) for mask in found]
    return found


def gather_parts(sketch, frontal, before, after):
    depth = sketch.shape[0] // len(ORDERS)
    stacks = [sketch[None, part * depth : (part + 1) * depth] for part in range(len(ORDERS))]
    for step in range(3):
        received = [from_row(stack, step, masks) for stack, masks in zip(stacks, ORDERS)]
        if step == 1:
            received, before = lax.optimization_barrier((received, before))
        if step < 2:
            stacks = [jnp.concatenate(pair, 0) for pair in zip(stacks, received)]
    stacks, received, ready, frontal = lax.optimization_barrier(
        (stacks, received, after(*before), frontal)
    )
    chunks, start = [], 0
    for width in WIDTHS:
        columns = slice(start, start + width)
        own = [
            jnp.concatenate([stack[:, :, columns], other[:, :, columns]], 0)
            for stack, other in zip(stacks, received)
        ]
        chunks.append(own + [from_row(value, 3, masks) for value, masks in zip(own, ORDERS)])
        start += width
    return chunks, ready, frontal


def split_kernel(value_ref, high_ref, low_ref):
    value = value_ref[...]
    rows = pl.ds(pl.multiple_of(pl.program_id(0) * LEAF, LEAF), LEAF)
    high = value.astype(jnp.bfloat16)
    high_ref[rows, :] = high
    low_ref[rows, :] = (value - high.astype(jnp.float32)).astype(jnp.bfloat16)


def split(value):
    rows, order = value.shape
    return pl.pallas_call(
        split_kernel,
        out_shape=[pltpu.VMEM(value.shape, jnp.bfloat16)] * 2,
        grid=(rows // LEAF,),
        in_specs=[pl.BlockSpec((LEAF, order), lambda i: (i, 0))],
        out_specs=[pl.BlockSpec(memory_space=pltpu.VMEM)] * 2,
        compiler_params=pltpu.CompilerParams(vmem_limit_bytes=6 * 2**20),
        cost_estimate=pl.CostEstimate(
            flops=4 * rows * order, bytes_accessed=8 * rows * order, transcendentals=0
        ),
        name="split",
    )(pltpu.with_memory_space_constraint(value, pltpu.HBM))


def convert(place_ref, pieces, high, low):
    parts = len(ORDERS)
    depth = pieces[0].shape[1]
    for part, masks in enumerate(ORDERS):
        for at, (mask_0, mask_1) in enumerate(zip(origins(0, masks), origins(1, masks))):
            source = pieces[part + parts * (at // 8)]
            mask = jnp.where(place_ref[2] == 0, mask_0, mask_1)
            block = jnp.bitwise_xor(place_ref[0], mask)
            start = pl.multiple_of((block * parts + part) * depth, depth)
            value = source[at % 8]
            top = value.astype(jnp.bfloat16)
            high[pl.ds(start, depth), :] = top
            low[pl.ds(start, depth), :] = (value - top.astype(jnp.float32)).astype(jnp.bfloat16)


def multiply(place_ref, core, a_high, a_low, high, low, total, out_ref):
    left = a_high[:, core].reshape(-1, high.shape[0])
    low_left = a_low[:, core].reshape(-1, high.shape[0])
    right = high[...]
    total[...] = jnp.dot(
        jnp.concatenate([left, left, low_left], 1),
        jnp.concatenate([right, low[...], right], 0),
        preferred_element_type=jnp.float32,
    ).reshape(total.shape)
    orders = zip((0, SECOND, FIRST, FIRST ^ SECOND), (0, FIRST, SECOND, FIRST ^ SECOND))
    for at, masks in enumerate(orders):
        chip = jnp.bitwise_xor(place_ref[1], jnp.where(core == 0, *masks))
        out_ref[at] = total[chip]


def other_kernel(place_ref, a_high, a_low, *refs):
    pieces = refs[: 2 * len(ORDERS)]
    out_ref, high, low, total = refs[2 * len(ORDERS) :]
    convert(place_ref, pieces, high, low)
    multiply(place_ref, 1 - place_ref[2], a_high, a_low, high, low, total, out_ref)


def own_kernel(place_ref, a_high, a_low, high, low, out_ref, total):
    multiply(place_ref, place_ref[2], a_high, a_low, high, low, total, out_ref)


def product(kernel, place, halves, arrays, outs, cost, name):
    in_vmem = pl.BlockSpec(memory_space=pltpu.VMEM)
    halves = [pltpu.with_memory_space_constraint(half, pltpu.VMEM) for half in halves]
    return pl.pallas_call(
        kernel,
        out_shape=outs,
        in_specs=[pl.BlockSpec(memory_space=pltpu.SMEM)] + [in_vmem] * (2 + len(arrays)),
        out_specs=[in_vmem] * len(outs),
        scratch_shapes=[pltpu.VMEM(outs[0].shape, jnp.float32)],
        compiler_params=pltpu.CompilerParams(vmem_limit_bytes=8 * 2**20),
        cost_estimate=pl.CostEstimate(flops=cost, bytes_accessed=cost // 400, transcendentals=0),
        name=name,
    )(place, *halves, *arrays)


def product_other(halves, pieces, place):
    leaves, _, leaf, order = halves[0].shape
    width = pieces[0].shape[-1]
    outs = [jax.ShapeDtypeStruct((leaves, leaf, width), jnp.float32)]
    outs += [jax.ShapeDtypeStruct((order, width), jnp.bfloat16)] * 2
    return product(other_kernel, place, halves, pieces, outs, 1, "product_other")


def product_own(halves, sketch, place, last):
    leaves, _, leaf, order = halves[0].shape
    width = sketch[0].shape[-1]
    outs = [jax.ShapeDtypeStruct((leaves, leaf, width), jnp.float32)]
    cost = 6 * leaves * leaf * order * width if last else 1
    return product(own_kernel, place, halves, sketch, outs, cost, "product_own")[0]


def from_x(value, step):
    pairs = []
    for column in range(2 * SIDE):
        mask = ORDERS[column % 2][step]
        pairs.append((column, column ^ (2 * mask)))
    return lax.ppermute(value, "col", pairs)


def sum_over_x(core_sum):
    kept = from_x(core_sum[2:], 0)
    return [core_sum[0], kept[0], from_x(core_sum[1] + kept[1], 1)]


BLOCK = 8
NODES = 3


def lane_of(value, lane):
    return jnp.broadcast_to(value[:, lane : lane + 1], value.shape)


def invert_pivot(entry):
    def at(i, j):
        return entry[max(i, j)][min(i, j)]

    def put(i, j, value):
        entry[max(i, j)][min(i, j)] = value

    for p in range(0, BLOCK, 2):
        q = p + 1
        a, b, c = at(p, p), at(q, p), at(q, q)
        scale = 1.0 / (a * c - b * b)
        w_pp, w_pq, w_qq = c * scale, -b * scale, a * scale
        rest = [i for i in range(BLOCK) if i not in (p, q)]
        first = {i: at(i, p) for i in rest}
        second = {i: at(i, q) for i in rest}
        left = {i: w_pp * first[i] + w_pq * second[i] for i in rest}
        right = {i: w_pq * first[i] + w_qq * second[i] for i in rest}
        for i in rest:
            for j in rest:
                if j <= i:
                    put(i, j, at(i, j) - (left[i] * first[j] + right[i] * second[j]))
        for i in rest:
            put(i, p, left[i])
            put(i, q, right[i])
        put(p, p, -w_pp)
        put(q, p, -w_pq)
        put(q, q, -w_qq)
    return at


def sweep(tiles, rows_scratch, new_scratch):
    lanes = lax.broadcasted_iota(jnp.int32, (BLOCK, 128), 1)
    count = KMAX // BLOCK
    for block in range(count):
        at_lane = block * BLOCK
        slot = block % 2
        inside = (lanes >= at_lane) & (lanes < at_lane + BLOCK)
        for node in range(NODES):
            rows_scratch[slot, node * BLOCK : (node + 1) * BLOCK, :] = tiles[node][block]
        rows = [rows_scratch[slot, pl.ds(k, BLOCK, stride=BLOCK), :] for k in range(BLOCK)]
        entry = [[lane_of(rows[k], at_lane + i) for i in range(k + 1)] for k in range(BLOCK)]
        at = invert_pivot(entry)
        wide = [
            jnp.where(lanes == at_lane + k, 1.0, jnp.where(inside, 0.0, -rows[k]))
            for k in range(BLOCK)
        ]
        for k in range(BLOCK):
            total = at(k, 0) * wide[0]
            for i in range(1, BLOCK):
                total = total + at(k, i) * wide[i]
            new_scratch[slot, pl.ds(k, BLOCK, stride=BLOCK), :] = total
        for node in range(NODES):
            new_rows = [
                jnp.broadcast_to(
                    new_scratch[slot, node * BLOCK + k : node * BLOCK + k + 1, :], (BLOCK, 128)
                )
                for k in range(BLOCK)
            ]
            for t in range(count):
                if t == block:
                    continue
                old = tiles[node][t]
                value = jnp.where(inside, 0.0, old)
                for k in range(BLOCK):
                    value = value - lane_of(old, at_lane + k) * new_rows[k]
                tiles[node][t] = value
            tiles[node][block] = new_scratch[slot, node * BLOCK : (node + 1) * BLOCK, :]
    return tiles


def invert_all(matrices, rows_scratch, new_scratch):
    count = KMAX // BLOCK
    lanes = lax.broadcasted_iota(jnp.int32, (BLOCK, 128), 1)
    sublanes = lax.broadcasted_iota(jnp.int32, (BLOCK, 128), 0)
    rows_scratch[...] = jnp.zeros_like(rows_scratch)
    all_tiles, all_down, all_across = [], [], []
    for matrix in matrices:
        wide = jnp.concatenate([matrix, jnp.zeros((KMAX, 128 - KMAX), jnp.float32)], 1)
        tiles = [wide[t * BLOCK : (t + 1) * BLOCK] for t in range(count)]
        on_diagonal = [
            jnp.where(lanes == sublanes + t * BLOCK, tiles[t], 0.0) for t in range(count)
        ]
        down = [lax.rsqrt(jnp.sum(part, axis=1, keepdims=True)) for part in on_diagonal]
        line = functools.reduce(jnp.add, on_diagonal)
        line = jnp.sum(line, axis=0, keepdims=True)
        across = lax.rsqrt(jnp.where(lanes[:1] < KMAX, line, 1.0))
        all_tiles.append([tiles[t] * down[t] * across for t in range(count)])
        all_down.append(down)
        all_across.append(across)
    all_tiles = sweep(all_tiles, rows_scratch, new_scratch)
    inverses = []
    for tiles, down, across in zip(all_tiles, all_down, all_across):
        scaled = [-(tiles[t] * down[t] * across) for t in range(count)]
        inverses.append(jnp.concatenate(scaled, 0)[:, :KMAX])
    return inverses


def select_rows(source, pivots_ref, node, rank, target, target_at):
    for row in range(KMAX):
        picked = source[pl.ds(pivots_ref[node, row], 1), :]
        target[target_at + row : target_at + row + 1, :] = jnp.where(row < rank, picked, 0.0)


def rank_of(info_ref, ranks_ref, level):
    place = info_ref[0] // 2**level
    starts = [0, LEAVES, LEAVES + LEAVES // 2]
    return ranks_ref[starts[level] + place]


def leaf_kernel(info_ref, ranks_ref, pivots_ref, *refs):
    parts, (rows_ref, skeleton_ref) = refs[:-2], refs[-2:]
    rows_ref[...] = functools.reduce(jnp.add, [part[...] for part in parts])
    select_rows(rows_ref, pivots_ref, 0, rank_of(info_ref, ranks_ref, 0), skeleton_ref, 0)


def mid_kernel(info_ref, ranks_ref, pivots_ref, own_ref, other_ref, rows_ref, skeleton_ref):
    own_at = pl.multiple_of((info_ref[0] % 2) * KMAX, KMAX)
    other_at = pl.multiple_of((1 - info_ref[0] % 2) * KMAX, KMAX)
    rows_ref[pl.ds(own_at, KMAX), :] = own_ref[...]
    rows_ref[pl.ds(other_at, KMAX), :] = other_ref[...]
    select_rows(rows_ref, pivots_ref, 1, rank_of(info_ref, ranks_ref, 1), skeleton_ref, 0)


def top_kernel(info_ref, ranks_ref, pivots_ref, *refs):
    chunks = len(WIDTHS)
    groups = [refs[5 * chunk : 5 * chunk + 5] for chunk in range(chunks)]
    leaf_out, mid_out, top_out, rows_out = refs[5 * chunks : 5 * chunks + 4]
    scratch = refs[5 * chunks + 4 :]
    tops, chosen, (rows_scratch, new_scratch) = (
        scratch[:chunks], scratch[chunks : 2 * chunks], scratch[2 * chunks :]
    )
    own_at = pl.multiple_of((info_ref[0] // 2 % 2) * KMAX, KMAX)
    other_at = pl.multiple_of((1 - info_ref[0] // 2 % 2) * KMAX, KMAX)
    start = 0
    for group, top, skeleton in zip(groups, tops, chosen):
        top[pl.ds(own_at, KMAX), :] = group[3][...]
        top[pl.ds(other_at, KMAX), :] = group[4][...]
        select_rows(top, pivots_ref, 2, rank_of(info_ref, ranks_ref, 2), skeleton, 0)
        width = skeleton.shape[-1]
        rows_out[:, start : start + width] = skeleton[...]
        start += width
    row_ids = lax.broadcasted_iota(jnp.int32, (KMAX, KMAX), 0)
    column_ids = lax.broadcasted_iota(jnp.int32, (KMAX, KMAX), 1)
    dot = functools.partial(
        lax.dot_general,
        dimension_numbers=(((1,), (1,)), ((), ())),
        precision=lax.Precision.HIGHEST,
        preferred_element_type=jnp.float32,
    )
    levels = (
        ([group[0] for group in groups], [group[1] for group in groups]),
        ([group[2] for group in groups], [group[3] for group in groups]),
        (tops, chosen),
    )
    grams, crosses = [], []
    for node, (rows, skeletons) in enumerate(levels):
        gram = functools.reduce(jnp.add, [dot(part[...], part[...]) for part in skeletons])
        cross = functools.reduce(
            jnp.add, [dot(row[...], part[...]) for row, part in zip(rows, skeletons)]
        )
        empty = (row_ids == column_ids) & (row_ids >= rank_of(info_ref, ranks_ref, node))
        grams.append(gram * (1.0 / SAMPLES) + jnp.where(empty, 1.0, 0.0))
        crosses.append(cross * (1.0 / SAMPLES))
    inverses = invert_all(grams, rows_scratch, new_scratch)
    for inverse, cross, out in zip(inverses, crosses, (leaf_out, mid_out, top_out)):
        out[...] = dot(inverse, cross)


def vmem_call(kernel, outs, scratch, name):
    in_vmem = pl.BlockSpec(memory_space=pltpu.VMEM)

    def call(info, ranks, pivots, *arrays):
        return pl.pallas_call(
            kernel,
            out_shape=[jax.ShapeDtypeStruct(shape, jnp.float32) for shape in outs],
            in_specs=[pl.BlockSpec(memory_space=pltpu.SMEM)] * 3 + [in_vmem] * len(arrays),
            out_specs=[in_vmem] * len(outs),
            scratch_shapes=scratch,
            compiler_params=pltpu.CompilerParams(vmem_limit_bytes=6 * 2**20),
            name=name,
        )(info, ranks, pivots, *arrays)

    return call


def on_device(
    frontal, sketch, leaf_ranks, leaf_pivots, mid_ranks, mid_pivots, top_ranks, top_pivots
):
    col_count = lax.axis_size("col")
    col_index = lax.axis_index("col")
    row_index = lax.axis_index("row")
    leaf_index = row_index * col_count + col_index
    place = jnp.stack([row_index, col_index // 2, col_index % 2]).astype(jnp.int32)
    nodes = (leaf_index, leaf_index // 2, leaf_index // 4)

    def prepare(*tables):
        ranks = jnp.concatenate(tables[:3])
        pivots = [pick_entry(table, node)[:KMAX] for table, node in zip(tables[3:], nodes)]
        return ranks, jnp.stack(pivots)

    tables = (leaf_ranks, mid_ranks, top_ranks, leaf_pivots, mid_pivots, top_pivots)
    chunks, (ranks, pivots), frontal = gather_parts(sketch, frontal, tables, prepare)
    info = jnp.stack([leaf_index]).astype(jnp.int32)
    halves = [part.reshape(SIDE, 2, LEAF, -1) for part in split(frontal)]
    core_sums, own = [], ()
    for chunk, pieces in enumerate(chunks):
        place, own = lax.optimization_barrier((place, own))
        other, *parts = product_other(halves, pieces, place)
        received = from_partner(other, "col", 0)
        last = chunk == len(chunks) - 1
        if chunk > 0:
            core_sums[-1] = own + core_sums[-1]
            place, core_sums = lax.optimization_barrier((place, core_sums))
        own = product_own(halves, parts, place, last)
        core_sums.append(received)
    core_sums[-1] = own + core_sums[-1]
    groups = [sum_over_x(core_sum) for core_sum in core_sums]
    arrays = []
    for group, width in zip(groups, WIDTHS):
        skeleton_shape, pair_shape = (KMAX, width), (2 * KMAX, width)
        rows, skeleton = vmem_call(
            leaf_kernel, [(LEAF, width), skeleton_shape], [], "leaf_rows"
        )(info, ranks, pivots, *group)
        mid_rows, mid_skeleton = vmem_call(
            mid_kernel, [pair_shape, skeleton_shape], [], "mid_rows"
        )(info, ranks, pivots, skeleton, from_partner(skeleton, "col", 0))
        arrays += [rows, skeleton, mid_rows, mid_skeleton, from_partner(mid_skeleton, "col", 1)]
    scratch = [pltpu.VMEM((2 * KMAX, width), jnp.float32) for width in WIDTHS]
    scratch += [pltpu.VMEM((KMAX, width), jnp.float32) for width in WIDTHS]
    scratch += [pltpu.VMEM((2, BLOCK * BLOCK, 128), jnp.float32)] * 2
    outs = vmem_call(
        top_kernel,
        [(KMAX, LEAF), (KMAX, 2 * KMAX), (KMAX, 2 * KMAX), (KMAX, SAMPLES)],
        scratch,
        "interpolation",
    )(info, ranks, pivots, *arrays)
    return tuple(out[None] for out in outs)


def solution(mesh):
    return jax.shard_map(
        on_device,
        mesh=mesh,
        in_specs=(P("row", "col"), P(("col", "row"), None), P(), P(), P(), P(), P(), P()),
        out_specs=(
            P(("row", "col"), None, None),
            P(("row", "col"), None, None),
            P(("row", "col"), None, None),
            P(("row", "col"), None, None),
        ),
        check_vma=False,
    )
```

```python
import functools

import jax
import jax.numpy as jnp
from jax import lax
from jax.experimental import pallas as pl
from jax.experimental.pallas import tpu as pltpu
from jax.sharding import PartitionSpec as P

SAMPLES = 512
KMAX = 96
SIDE = 4
LEAF = 128
LEAVES = 128
WIDTHS = (256, 256)


def from_partner(value, axis, apart):
    mask = 2**apart
    pairs = [(source, source ^ mask) for source in range(lax.axis_size(axis))]
    return lax.ppermute(value, axis, pairs)


def pick_entry(table, position):
    return lax.dynamic_index_in_dim(table, position, 0, keepdims=False)


FIRST, SECOND = 1, 3
ORDERS = ((FIRST, SECOND), (SECOND, FIRST))


def row_mask(core, step, masks):
    along_y = (step < 2) == (core == 0)
    return masks[step % 2] * SIDE if along_y else masks[step % 2]


def from_row(value, step, masks):
    columns = 2 * SIDE
    pairs = []
    for row in range(SIDE * SIDE):
        for column in range(columns):
            partner = row ^ row_mask(column % 2, step, masks)
            pairs.append((row * columns + column, partner * columns + column))
    return lax.ppermute(value, ("row", "col"), pairs)


def origins(core, masks):
    found = [0]
    for step in range(4):
        found += [mask ^ row_mask(core, step, masks) for mask in found]
    return found


def gather_parts(sketch, frontal, before, after):
    depth = sketch.shape[0] // len(ORDERS)
    stacks = [sketch[None, part * depth : (part + 1) * depth] for part in range(len(ORDERS))]
    for step in range(3):
        received = [from_row(stack, step, masks) for stack, masks in zip(stacks, ORDERS)]
        if step == 1:
            received, before = lax.optimization_barrier((received, before))
        if step < 2:
            stacks = [jnp.concatenate(pair, 0) for pair in zip(stacks, received)]
    stacks, received, ready, frontal = lax.optimization_barrier(
        (stacks, received, after(*before), frontal)
    )
    chunks, start = [], 0
    for width in WIDTHS:
        columns = slice(start, start + width)
        own = [
            jnp.concatenate([stack[:, :, columns], other[:, :, columns]], 0)
            for stack, other in zip(stacks, received)
        ]
        chunks.append(own + [from_row(value, 3, masks) for value, masks in zip(own, ORDERS)])
        start += width
    return chunks, ready, frontal


def split_kernel(*refs):
    values, (high_ref, low_ref) = refs[:-2], refs[-2:]
    for at, value_ref in enumerate(values):
        value = value_ref[...]
        depth = value.shape[0]
        start = (pl.program_id(0) * len(values) + at) * depth
        rows = pl.ds(pl.multiple_of(start, depth), depth)
        high = value.astype(jnp.bfloat16)
        high_ref[rows, :] = high
        low_ref[rows, :] = (value - high.astype(jnp.float32)).astype(jnp.bfloat16)


def split(value):
    rows, order = value.shape
    depth, streams = LEAF // 2, 4
    blocks = [
        pl.BlockSpec((depth, order), lambda i, at=at: (i * streams + at, 0)) for at in range(streams)
    ]
    value = pltpu.with_memory_space_constraint(value, pltpu.HBM)
    return pl.pallas_call(
        split_kernel,
        out_shape=[pltpu.VMEM((rows, order), jnp.bfloat16)] * 2,
        grid=(rows // depth // streams,),
        in_specs=blocks,
        out_specs=[pl.BlockSpec(memory_space=pltpu.VMEM)] * 2,
        compiler_params=pltpu.CompilerParams(vmem_limit_bytes=10 * 2**20),
        cost_estimate=pl.CostEstimate(
            flops=4 * rows * order, bytes_accessed=8 * rows * order, transcendentals=0
        ),
        name="split",
    )(*[value] * streams)


def convert(place_ref, pieces, high, low):
    parts = len(ORDERS)
    depth = pieces[0].shape[1]
    for part, masks in enumerate(ORDERS):
        for at, (mask_0, mask_1) in enumerate(zip(origins(0, masks), origins(1, masks))):
            source = pieces[part + parts * (at // 8)]
            mask = jnp.where(place_ref[2] == 0, mask_0, mask_1)
            block = jnp.bitwise_xor(place_ref[0], mask)
            start = pl.multiple_of((block * parts + part) * depth, depth)
            value = source[at % 8]
            top = value.astype(jnp.bfloat16)
            high[pl.ds(start, depth), :] = top
            low[pl.ds(start, depth), :] = (value - top.astype(jnp.float32)).astype(jnp.bfloat16)


def multiply(place_ref, core, a_high, a_low, high, low, total, out_ref):
    left = a_high[:, core].reshape(-1, high.shape[0])
    low_left = a_low[:, core].reshape(-1, high.shape[0])
    right = high[...]
    total[...] = jnp.dot(
        jnp.concatenate([left, left, low_left], 1),
        jnp.concatenate([right, low[...], right], 0),
        preferred_element_type=jnp.float32,
    ).reshape(total.shape)
    orders = zip((0, SECOND, FIRST, FIRST ^ SECOND), (0, FIRST, SECOND, FIRST ^ SECOND))
    for at, masks in enumerate(orders):
        chip = jnp.bitwise_xor(place_ref[1], jnp.where(core == 0, *masks))
        out_ref[at] = total[chip]


def other_kernel(place_ref, a_high, a_low, *refs):
    pieces = refs[: 2 * len(ORDERS)]
    out_ref, high, low, total = refs[2 * len(ORDERS) :]
    convert(place_ref, pieces, high, low)
    multiply(place_ref, 1 - place_ref[2], a_high, a_low, high, low, total, out_ref)


def own_kernel(place_ref, a_high, a_low, high, low, out_ref, total):
    multiply(place_ref, place_ref[2], a_high, a_low, high, low, total, out_ref)


def product(kernel, place, halves, arrays, outs, cost, name):
    in_vmem = pl.BlockSpec(memory_space=pltpu.VMEM)
    halves = [pltpu.with_memory_space_constraint(half, pltpu.VMEM) for half in halves]
    return pl.pallas_call(
        kernel,
        out_shape=outs,
        in_specs=[pl.BlockSpec(memory_space=pltpu.SMEM)] + [in_vmem] * (2 + len(arrays)),
        out_specs=[in_vmem] * len(outs),
        scratch_shapes=[pltpu.VMEM(outs[0].shape, jnp.float32)],
        compiler_params=pltpu.CompilerParams(vmem_limit_bytes=8 * 2**20),
        cost_estimate=pl.CostEstimate(flops=cost, bytes_accessed=cost // 400, transcendentals=0),
        name=name,
    )(place, *halves, *arrays)


def product_other(halves, pieces, place, last):
    leaves, _, leaf, order = halves[0].shape
    width = pieces[0].shape[-1]
    outs = [jax.ShapeDtypeStruct((leaves, leaf, width), jnp.float32)]
    outs += [jax.ShapeDtypeStruct((order, width), jnp.bfloat16)] * 2
    cost = 6 * leaves * leaf * order * width if last else 1
    return product(other_kernel, place, halves, pieces, outs, cost, "product_other")


def product_own(halves, sketch, place, last):
    leaves, _, leaf, order = halves[0].shape
    width = sketch[0].shape[-1]
    outs = [jax.ShapeDtypeStruct((leaves, leaf, width), jnp.float32)]
    cost = 6 * leaves * leaf * order * width if last else 1
    return product(own_kernel, place, halves, sketch, outs, cost, "product_own")[0]


def from_x(value, step):
    pairs = []
    for column in range(2 * SIDE):
        mask = ORDERS[column % 2][step]
        pairs.append((column, column ^ (2 * mask)))
    return lax.ppermute(value, "col", pairs)


def sum_over_x(core_sum):
    kept = from_x(core_sum[2:], 0)
    second = core_sum[1] + kept[1]
    return [core_sum[0], kept[0], from_x(second, 1)], second


BLOCK = 8
NODES = 3


def lane_of(value, lane):
    return jnp.broadcast_to(value[:, lane : lane + 1], value.shape)


def invert_pivot(entry):
    def at(i, j):
        return entry[max(i, j)][min(i, j)]

    def put(i, j, value):
        entry[max(i, j)][min(i, j)] = value

    for p in range(0, BLOCK, 2):
        q = p + 1
        a, b, c = at(p, p), at(q, p), at(q, q)
        scale = 1.0 / (a * c - b * b)
        w_pp, w_pq, w_qq = c * scale, -b * scale, a * scale
        rest = [i for i in range(BLOCK) if i not in (p, q)]
        first = {i: at(i, p) for i in rest}
        second = {i: at(i, q) for i in rest}
        left = {i: w_pp * first[i] + w_pq * second[i] for i in rest}
        right = {i: w_pq * first[i] + w_qq * second[i] for i in rest}
        for i in rest:
            for j in rest:
                if j <= i:
                    put(i, j, at(i, j) - (left[i] * first[j] + right[i] * second[j]))
        for i in rest:
            put(i, p, left[i])
            put(i, q, right[i])
        put(p, p, -w_pp)
        put(q, p, -w_pq)
        put(q, q, -w_qq)
    return at


def sweep(tiles, rows_scratch, new_scratch):
    lanes = lax.broadcasted_iota(jnp.int32, (BLOCK, 128), 1)
    count = KMAX // BLOCK
    for block in range(count):
        at_lane = block * BLOCK
        slot = block % 2
        inside = (lanes >= at_lane) & (lanes < at_lane + BLOCK)
        for node in range(NODES):
            rows_scratch[slot, node * BLOCK : (node + 1) * BLOCK, :] = tiles[node][block]
        rows = [rows_scratch[slot, pl.ds(k, BLOCK, stride=BLOCK), :] for k in range(BLOCK)]
        entry = [[lane_of(rows[k], at_lane + i) for i in range(k + 1)] for k in range(BLOCK)]
        at = invert_pivot(entry)
        wide = [
            jnp.where(lanes == at_lane + k, 1.0, jnp.where(inside, 0.0, -rows[k]))
            for k in range(BLOCK)
        ]
        for k in range(BLOCK):
            total = at(k, 0) * wide[0]
            for i in range(1, BLOCK):
                total = total + at(k, i) * wide[i]
            new_scratch[slot, pl.ds(k, BLOCK, stride=BLOCK), :] = total
        for node in range(NODES):
            new_rows = [
                jnp.broadcast_to(
                    new_scratch[slot, node * BLOCK + k : node * BLOCK + k + 1, :], (BLOCK, 128)
                )
                for k in range(BLOCK)
            ]
            for t in range(count):
                if t == block:
                    continue
                old = tiles[node][t]
                value = jnp.where(inside, 0.0, old)
                for k in range(BLOCK):
                    value = value - lane_of(old, at_lane + k) * new_rows[k]
                tiles[node][t] = value
            tiles[node][block] = new_scratch[slot, node * BLOCK : (node + 1) * BLOCK, :]
    return tiles


def invert_all(matrices, rows_scratch, new_scratch):
    count = KMAX // BLOCK
    lanes = lax.broadcasted_iota(jnp.int32, (BLOCK, 128), 1)
    sublanes = lax.broadcasted_iota(jnp.int32, (BLOCK, 128), 0)
    rows_scratch[...] = jnp.zeros_like(rows_scratch)
    all_tiles, all_down, all_across = [], [], []
    for matrix in matrices:
        wide = jnp.concatenate([matrix, jnp.zeros((KMAX, 128 - KMAX), jnp.float32)], 1)
        tiles = [wide[t * BLOCK : (t + 1) * BLOCK] for t in range(count)]
        on_diagonal = [
            jnp.where(lanes == sublanes + t * BLOCK, tiles[t], 0.0) for t in range(count)
        ]
        down = [lax.rsqrt(jnp.sum(part, axis=1, keepdims=True)) for part in on_diagonal]
        line = functools.reduce(jnp.add, on_diagonal)
        line = jnp.sum(line, axis=0, keepdims=True)
        across = lax.rsqrt(jnp.where(lanes[:1] < KMAX, line, 1.0))
        all_tiles.append([tiles[t] * down[t] * across for t in range(count)])
        all_down.append(down)
        all_across.append(across)
    all_tiles = sweep(all_tiles, rows_scratch, new_scratch)
    inverses = []
    for tiles, down, across in zip(all_tiles, all_down, all_across):
        scaled = [-(tiles[t] * down[t] * across) for t in range(count)]
        inverses.append(jnp.concatenate(scaled, 0)[:, :KMAX])
    return inverses


def select_rows(source, pivots_ref, node, rank, target, target_at):
    for row in range(KMAX):
        picked = source[pl.ds(pivots_ref[node, row], 1), :]
        target[target_at + row : target_at + row + 1, :] = jnp.where(row < rank, picked, 0.0)


def rank_of(info_ref, ranks_ref, level):
    place = info_ref[0] // 2**level
    starts = [0, LEAVES, LEAVES + LEAVES // 2]
    return ranks_ref[starts[level] + place]


def leaf_kernel(info_ref, ranks_ref, pivots_ref, *refs):
    parts, (rows_ref, skeleton_ref) = refs[:-2], refs[-2:]
    rows_ref[...] = functools.reduce(jnp.add, [part[...] for part in parts])
    select_rows(rows_ref, pivots_ref, 0, rank_of(info_ref, ranks_ref, 0), skeleton_ref, 0)


def mid_kernel(info_ref, ranks_ref, pivots_ref, own_ref, other_ref, rows_ref, skeleton_ref):
    own_at = pl.multiple_of((info_ref[0] % 2) * KMAX, KMAX)
    other_at = pl.multiple_of((1 - info_ref[0] % 2) * KMAX, KMAX)
    rows_ref[pl.ds(own_at, KMAX), :] = own_ref[...]
    rows_ref[pl.ds(other_at, KMAX), :] = other_ref[...]
    select_rows(rows_ref, pivots_ref, 1, rank_of(info_ref, ranks_ref, 1), skeleton_ref, 0)


def top_kernel(info_ref, ranks_ref, pivots_ref, *refs):
    chunks = len(WIDTHS)
    groups = [refs[5 * chunk : 5 * chunk + 5] for chunk in range(chunks)]
    leaf_out, mid_out, top_out, rows_out = refs[5 * chunks : 5 * chunks + 4]
    scratch = refs[5 * chunks + 4 :]
    tops, chosen, (rows_scratch, new_scratch) = (
        scratch[:chunks], scratch[chunks : 2 * chunks], scratch[2 * chunks :]
    )
    own_at = pl.multiple_of((info_ref[0] // 2 % 2) * KMAX, KMAX)
    other_at = pl.multiple_of((1 - info_ref[0] // 2 % 2) * KMAX, KMAX)
    start = 0
    for group, top, skeleton in zip(groups, tops, chosen):
        top[pl.ds(own_at, KMAX), :] = group[3][...]
        top[pl.ds(other_at, KMAX), :] = group[4][...]
        select_rows(top, pivots_ref, 2, rank_of(info_ref, ranks_ref, 2), skeleton, 0)
        width = skeleton.shape[-1]
        rows_out[:, start : start + width] = skeleton[...]
        start += width
    row_ids = lax.broadcasted_iota(jnp.int32, (KMAX, KMAX), 0)
    column_ids = lax.broadcasted_iota(jnp.int32, (KMAX, KMAX), 1)
    dot = functools.partial(
        lax.dot_general,
        dimension_numbers=(((1,), (1,)), ((), ())),
        precision=lax.Precision.HIGHEST,
        preferred_element_type=jnp.float32,
    )
    levels = (
        ([group[0] for group in groups], [group[1] for group in groups]),
        ([group[2] for group in groups], [group[3] for group in groups]),
        (tops, chosen),
    )
    grams, crosses = [], []
    for node, (rows, skeletons) in enumerate(levels):
        gram = functools.reduce(jnp.add, [dot(part[...], part[...]) for part in skeletons])
        cross = functools.reduce(
            jnp.add, [dot(row[...], part[...]) for row, part in zip(rows, skeletons)]
        )
        empty = (row_ids == column_ids) & (row_ids >= rank_of(info_ref, ranks_ref, node))
        grams.append(gram * (1.0 / SAMPLES) + jnp.where(empty, 1.0, 0.0))
        crosses.append(cross * (1.0 / SAMPLES))
    inverses = invert_all(grams, rows_scratch, new_scratch)
    for inverse, cross, out in zip(inverses, crosses, (leaf_out, mid_out, top_out)):
        out[...] = dot(inverse, cross)


def vmem_call(kernel, outs, scratch, name):
    in_vmem = pl.BlockSpec(memory_space=pltpu.VMEM)

    def call(info, ranks, pivots, *arrays):
        return pl.pallas_call(
            kernel,
            out_shape=[jax.ShapeDtypeStruct(shape, jnp.float32) for shape in outs],
            in_specs=[pl.BlockSpec(memory_space=pltpu.SMEM)] * 3 + [in_vmem] * len(arrays),
            out_specs=[in_vmem] * len(outs),
            scratch_shapes=scratch,
            compiler_params=pltpu.CompilerParams(vmem_limit_bytes=6 * 2**20),
            name=name,
        )(info, ranks, pivots, *arrays)

    return call


def on_device(
    frontal, sketch, leaf_ranks, leaf_pivots, mid_ranks, mid_pivots, top_ranks, top_pivots
):
    col_count = lax.axis_size("col")
    col_index = lax.axis_index("col")
    row_index = lax.axis_index("row")
    leaf_index = row_index * col_count + col_index
    place = jnp.stack([row_index, col_index // 2, col_index % 2]).astype(jnp.int32)
    nodes = (leaf_index, leaf_index // 2, leaf_index // 4)

    def prepare(*tables):
        ranks = jnp.concatenate(tables[:3])
        pivots = [pick_entry(table, node)[:KMAX] for table, node in zip(tables[3:], nodes)]
        return ranks, jnp.stack(pivots)

    tables = (leaf_ranks, mid_ranks, top_ranks, leaf_pivots, mid_pivots, top_pivots)
    chunks, (ranks, pivots), frontal = gather_parts(sketch, frontal, tables, prepare)
    info = jnp.stack([leaf_index]).astype(jnp.int32)
    halves = [part.reshape(SIDE, 2, LEAF, -1) for part in split(frontal)]
    groups, core_sum, ready = [], None, ()
    for chunk, pieces in enumerate(chunks):
        last = chunk == len(chunks) - 1
        if core_sum is not None:
            place, core_sum = lax.optimization_barrier((place, core_sum))
            group, ready = sum_over_x(core_sum)
            groups.append(group)
        other, *parts = product_other(halves, pieces, place, last)
        received = from_partner(other, "col", 0)
        place, ready = lax.optimization_barrier((place, ready))
        core_sum = product_own(halves, parts, place, last) + received
    groups.append(sum_over_x(core_sum)[0])
    arrays = []
    for group, width in zip(groups, WIDTHS):
        skeleton_shape, pair_shape = (KMAX, width), (2 * KMAX, width)
        rows, skeleton = vmem_call(
            leaf_kernel, [(LEAF, width), skeleton_shape], [], "leaf_rows"
        )(info, ranks, pivots, *group)
        mid_rows, mid_skeleton = vmem_call(
            mid_kernel, [pair_shape, skeleton_shape], [], "mid_rows"
        )(info, ranks, pivots, skeleton, from_partner(skeleton, "col", 0))
        arrays += [rows, skeleton, mid_rows, mid_skeleton, from_partner(mid_skeleton, "col", 1)]
    scratch = [pltpu.VMEM((2 * KMAX, width), jnp.float32) for width in WIDTHS]
    scratch += [pltpu.VMEM((KMAX, width), jnp.float32) for width in WIDTHS]
    scratch += [pltpu.VMEM((2, BLOCK * BLOCK, 128), jnp.float32)] * 2
    outs = vmem_call(
        top_kernel,
        [(KMAX, LEAF), (KMAX, 2 * KMAX), (KMAX, 2 * KMAX), (KMAX, SAMPLES)],
        scratch,
        "interpolation",
    )(info, ranks, pivots, *arrays)
    return tuple(out[None] for out in outs)


def solution(mesh):
    return jax.shard_map(
        on_device,
        mesh=mesh,
        in_specs=(P("row", "col"), P(("col", "row"), None), P(), P(), P(), P(), P(), P()),
        out_specs=(
            P(("row", "col"), None, None),
            P(("row", "col"), None, None),
            P(("row", "col"), None, None),
            P(("row", "col"), None, None),
        ),
        check_vma=False,
    )
```

```python
import functools

import jax
import jax.numpy as jnp
from jax import lax
from jax.experimental import pallas as pl
from jax.experimental.pallas import tpu as pltpu
from jax.sharding import PartitionSpec as P

SAMPLES = 512
KMAX = 96
SIDE = 4
LEAF = 128
LEAVES = 128
WIDTHS = (256, 256)


def from_partner(value, axis, apart):
    mask = 2**apart
    pairs = [(source, source ^ mask) for source in range(lax.axis_size(axis))]
    return lax.ppermute(value, axis, pairs)


def pick_entry(table, position):
    return lax.dynamic_index_in_dim(table, position, 0, keepdims=False)


FIRST, SECOND = 1, 3
ORDERS = ((FIRST, SECOND), (SECOND, FIRST))


def row_mask(core, step, masks):
    along_y = (step < 2) == (core == 0)
    return masks[step % 2] * SIDE if along_y else masks[step % 2]


def from_row(value, step, masks):
    columns = 2 * SIDE
    pairs = []
    for row in range(SIDE * SIDE):
        for column in range(columns):
            partner = row ^ row_mask(column % 2, step, masks)
            pairs.append((row * columns + column, partner * columns + column))
    return lax.ppermute(value, ("row", "col"), pairs)


def origins(core, masks):
    found = [0]
    for step in range(4):
        found += [mask ^ row_mask(core, step, masks) for mask in found]
    return found


def gather_parts(sketch, frontal, before, after):
    depth = sketch.shape[0] // len(ORDERS)
    stacks = [sketch[None, part * depth : (part + 1) * depth] for part in range(len(ORDERS))]
    for step in range(3):
        received = [from_row(stack, step, masks) for stack, masks in zip(stacks, ORDERS)]
        if step == 1:
            received, before = lax.optimization_barrier((received, before))
        if step < 2:
            stacks = [jnp.concatenate(pair, 0) for pair in zip(stacks, received)]
    stacks, received, ready, frontal = lax.optimization_barrier(
        (stacks, received, after(*before), frontal)
    )
    chunks, start = [], 0
    for width in WIDTHS:
        columns = slice(start, start + width)
        own = [
            jnp.concatenate([stack[:, :, columns], other[:, :, columns]], 0)
            for stack, other in zip(stacks, received)
        ]
        chunks.append(own + [from_row(value, 3, masks) for value, masks in zip(own, ORDERS)])
        start += width
    return chunks, ready, frontal


def split_kernel(*refs):
    values, (high_ref, low_ref) = refs[:-2], refs[-2:]
    for at, value_ref in enumerate(values):
        value = value_ref[...]
        depth = value.shape[0]
        start = (pl.program_id(0) * len(values) + at) * depth
        rows = pl.ds(pl.multiple_of(start, depth), depth)
        high = value.astype(jnp.bfloat16)
        high_ref[rows, :] = high
        low_ref[rows, :] = (value - high.astype(jnp.float32)).astype(jnp.bfloat16)


def split(value):
    rows, order = value.shape
    depth, streams = LEAF // 2, 4
    blocks = [
        pl.BlockSpec((depth, order), lambda i, at=at: (i * streams + at, 0)) for at in range(streams)
    ]
    value = pltpu.with_memory_space_constraint(value, pltpu.HBM)
    return pl.pallas_call(
        split_kernel,
        out_shape=[pltpu.VMEM((rows, order), jnp.bfloat16)] * 2,
        grid=(rows // depth // streams,),
        in_specs=blocks,
        out_specs=[pl.BlockSpec(memory_space=pltpu.VMEM)] * 2,
        compiler_params=pltpu.CompilerParams(vmem_limit_bytes=10 * 2**20),
        cost_estimate=pl.CostEstimate(
            flops=4 * rows * order, bytes_accessed=8 * rows * order, transcendentals=0
        ),
        name="split",
    )(*[value] * streams)


def convert(place_ref, pieces, high, low):
    parts = len(ORDERS)
    depth = pieces[0].shape[1]
    for part, masks in enumerate(ORDERS):
        for at, (mask_0, mask_1) in enumerate(zip(origins(0, masks), origins(1, masks))):
            source = pieces[part + parts * (at // 8)]
            mask = jnp.where(place_ref[2] == 0, mask_0, mask_1)
            block = jnp.bitwise_xor(place_ref[0], mask)
            start = pl.multiple_of((block * parts + part) * depth, depth)
            value = source[at % 8]
            top = value.astype(jnp.bfloat16)
            high[pl.ds(start, depth), :] = top
            low[pl.ds(start, depth), :] = (value - top.astype(jnp.float32)).astype(jnp.bfloat16)


def multiply(place_ref, core, a_high, a_low, high, low, total, out_ref):
    left = a_high[:, core].reshape(-1, high.shape[0])
    low_left = a_low[:, core].reshape(-1, high.shape[0])
    right = high[...]
    total[...] = jnp.dot(
        jnp.concatenate([left, left, low_left], 1),
        jnp.concatenate([right, low[...], right], 0),
        preferred_element_type=jnp.float32,
    ).reshape(total.shape)
    orders = zip((0, SECOND, FIRST, FIRST ^ SECOND), (0, FIRST, SECOND, FIRST ^ SECOND))
    for at, masks in enumerate(orders):
        chip = jnp.bitwise_xor(place_ref[1], jnp.where(core == 0, *masks))
        out_ref[at] = total[chip]


def other_kernel(place_ref, a_high, a_low, *refs):
    pieces = refs[: 2 * len(ORDERS)]
    out_ref, high, low, total = refs[2 * len(ORDERS) :]
    convert(place_ref, pieces, high, low)
    multiply(place_ref, 1 - place_ref[2], a_high, a_low, high, low, total, out_ref)


def own_kernel(place_ref, a_high, a_low, high, low, out_ref, total):
    multiply(place_ref, place_ref[2], a_high, a_low, high, low, total, out_ref)


def product(kernel, place, halves, arrays, outs, cost, name):
    in_vmem = pl.BlockSpec(memory_space=pltpu.VMEM)
    halves = [pltpu.with_memory_space_constraint(half, pltpu.VMEM) for half in halves]
    return pl.pallas_call(
        kernel,
        out_shape=outs,
        in_specs=[pl.BlockSpec(memory_space=pltpu.SMEM)] + [in_vmem] * (2 + len(arrays)),
        out_specs=[in_vmem] * len(outs),
        scratch_shapes=[pltpu.VMEM(outs[0].shape, jnp.float32)],
        compiler_params=pltpu.CompilerParams(vmem_limit_bytes=8 * 2**20),
        cost_estimate=pl.CostEstimate(flops=cost, bytes_accessed=cost // 400, transcendentals=0),
        name=name,
    )(place, *halves, *arrays)


def product_other(halves, pieces, place, last):
    leaves, _, leaf, order = halves[0].shape
    width = pieces[0].shape[-1]
    outs = [jax.ShapeDtypeStruct((leaves, leaf, width), jnp.float32)]
    outs += [jax.ShapeDtypeStruct((order, width), jnp.bfloat16)] * 2
    cost = 6 * leaves * leaf * order * width if last else 1
    return product(other_kernel, place, halves, pieces, outs, cost, "product_other")


def product_own(halves, sketch, place, last):
    leaves, _, leaf, order = halves[0].shape
    width = sketch[0].shape[-1]
    outs = [jax.ShapeDtypeStruct((leaves, leaf, width), jnp.float32)]
    cost = 6 * leaves * leaf * order * width if last else 1
    return product(own_kernel, place, halves, sketch, outs, cost, "product_own")[0]


def from_x(value, step):
    pairs = []
    for column in range(2 * SIDE):
        mask = ORDERS[column % 2][step]
        pairs.append((column, column ^ (2 * mask)))
    return lax.ppermute(value, "col", pairs)


def sum_over_x(core_sum):
    kept = from_x(core_sum[2:], 0)
    second = core_sum[1] + kept[1]
    return [core_sum[0], kept[0], from_x(second, 1)], second


BLOCK = 8
NODES = 3


def lane_of(value, lane):
    return jnp.broadcast_to(value[:, lane : lane + 1], value.shape)


def invert_pivot(entry):
    def at(i, j):
        return entry[max(i, j)][min(i, j)]

    def put(i, j, value):
        entry[max(i, j)][min(i, j)] = value

    for p in range(0, BLOCK, 2):
        q = p + 1
        a, b, c = at(p, p), at(q, p), at(q, q)
        scale = 1.0 / (a * c - b * b)
        w_pp, w_pq, w_qq = c * scale, -b * scale, a * scale
        rest = [i for i in range(BLOCK) if i not in (p, q)]
        first = {i: at(i, p) for i in rest}
        second = {i: at(i, q) for i in rest}
        left = {i: w_pp * first[i] + w_pq * second[i] for i in rest}
        right = {i: w_pq * first[i] + w_qq * second[i] for i in rest}
        for i in rest:
            for j in rest:
                if j <= i:
                    put(i, j, at(i, j) - (left[i] * first[j] + right[i] * second[j]))
        for i in rest:
            put(i, p, left[i])
            put(i, q, right[i])
        put(p, p, -w_pp)
        put(q, p, -w_pq)
        put(q, q, -w_qq)
    return at


def sweep(tiles, rows_scratch, new_scratch):
    lanes = lax.broadcasted_iota(jnp.int32, (BLOCK, 128), 1)
    count = KMAX // BLOCK
    for block in range(count):
        at_lane = block * BLOCK
        slot = block % 2
        inside = (lanes >= at_lane) & (lanes < at_lane + BLOCK)
        for node in range(NODES):
            rows_scratch[slot, node * BLOCK : (node + 1) * BLOCK, :] = tiles[node][block]
        rows = [rows_scratch[slot, pl.ds(k, BLOCK, stride=BLOCK), :] for k in range(BLOCK)]
        entry = [[lane_of(rows[k], at_lane + i) for i in range(k + 1)] for k in range(BLOCK)]
        at = invert_pivot(entry)
        wide = [
            jnp.where(lanes == at_lane + k, 1.0, jnp.where(inside, 0.0, -rows[k]))
            for k in range(BLOCK)
        ]
        for k in range(BLOCK):
            total = at(k, 0) * wide[0]
            for i in range(1, BLOCK):
                total = total + at(k, i) * wide[i]
            new_scratch[slot, pl.ds(k, BLOCK, stride=BLOCK), :] = total
        for node in range(NODES):
            new_rows = [
                jnp.broadcast_to(
                    new_scratch[slot, node * BLOCK + k : node * BLOCK + k + 1, :], (BLOCK, 128)
                )
                for k in range(BLOCK)
            ]
            for t in range(count):
                if t == block:
                    continue
                old = tiles[node][t]
                value = jnp.where(inside, 0.0, old)
                for k in range(BLOCK):
                    value = value - lane_of(old, at_lane + k) * new_rows[k]
                tiles[node][t] = value
            tiles[node][block] = new_scratch[slot, node * BLOCK : (node + 1) * BLOCK, :]
    return tiles


def invert_all(matrices, rows_scratch, new_scratch):
    count = KMAX // BLOCK
    lanes = lax.broadcasted_iota(jnp.int32, (BLOCK, 128), 1)
    sublanes = lax.broadcasted_iota(jnp.int32, (BLOCK, 128), 0)
    rows_scratch[...] = jnp.zeros_like(rows_scratch)
    all_tiles, all_down, all_across = [], [], []
    for matrix in matrices:
        wide = jnp.concatenate([matrix, jnp.zeros((KMAX, 128 - KMAX), jnp.float32)], 1)
        tiles = [wide[t * BLOCK : (t + 1) * BLOCK] for t in range(count)]
        on_diagonal = [
            jnp.where(lanes == sublanes + t * BLOCK, tiles[t], 0.0) for t in range(count)
        ]
        down = [lax.rsqrt(jnp.sum(part, axis=1, keepdims=True)) for part in on_diagonal]
        line = functools.reduce(jnp.add, on_diagonal)
        line = jnp.sum(line, axis=0, keepdims=True)
        across = lax.rsqrt(jnp.where(lanes[:1] < KMAX, line, 1.0))
        all_tiles.append([tiles[t] * down[t] * across for t in range(count)])
        all_down.append(down)
        all_across.append(across)
    all_tiles = sweep(all_tiles, rows_scratch, new_scratch)
    inverses = []
    for tiles, down, across in zip(all_tiles, all_down, all_across):
        scaled = [-(tiles[t] * down[t] * across) for t in range(count)]
        inverses.append(jnp.concatenate(scaled, 0)[:, :KMAX])
    return inverses


def select_rows(source, pivots_ref, node, rank, target, target_at):
    for row in range(KMAX):
        picked = source[pl.ds(pivots_ref[node, row], 1), :]
        target[target_at + row : target_at + row + 1, :] = jnp.where(row < rank, picked, 0.0)


def rank_of(info_ref, ranks_ref, level):
    place = info_ref[0] // 2**level
    starts = [0, LEAVES, LEAVES + LEAVES // 2]
    return ranks_ref[starts[level] + place]


def leaf_kernel(info_ref, ranks_ref, pivots_ref, *refs):
    parts, (rows_ref, skeleton_ref) = refs[:-2], refs[-2:]
    rows_ref[...] = functools.reduce(jnp.add, [part[...] for part in parts])
    select_rows(rows_ref, pivots_ref, 0, rank_of(info_ref, ranks_ref, 0), skeleton_ref, 0)


def mid_kernel(info_ref, ranks_ref, pivots_ref, own_ref, other_ref, rows_ref, skeleton_ref):
    own_at = pl.multiple_of((info_ref[0] % 2) * KMAX, KMAX)
    other_at = pl.multiple_of((1 - info_ref[0] % 2) * KMAX, KMAX)
    rows_ref[pl.ds(own_at, KMAX), :] = own_ref[...]
    rows_ref[pl.ds(other_at, KMAX), :] = other_ref[...]
    select_rows(rows_ref, pivots_ref, 1, rank_of(info_ref, ranks_ref, 1), skeleton_ref, 0)


def dot_rows(left, right):
    return lax.dot_general(
        left,
        right,
        (((1,), (1,)), ((), ())),
        precision=lax.Precision.HIGHEST,
        preferred_element_type=jnp.float32,
    )


def lower_kernel(*refs):
    arrays, outs = refs[: 4 * len(WIDTHS)], refs[4 * len(WIDTHS) :]
    for node in range(2):
        pairs = [arrays[4 * chunk + 2 * node :][:2] for chunk in range(len(WIDTHS))]
        grams = [dot_rows(skeleton[...], skeleton[...]) for _, skeleton in pairs]
        crosses = [dot_rows(rows[...], skeleton[...]) for rows, skeleton in pairs]
        outs[2 * node][...] = functools.reduce(jnp.add, grams)
        outs[2 * node + 1][...] = functools.reduce(jnp.add, crosses)


def select_top(info_ref, ranks_ref, pivots_ref, own_ref, cousin_ref, rows, skeleton):
    own_at = pl.multiple_of((info_ref[0] // 2 % 2) * KMAX, KMAX)
    other_at = pl.multiple_of((1 - info_ref[0] // 2 % 2) * KMAX, KMAX)
    rows[pl.ds(own_at, KMAX), :] = own_ref[...]
    rows[pl.ds(other_at, KMAX), :] = cousin_ref[...]
    select_rows(rows, pivots_ref, 2, rank_of(info_ref, ranks_ref, 2), skeleton, 0)
    chosen = skeleton[...]
    return dot_rows(chosen, chosen), dot_rows(rows[...], chosen)


def upper_kernel(
    info_ref, ranks_ref, pivots_ref, own_ref, cousin_ref, skeleton_ref, gram_ref, cross_ref, rows
):
    gram_ref[...], cross_ref[...] = select_top(
        info_ref, ranks_ref, pivots_ref, own_ref, cousin_ref, rows, skeleton_ref
    )


def top_kernel(
    info_ref, ranks_ref, pivots_ref, leaf_gram, leaf_cross, mid_gram, mid_cross, first_skeleton,
    top_gram, top_cross, own_ref, cousin_ref, leaf_out, mid_out, top_out, rows_out, rows, skeleton,
    rows_scratch, new_scratch,
):
    gram, cross = select_top(
        info_ref, ranks_ref, pivots_ref, own_ref, cousin_ref, rows, skeleton
    )
    rows_out[:, : WIDTHS[0]] = first_skeleton[...]
    rows_out[:, WIDTHS[0] :] = skeleton[...]
    row_ids = lax.broadcasted_iota(jnp.int32, (KMAX, KMAX), 0)
    column_ids = lax.broadcasted_iota(jnp.int32, (KMAX, KMAX), 1)
    grams = []
    sums = (leaf_gram[...], mid_gram[...], top_gram[...] + gram)
    for node, total in enumerate(sums):
        empty = (row_ids == column_ids) & (row_ids >= rank_of(info_ref, ranks_ref, node))
        grams.append(total * (1.0 / SAMPLES) + jnp.where(empty, 1.0, 0.0))
    inverses = invert_all(grams, rows_scratch, new_scratch)
    crosses = (leaf_cross[...], mid_cross[...], top_cross[...] + cross)
    for inverse, total, out in zip(inverses, crosses, (leaf_out, mid_out, top_out)):
        out[...] = dot_rows(inverse, total * (1.0 / SAMPLES))


def vmem_call(kernel, outs, scratch, name):
    in_vmem = pl.BlockSpec(memory_space=pltpu.VMEM)

    def call(tables, *arrays):
        return pl.pallas_call(
            kernel,
            out_shape=[jax.ShapeDtypeStruct(shape, jnp.float32) for shape in outs],
            in_specs=[pl.BlockSpec(memory_space=pltpu.SMEM)] * len(tables) + [in_vmem] * len(arrays),
            out_specs=[in_vmem] * len(outs),
            scratch_shapes=scratch,
            compiler_params=pltpu.CompilerParams(vmem_limit_bytes=6 * 2**20),
            name=name,
        )(*tables, *arrays)

    return call


def on_device(
    frontal, sketch, leaf_ranks, leaf_pivots, mid_ranks, mid_pivots, top_ranks, top_pivots
):
    col_count = lax.axis_size("col")
    col_index = lax.axis_index("col")
    row_index = lax.axis_index("row")
    leaf_index = row_index * col_count + col_index
    place = jnp.stack([row_index, col_index // 2, col_index % 2]).astype(jnp.int32)
    nodes = (leaf_index, leaf_index // 2, leaf_index // 4)

    def prepare(*tables):
        ranks = jnp.concatenate(tables[:3])
        pivots = [pick_entry(table, node)[:KMAX] for table, node in zip(tables[3:], nodes)]
        return ranks, jnp.stack(pivots)

    tables = (leaf_ranks, mid_ranks, top_ranks, leaf_pivots, mid_pivots, top_pivots)
    chunks, (ranks, pivots), frontal = gather_parts(sketch, frontal, tables, prepare)
    info = jnp.stack([leaf_index]).astype(jnp.int32)
    halves = [part.reshape(SIDE, 2, LEAF, -1) for part in split(frontal)]
    groups, core_sum, ready = [], None, ()
    for chunk, pieces in enumerate(chunks):
        last = chunk == len(chunks) - 1
        if core_sum is not None:
            place, core_sum = lax.optimization_barrier((place, core_sum))
            group, ready = sum_over_x(core_sum)
            groups.append(group)
        other, *parts = product_other(halves, pieces, place, last)
        received = from_partner(other, "col", 0)
        place, ready = lax.optimization_barrier((place, ready))
        core_sum = product_own(halves, parts, place, last) + received
    core_sum, groups = lax.optimization_barrier((core_sum, groups))
    groups.append(sum_over_x(core_sum)[0])
    tables = (info, ranks, pivots)
    arrays, tops = [], []
    for group, width in zip(groups, WIDTHS):
        skeleton_shape, pair_shape = (KMAX, width), (2 * KMAX, width)
        rows, skeleton = vmem_call(
            leaf_kernel, [(LEAF, width), skeleton_shape], [], "leaf_rows"
        )(tables, *group)
        mid_rows, mid_skeleton = vmem_call(
            mid_kernel, [pair_shape, skeleton_shape], [], "mid_rows"
        )(tables, skeleton, from_partner(skeleton, "col", 0))
        arrays += [rows, skeleton, mid_rows, mid_skeleton]
        tops.append((mid_skeleton, from_partner(mid_skeleton, "col", 1)))
    square, leaf_cross, pair_cross = (KMAX, KMAX), (LEAF, KMAX), (2 * KMAX, KMAX)
    lower = vmem_call(
        lower_kernel, [square, leaf_cross, square, pair_cross], [], "lower_sums"
    )((), *arrays)
    first = vmem_call(
        upper_kernel,
        [(KMAX, WIDTHS[0]), square, pair_cross],
        [pltpu.VMEM((2 * KMAX, WIDTHS[0]), jnp.float32)],
        "upper_sums",
    )(tables, *tops[0])
    scratch = [pltpu.VMEM((rows, WIDTHS[1]), jnp.float32) for rows in (2 * KMAX, KMAX)]
    scratch += [pltpu.VMEM((2, BLOCK * BLOCK, 128), jnp.float32)] * 2
    outs = vmem_call(
        top_kernel,
        [(KMAX, LEAF), (KMAX, 2 * KMAX), (KMAX, 2 * KMAX), (KMAX, SAMPLES)],
        scratch,
        "interpolation",
    )(tables, *lower, *first, *tops[1])
    return tuple(out[None] for out in outs)


def solution(mesh):
    return jax.shard_map(
        on_device,
        mesh=mesh,
        in_specs=(P("row", "col"), P(("col", "row"), None), P(), P(), P(), P(), P(), P()),
        out_specs=(
            P(("row", "col"), None, None),
            P(("row", "col"), None, None),
            P(("row", "col"), None, None),
            P(("row", "col"), None, None),
        ),
        check_vma=False,
    )
```

```python
import functools

import jax
import jax.numpy as jnp
from jax import lax
from jax.experimental import pallas as pl
from jax.experimental.pallas import tpu as pltpu
from jax.sharding import PartitionSpec as P

SAMPLES = 512
KMAX = 96
SIDE = 4
LEAF = 128
LEAVES = 128
WIDTHS = (256, 256)


def from_partner(value, axis, apart):
    mask = 2**apart
    pairs = [(source, source ^ mask) for source in range(lax.axis_size(axis))]
    return lax.ppermute(value, axis, pairs)


def pick_entry(table, position):
    return lax.dynamic_index_in_dim(table, position, 0, keepdims=False)


FIRST, SECOND = 1, 3
ORDERS = ((FIRST, SECOND), (SECOND, FIRST))


def row_mask(core, step, masks):
    along_y = (step < 2) == (core == 0)
    return masks[step % 2] * SIDE if along_y else masks[step % 2]


def from_row(value, step, masks):
    columns = 2 * SIDE
    pairs = []
    for row in range(SIDE * SIDE):
        for column in range(columns):
            partner = row ^ row_mask(column % 2, step, masks)
            pairs.append((row * columns + column, partner * columns + column))
    return lax.ppermute(value, ("row", "col"), pairs)


def origins(core, masks):
    found = [0]
    for step in range(4):
        found += [mask ^ row_mask(core, step, masks) for mask in found]
    return found


def gather_parts(sketch, frontal, before, after):
    depth = sketch.shape[0] // len(ORDERS)
    stacks = [sketch[None, part * depth : (part + 1) * depth] for part in range(len(ORDERS))]
    for step in range(3):
        received = [from_row(stack, step, masks) for stack, masks in zip(stacks, ORDERS)]
        if step == 1:
            received, before = lax.optimization_barrier((received, before))
        if step < 2:
            stacks = [jnp.concatenate(pair, 0) for pair in zip(stacks, received)]
    stacks, received, ready, frontal = lax.optimization_barrier(
        (stacks, received, after(*before), frontal)
    )
    chunks, start = [], 0
    for width in WIDTHS:
        columns = slice(start, start + width)
        own = [
            jnp.concatenate([stack[:, :, columns], other[:, :, columns]], 0)
            for stack, other in zip(stacks, received)
        ]
        chunks.append(own + [from_row(value, 3, masks) for value, masks in zip(own, ORDERS)])
        start += width
    return chunks, ready, frontal


def split_kernel(*refs):
    values, (high_ref, low_ref) = refs[:-2], refs[-2:]
    for at, value_ref in enumerate(values):
        value = value_ref[...]
        depth = value.shape[0]
        start = (pl.program_id(0) * len(values) + at) * depth
        rows = pl.ds(pl.multiple_of(start, depth), depth)
        high = value.astype(jnp.bfloat16)
        high_ref[rows, :] = high
        low_ref[rows, :] = (value - high.astype(jnp.float32)).astype(jnp.bfloat16)


def split(value):
    rows, order = value.shape
    depth, streams = LEAF // 2, 4
    blocks = [
        pl.BlockSpec((depth, order), lambda i, at=at: (i * streams + at, 0)) for at in range(streams)
    ]
    value = pltpu.with_memory_space_constraint(value, pltpu.HBM)
    return pl.pallas_call(
        split_kernel,
        out_shape=[pltpu.VMEM((rows, order), jnp.bfloat16)] * 2,
        grid=(rows // depth // streams,),
        in_specs=blocks,
        out_specs=[pl.BlockSpec(memory_space=pltpu.VMEM)] * 2,
        compiler_params=pltpu.CompilerParams(vmem_limit_bytes=10 * 2**20),
        cost_estimate=pl.CostEstimate(
            flops=4 * rows * order, bytes_accessed=8 * rows * order, transcendentals=0
        ),
        name="split",
    )(*[value] * streams)


def convert(place_ref, pieces, high, low, received):
    depth = pieces[0].shape[1]
    count = pieces[0].shape[0]
    for part, masks in enumerate(ORDERS):
        found = list(zip(origins(0, masks), origins(1, masks)))
        for at, (mask_0, mask_1) in enumerate(found[count:] if received else found[:count]):
            mask = jnp.where(place_ref[2] == 0, mask_0, mask_1)
            block = jnp.bitwise_xor(place_ref[0], mask)
            start = pl.multiple_of((block * len(ORDERS) + part) * depth, depth)
            value = pieces[part][at]
            top = value.astype(jnp.bfloat16)
            high[pl.ds(start, depth), :] = top
            low[pl.ds(start, depth), :] = (value - top.astype(jnp.float32)).astype(jnp.bfloat16)


def early_kernel(place_ref, *refs):
    parts = len(ORDERS)
    for chunk in range(len(WIDTHS)):
        high, low = refs[parts * len(WIDTHS) + 2 * chunk :][:2]
        convert(place_ref, refs[parts * chunk :][:parts], high, low, False)


def convert_early(own, order, place):
    in_vmem = pl.BlockSpec(memory_space=pltpu.VMEM)
    outs = [pltpu.VMEM((order, width), jnp.bfloat16) for width in WIDTHS for _ in range(2)]
    return pl.pallas_call(
        early_kernel,
        out_shape=outs,
        in_specs=[pl.BlockSpec(memory_space=pltpu.SMEM)] + [in_vmem] * len(own),
        out_specs=[in_vmem] * len(outs),
        compiler_params=pltpu.CompilerParams(vmem_limit_bytes=8 * 2**20),
        cost_estimate=pl.CostEstimate(flops=1, bytes_accessed=1, transcendentals=0),
        name="convert_early",
    )(place, *own)


def multiply(place_ref, core, a_high, a_low, high, low, total, out_ref):
    left = a_high[:, core].reshape(-1, high.shape[0])
    low_left = a_low[:, core].reshape(-1, high.shape[0])
    right = high[...]
    total[...] = jnp.dot(
        jnp.concatenate([left, left, low_left], 1),
        jnp.concatenate([right, low[...], right], 0),
        preferred_element_type=jnp.float32,
    ).reshape(total.shape)
    orders = zip((0, SECOND, FIRST, FIRST ^ SECOND), (0, FIRST, SECOND, FIRST ^ SECOND))
    for at, masks in enumerate(orders):
        chip = jnp.bitwise_xor(place_ref[1], jnp.where(core == 0, *masks))
        out_ref[at] = total[chip]


def other_kernel(place_ref, a_high, a_low, *refs):
    parts = len(ORDERS)
    pieces = refs[:parts]
    out_ref, high, low, total = refs[parts + 2 :]
    convert(place_ref, pieces, high, low, True)
    multiply(place_ref, 1 - place_ref[2], a_high, a_low, high, low, total, out_ref)


def own_kernel(place_ref, a_high, a_low, high, low, out_ref, total):
    multiply(place_ref, place_ref[2], a_high, a_low, high, low, total, out_ref)


def product(kernel, place, halves, arrays, outs, cost, name, aliases):
    in_vmem = pl.BlockSpec(memory_space=pltpu.VMEM)
    halves = [pltpu.with_memory_space_constraint(half, pltpu.VMEM) for half in halves]
    return pl.pallas_call(
        kernel,
        out_shape=outs,
        in_specs=[pl.BlockSpec(memory_space=pltpu.SMEM)] + [in_vmem] * (2 + len(arrays)),
        out_specs=[in_vmem] * len(outs),
        scratch_shapes=[pltpu.VMEM(outs[0].shape, jnp.float32)],
        input_output_aliases=aliases,
        compiler_params=pltpu.CompilerParams(vmem_limit_bytes=8 * 2**20),
        cost_estimate=pl.CostEstimate(flops=cost, bytes_accessed=cost // 400, transcendentals=0),
        name=name,
    )(place, *halves, *arrays)


def product_other(halves, pieces, place, last):
    leaves, _, leaf, order = halves[0].shape
    width = pieces[0].shape[-1]
    outs = [jax.ShapeDtypeStruct((leaves, leaf, width), jnp.float32)]
    outs += [pltpu.VMEM((order, width), jnp.bfloat16)] * 2
    at = 3 + len(ORDERS)
    cost = 6 * leaves * leaf * order * width if last else 1
    return product(
        other_kernel, place, halves, pieces, outs, cost, "product_other", {at: 1, at + 1: 2}
    )


def product_own(halves, sketch, place, last):
    leaves, _, leaf, order = halves[0].shape
    width = sketch[0].shape[-1]
    outs = [jax.ShapeDtypeStruct((leaves, leaf, width), jnp.float32)]
    cost = 6 * leaves * leaf * order * width if last else 1
    return product(own_kernel, place, halves, sketch, outs, cost, "product_own", {})[0]


def from_x(value, step):
    pairs = []
    for column in range(2 * SIDE):
        mask = ORDERS[column % 2][step]
        pairs.append((column, column ^ (2 * mask)))
    return lax.ppermute(value, "col", pairs)


def sum_over_x(core_sum):
    kept = from_x(core_sum[2:], 0)
    second = core_sum[1] + kept[1]
    return [core_sum[0], kept[0], from_x(second, 1)], second


BLOCK = 8
NODES = 3


def lane_of(value, lane):
    return jnp.broadcast_to(value[:, lane : lane + 1], value.shape)


def invert_pivot(entry):
    def at(i, j):
        return entry[max(i, j)][min(i, j)]

    def put(i, j, value):
        entry[max(i, j)][min(i, j)] = value

    for p in range(0, BLOCK, 2):
        q = p + 1
        a, b, c = at(p, p), at(q, p), at(q, q)
        scale = 1.0 / (a * c - b * b)
        w_pp, w_pq, w_qq = c * scale, -b * scale, a * scale
        rest = [i for i in range(BLOCK) if i not in (p, q)]
        first = {i: at(i, p) for i in rest}
        second = {i: at(i, q) for i in rest}
        left = {i: w_pp * first[i] + w_pq * second[i] for i in rest}
        right = {i: w_pq * first[i] + w_qq * second[i] for i in rest}
        for i in rest:
            for j in rest:
                if j <= i:
                    put(i, j, at(i, j) - (left[i] * first[j] + right[i] * second[j]))
        for i in rest:
            put(i, p, left[i])
            put(i, q, right[i])
        put(p, p, -w_pp)
        put(q, p, -w_pq)
        put(q, q, -w_qq)
    return at


def sweep(tiles, rows_scratch, new_scratch):
    lanes = lax.broadcasted_iota(jnp.int32, (BLOCK, 128), 1)
    count = KMAX // BLOCK
    for block in range(count):
        at_lane = block * BLOCK
        slot = block % 2
        inside = (lanes >= at_lane) & (lanes < at_lane + BLOCK)
        for node in range(NODES):
            rows_scratch[slot, node * BLOCK : (node + 1) * BLOCK, :] = tiles[node][block]
        rows = [rows_scratch[slot, pl.ds(k, BLOCK, stride=BLOCK), :] for k in range(BLOCK)]
        entry = [[lane_of(rows[k], at_lane + i) for i in range(k + 1)] for k in range(BLOCK)]
        at = invert_pivot(entry)
        wide = [
            jnp.where(lanes == at_lane + k, 1.0, jnp.where(inside, 0.0, -rows[k]))
            for k in range(BLOCK)
        ]
        for k in range(BLOCK):
            total = at(k, 0) * wide[0]
            for i in range(1, BLOCK):
                total = total + at(k, i) * wide[i]
            new_scratch[slot, pl.ds(k, BLOCK, stride=BLOCK), :] = total
        for node in range(NODES):
            new_rows = [
                jnp.broadcast_to(
                    new_scratch[slot, node * BLOCK + k : node * BLOCK + k + 1, :], (BLOCK, 128)
                )
                for k in range(BLOCK)
            ]
            for t in range(count):
                if t == block:
                    continue
                old = tiles[node][t]
                value = jnp.where(inside, 0.0, old)
                for k in range(BLOCK):
                    value = value - lane_of(old, at_lane + k) * new_rows[k]
                tiles[node][t] = value
            tiles[node][block] = new_scratch[slot, node * BLOCK : (node + 1) * BLOCK, :]
    return tiles


def invert_all(matrices, rows_scratch, new_scratch):
    count = KMAX // BLOCK
    lanes = lax.broadcasted_iota(jnp.int32, (BLOCK, 128), 1)
    sublanes = lax.broadcasted_iota(jnp.int32, (BLOCK, 128), 0)
    rows_scratch[...] = jnp.zeros_like(rows_scratch)
    all_tiles, all_down, all_across = [], [], []
    for matrix in matrices:
        wide = jnp.concatenate([matrix, jnp.zeros((KMAX, 128 - KMAX), jnp.float32)], 1)
        tiles = [wide[t * BLOCK : (t + 1) * BLOCK] for t in range(count)]
        on_diagonal = [
            jnp.where(lanes == sublanes + t * BLOCK, tiles[t], 0.0) for t in range(count)
        ]
        down = [lax.rsqrt(jnp.sum(part, axis=1, keepdims=True)) for part in on_diagonal]
        line = functools.reduce(jnp.add, on_diagonal)
        line = jnp.sum(line, axis=0, keepdims=True)
        across = lax.rsqrt(jnp.where(lanes[:1] < KMAX, line, 1.0))
        all_tiles.append([tiles[t] * down[t] * across for t in range(count)])
        all_down.append(down)
        all_across.append(across)
    all_tiles = sweep(all_tiles, rows_scratch, new_scratch)
    inverses = []
    for tiles, down, across in zip(all_tiles, all_down, all_across):
        scaled = [-(tiles[t] * down[t] * across) for t in range(count)]
        inverses.append(jnp.concatenate(scaled, 0)[:, :KMAX])
    return inverses


def select_rows(source, pivots_ref, node, rank, target, target_at):
    for row in range(KMAX):
        picked = source[pl.ds(pivots_ref[node, row], 1), :]
        target[target_at + row : target_at + row + 1, :] = jnp.where(row < rank, picked, 0.0)


def rank_of(info_ref, ranks_ref, level):
    place = info_ref[0] // 2**level
    starts = [0, LEAVES, LEAVES + LEAVES // 2]
    return ranks_ref[starts[level] + place]


def leaf_kernel(info_ref, ranks_ref, pivots_ref, *refs):
    parts, (rows_ref, skeleton_ref) = refs[:-2], refs[-2:]
    rows_ref[...] = functools.reduce(jnp.add, [part[...] for part in parts])
    select_rows(rows_ref, pivots_ref, 0, rank_of(info_ref, ranks_ref, 0), skeleton_ref, 0)


def mid_kernel(info_ref, ranks_ref, pivots_ref, own_ref, other_ref, rows_ref, skeleton_ref):
    own_at = pl.multiple_of((info_ref[0] % 2) * KMAX, KMAX)
    other_at = pl.multiple_of((1 - info_ref[0] % 2) * KMAX, KMAX)
    rows_ref[pl.ds(own_at, KMAX), :] = own_ref[...]
    rows_ref[pl.ds(other_at, KMAX), :] = other_ref[...]
    select_rows(rows_ref, pivots_ref, 1, rank_of(info_ref, ranks_ref, 1), skeleton_ref, 0)


def top_kernel(info_ref, ranks_ref, pivots_ref, *refs):
    chunks = len(WIDTHS)
    groups = [refs[5 * chunk : 5 * chunk + 5] for chunk in range(chunks)]
    leaf_out, mid_out, top_out, rows_out = refs[5 * chunks : 5 * chunks + 4]
    scratch = refs[5 * chunks + 4 :]
    tops, chosen, (rows_scratch, new_scratch) = (
        scratch[:chunks], scratch[chunks : 2 * chunks], scratch[2 * chunks :]
    )
    own_at = pl.multiple_of((info_ref[0] // 2 % 2) * KMAX, KMAX)
    other_at = pl.multiple_of((1 - info_ref[0] // 2 % 2) * KMAX, KMAX)
    start = 0
    for group, top, skeleton in zip(groups, tops, chosen):
        top[pl.ds(own_at, KMAX), :] = group[3][...]
        top[pl.ds(other_at, KMAX), :] = group[4][...]
        select_rows(top, pivots_ref, 2, rank_of(info_ref, ranks_ref, 2), skeleton, 0)
        width = skeleton.shape[-1]
        rows_out[:, start : start + width] = skeleton[...]
        start += width
    row_ids = lax.broadcasted_iota(jnp.int32, (KMAX, KMAX), 0)
    column_ids = lax.broadcasted_iota(jnp.int32, (KMAX, KMAX), 1)
    dot = functools.partial(
        lax.dot_general,
        dimension_numbers=(((1,), (1,)), ((), ())),
        precision=lax.Precision.HIGHEST,
        preferred_element_type=jnp.float32,
    )
    levels = (
        ([group[0] for group in groups], [group[1] for group in groups]),
        ([group[2] for group in groups], [group[3] for group in groups]),
        (tops, chosen),
    )
    grams, crosses = [], []
    for node, (rows, skeletons) in enumerate(levels):
        gram = functools.reduce(jnp.add, [dot(part[...], part[...]) for part in skeletons])
        cross = functools.reduce(
            jnp.add, [dot(row[...], part[...]) for row, part in zip(rows, skeletons)]
        )
        empty = (row_ids == column_ids) & (row_ids >= rank_of(info_ref, ranks_ref, node))
        grams.append(gram * (1.0 / SAMPLES) + jnp.where(empty, 1.0, 0.0))
        crosses.append(cross * (1.0 / SAMPLES))
    inverses = invert_all(grams, rows_scratch, new_scratch)
    for inverse, cross, out in zip(inverses, crosses, (leaf_out, mid_out, top_out)):
        out[...] = dot(inverse, cross)


def vmem_call(kernel, outs, scratch, name):
    in_vmem = pl.BlockSpec(memory_space=pltpu.VMEM)

    def call(info, ranks, pivots, *arrays):
        return pl.pallas_call(
            kernel,
            out_shape=[jax.ShapeDtypeStruct(shape, jnp.float32) for shape in outs],
            in_specs=[pl.BlockSpec(memory_space=pltpu.SMEM)] * 3 + [in_vmem] * len(arrays),
            out_specs=[in_vmem] * len(outs),
            scratch_shapes=scratch,
            compiler_params=pltpu.CompilerParams(vmem_limit_bytes=6 * 2**20),
            name=name,
        )(info, ranks, pivots, *arrays)

    return call


def on_device(
    frontal, sketch, leaf_ranks, leaf_pivots, mid_ranks, mid_pivots, top_ranks, top_pivots
):
    col_count = lax.axis_size("col")
    col_index = lax.axis_index("col")
    row_index = lax.axis_index("row")
    leaf_index = row_index * col_count + col_index
    place = jnp.stack([row_index, col_index // 2, col_index % 2]).astype(jnp.int32)
    nodes = (leaf_index, leaf_index // 2, leaf_index // 4)

    def prepare(*tables):
        ranks = jnp.concatenate(tables[:3])
        pivots = [pick_entry(table, node)[:KMAX] for table, node in zip(tables[3:], nodes)]
        return ranks, jnp.stack(pivots)

    tables = (leaf_ranks, mid_ranks, top_ranks, leaf_pivots, mid_pivots, top_pivots)
    chunks, (ranks, pivots), frontal = gather_parts(sketch, frontal, tables, prepare)
    info = jnp.stack([leaf_index]).astype(jnp.int32)
    halves = [part.reshape(SIDE, 2, LEAF, -1) for part in split(frontal)]
    parts = len(ORDERS)
    own = [piece for pieces in chunks for piece in pieces[:parts]]
    own, halves = lax.optimization_barrier((own, halves))
    early = convert_early(own, halves[0].shape[-1], place)
    chunks = [
        [*pieces[parts:], *early[2 * chunk : 2 * chunk + 2]] for chunk, pieces in enumerate(chunks)
    ]
    groups, core_sum, ready = [], None, ()
    for chunk, pieces in enumerate(chunks):
        last = chunk == len(chunks) - 1
        if core_sum is not None:
            place, core_sum = lax.optimization_barrier((place, core_sum))
            group, ready = sum_over_x(core_sum)
            groups.append(group)
        other, *converted = product_other(halves, pieces, place, last)
        received = from_partner(other, "col", 0)
        place, ready = lax.optimization_barrier((place, ready))
        core_sum = product_own(halves, converted, place, last) + received
    groups.append(sum_over_x(core_sum)[0])
    arrays = []
    for group, width in zip(groups, WIDTHS):
        skeleton_shape, pair_shape = (KMAX, width), (2 * KMAX, width)
        rows, skeleton = vmem_call(
            leaf_kernel, [(LEAF, width), skeleton_shape], [], "leaf_rows"
        )(info, ranks, pivots, *group)
        mid_rows, mid_skeleton = vmem_call(
            mid_kernel, [pair_shape, skeleton_shape], [], "mid_rows"
        )(info, ranks, pivots, skeleton, from_partner(skeleton, "col", 0))
        arrays += [rows, skeleton, mid_rows, mid_skeleton, from_partner(mid_skeleton, "col", 1)]
    scratch = [pltpu.VMEM((2 * KMAX, width), jnp.float32) for width in WIDTHS]
    scratch += [pltpu.VMEM((KMAX, width), jnp.float32) for width in WIDTHS]
    scratch += [pltpu.VMEM((2, BLOCK * BLOCK, 128), jnp.float32)] * 2
    outs = vmem_call(
        top_kernel,
        [(KMAX, LEAF), (KMAX, 2 * KMAX), (KMAX, 2 * KMAX), (KMAX, SAMPLES)],
        scratch,
        "interpolation",
    )(info, ranks, pivots, *arrays)
    return tuple(out[None] for out in outs)


def solution(mesh):
    return jax.shard_map(
        on_device,
        mesh=mesh,
        in_specs=(P("row", "col"), P(("col", "row"), None), P(), P(), P(), P(), P(), P()),
        out_specs=(
            P(("row", "col"), None, None),
            P(("row", "col"), None, None),
            P(("row", "col"), None, None),
            P(("row", "col"), None, None),
        ),
        check_vma=False,
    )
```

```python
import functools

import jax
import jax.numpy as jnp
from jax import lax
from jax.experimental import pallas as pl
from jax.experimental.pallas import tpu as pltpu
from jax.sharding import PartitionSpec as P

SAMPLES = 512
KMAX = 96
SIDE = 4
LEAF = 128
LEAVES = 128
WIDTHS = (256, 256)


def from_partner(value, axis, apart):
    mask = 2**apart
    pairs = [(source, source ^ mask) for source in range(lax.axis_size(axis))]
    return lax.ppermute(value, axis, pairs)


def pick_entry(table, position):
    return lax.dynamic_index_in_dim(table, position, 0, keepdims=False)


FIRST, SECOND = 1, 3
ORDERS = ((FIRST, SECOND), (SECOND, FIRST))


def row_mask(core, step, masks):
    along_y = (step < 2) == (core == 0)
    return masks[step % 2] * SIDE if along_y else masks[step % 2]


def from_row(value, step, masks):
    columns = 2 * SIDE
    pairs = []
    for row in range(SIDE * SIDE):
        for column in range(columns):
            partner = row ^ row_mask(column % 2, step, masks)
            pairs.append((row * columns + column, partner * columns + column))
    return lax.ppermute(value, ("row", "col"), pairs)


def origins(core, masks):
    found = [0]
    for step in range(4):
        found += [mask ^ row_mask(core, step, masks) for mask in found]
    return found


def gather_parts(sketch, frontal, before, after):
    depth = sketch.shape[0] // len(ORDERS)
    stacks = [sketch[None, part * depth : (part + 1) * depth] for part in range(len(ORDERS))]
    for step in range(3):
        received = [from_row(stack, step, masks) for stack, masks in zip(stacks, ORDERS)]
        if step == 1:
            received, before = lax.optimization_barrier((received, before))
        if step < 2:
            stacks = [jnp.concatenate(pair, 0) for pair in zip(stacks, received)]
    stacks, received, ready, frontal = lax.optimization_barrier(
        (stacks, received, after(*before), frontal)
    )
    chunks, start = [], 0
    for width in WIDTHS:
        columns = slice(start, start + width)
        own = [
            jnp.concatenate([stack[:, :, columns], other[:, :, columns]], 0)
            for stack, other in zip(stacks, received)
        ]
        chunks.append(own + [from_row(value, 3, masks) for value, masks in zip(own, ORDERS)])
        start += width
    return chunks, ready, frontal


def split_kernel(*refs):
    values, (high_ref, low_ref) = refs[:-2], refs[-2:]
    for at, value_ref in enumerate(values):
        value = value_ref[...]
        depth = value.shape[0]
        start = (pl.program_id(0) * len(values) + at) * depth
        rows = pl.ds(pl.multiple_of(start, depth), depth)
        high = value.astype(jnp.bfloat16)
        high_ref[rows, :] = high
        low_ref[rows, :] = (value - high.astype(jnp.float32)).astype(jnp.bfloat16)


def split(value):
    rows, order = value.shape
    depth, streams = LEAF // 2, 4
    blocks = [
        pl.BlockSpec((depth, order), lambda i, at=at: (i * streams + at, 0)) for at in range(streams)
    ]
    value = pltpu.with_memory_space_constraint(value, pltpu.HBM)
    return pl.pallas_call(
        split_kernel,
        out_shape=[pltpu.VMEM((rows, order), jnp.bfloat16)] * 2,
        grid=(rows // depth // streams,),
        in_specs=blocks,
        out_specs=[pl.BlockSpec(memory_space=pltpu.VMEM)] * 2,
        compiler_params=pltpu.CompilerParams(vmem_limit_bytes=10 * 2**20),
        cost_estimate=pl.CostEstimate(
            flops=4 * rows * order, bytes_accessed=8 * rows * order, transcendentals=0
        ),
        name="split",
    )(*[value] * streams)


def convert(place_ref, pieces, high, low, received):
    depth = pieces[0].shape[1]
    count = pieces[0].shape[0]
    for part, masks in enumerate(ORDERS):
        found = list(zip(origins(0, masks), origins(1, masks)))
        for at, (mask_0, mask_1) in enumerate(found[count:] if received else found[:count]):
            mask = jnp.where(place_ref[2] == 0, mask_0, mask_1)
            block = jnp.bitwise_xor(place_ref[0], mask)
            start = pl.multiple_of((block * len(ORDERS) + part) * depth, depth)
            value = pieces[part][at]
            top = value.astype(jnp.bfloat16)
            high[pl.ds(start, depth), :] = top
            low[pl.ds(start, depth), :] = (value - top.astype(jnp.float32)).astype(jnp.bfloat16)


def early_kernel(place_ref, *refs):
    parts = len(ORDERS)
    for chunk in range(len(WIDTHS)):
        high, low = refs[parts * len(WIDTHS) + 2 * chunk :][:2]
        convert(place_ref, refs[parts * chunk :][:parts], high, low, False)


def convert_early(own, order, place):
    in_vmem = pl.BlockSpec(memory_space=pltpu.VMEM)
    outs = [pltpu.VMEM((order, width), jnp.bfloat16) for width in WIDTHS for _ in range(2)]
    return pl.pallas_call(
        early_kernel,
        out_shape=outs,
        in_specs=[pl.BlockSpec(memory_space=pltpu.SMEM)] + [in_vmem] * len(own),
        out_specs=[in_vmem] * len(outs),
        compiler_params=pltpu.CompilerParams(vmem_limit_bytes=8 * 2**20),
        cost_estimate=pl.CostEstimate(flops=1, bytes_accessed=1, transcendentals=0),
        name="convert_early",
    )(place, *own)


def multiply(place_ref, core, a_high, a_low, high, low, total, out_ref):
    left = a_high[:, core].reshape(-1, high.shape[0])
    low_left = a_low[:, core].reshape(-1, high.shape[0])
    right = high[...]
    total[...] = jnp.dot(
        jnp.concatenate([left, left, low_left], 1),
        jnp.concatenate([right, low[...], right], 0),
        preferred_element_type=jnp.float32,
    ).reshape(total.shape)
    orders = zip((0, SECOND, FIRST, FIRST ^ SECOND), (0, FIRST, SECOND, FIRST ^ SECOND))
    for at, masks in enumerate(orders):
        chip = jnp.bitwise_xor(place_ref[1], jnp.where(core == 0, *masks))
        out_ref[at] = total[chip]


def other_kernel(place_ref, a_high, a_low, *refs):
    parts = len(ORDERS)
    pieces = refs[:parts]
    out_ref, high, low, total = refs[parts + 2 :]
    convert(place_ref, pieces, high, low, True)
    multiply(place_ref, 1 - place_ref[2], a_high, a_low, high, low, total, out_ref)


def own_kernel(place_ref, a_high, a_low, high, low, out_ref, total):
    multiply(place_ref, place_ref[2], a_high, a_low, high, low, total, out_ref)


def product(kernel, place, halves, arrays, outs, cost, name, aliases):
    in_vmem = pl.BlockSpec(memory_space=pltpu.VMEM)
    halves = [pltpu.with_memory_space_constraint(half, pltpu.VMEM) for half in halves]
    return pl.pallas_call(
        kernel,
        out_shape=outs,
        in_specs=[pl.BlockSpec(memory_space=pltpu.SMEM)] + [in_vmem] * (2 + len(arrays)),
        out_specs=[in_vmem] * len(outs),
        scratch_shapes=[pltpu.VMEM(outs[0].shape, jnp.float32)],
        input_output_aliases=aliases,
        compiler_params=pltpu.CompilerParams(vmem_limit_bytes=8 * 2**20),
        cost_estimate=pl.CostEstimate(flops=cost, bytes_accessed=cost // 400, transcendentals=0),
        name=name,
    )(place, *halves, *arrays)


def product_other(halves, pieces, place, last):
    leaves, _, leaf, order = halves[0].shape
    width = pieces[0].shape[-1]
    outs = [jax.ShapeDtypeStruct((leaves, leaf, width), jnp.float32)]
    outs += [pltpu.VMEM((order, width), jnp.bfloat16)] * 2
    at = 3 + len(ORDERS)
    cost = 6 * leaves * leaf * order * width if last else 1
    return product(
        other_kernel, place, halves, pieces, outs, cost, "product_other", {at: 1, at + 1: 2}
    )


def product_own(halves, sketch, place, last):
    leaves, _, leaf, order = halves[0].shape
    width = sketch[0].shape[-1]
    outs = [jax.ShapeDtypeStruct((leaves, leaf, width), jnp.float32)]
    cost = 6 * leaves * leaf * order * width if last else 1
    return product(own_kernel, place, halves, sketch, outs, cost, "product_own", {})[0]


def from_x(value, step):
    pairs = []
    for column in range(2 * SIDE):
        mask = ORDERS[column % 2][step]
        pairs.append((column, column ^ (2 * mask)))
    return lax.ppermute(value, "col", pairs)


def sum_over_x(core_sum):
    kept = from_x(core_sum[2:], 0)
    second = core_sum[1] + kept[1]
    return [core_sum[0], kept[0], from_x(second, 1)], second


BLOCK = 8
NODES = 3


def lane_of(value, lane):
    return jnp.broadcast_to(value[:, lane : lane + 1], value.shape)


def invert_pivot(entry):
    def at(i, j):
        return entry[max(i, j)][min(i, j)]

    def put(i, j, value):
        entry[max(i, j)][min(i, j)] = value

    for p in range(0, BLOCK, 2):
        q = p + 1
        a, b, c = at(p, p), at(q, p), at(q, q)
        scale = 1.0 / (a * c - b * b)
        w_pp, w_pq, w_qq = c * scale, -b * scale, a * scale
        rest = [i for i in range(BLOCK) if i not in (p, q)]
        first = {i: at(i, p) for i in rest}
        second = {i: at(i, q) for i in rest}
        left = {i: w_pp * first[i] + w_pq * second[i] for i in rest}
        right = {i: w_pq * first[i] + w_qq * second[i] for i in rest}
        for i in rest:
            for j in rest:
                if j <= i:
                    put(i, j, at(i, j) - (left[i] * first[j] + right[i] * second[j]))
        for i in rest:
            put(i, p, left[i])
            put(i, q, right[i])
        put(p, p, -w_pp)
        put(q, p, -w_pq)
        put(q, q, -w_qq)
    return at


def sweep(tiles, rows_scratch, new_scratch):
    lanes = lax.broadcasted_iota(jnp.int32, (BLOCK, 128), 1)
    count = KMAX // BLOCK
    for block in range(count):
        at_lane = block * BLOCK
        slot = block % 2
        inside = (lanes >= at_lane) & (lanes < at_lane + BLOCK)
        for node in range(NODES):
            rows_scratch[slot, node * BLOCK : (node + 1) * BLOCK, :] = tiles[node][block]
        rows = [rows_scratch[slot, pl.ds(k, BLOCK, stride=BLOCK), :] for k in range(BLOCK)]
        entry = [[lane_of(rows[k], at_lane + i) for i in range(k + 1)] for k in range(BLOCK)]
        at = invert_pivot(entry)
        wide = [
            jnp.where(lanes == at_lane + k, 1.0, jnp.where(inside, 0.0, -rows[k]))
            for k in range(BLOCK)
        ]
        for k in range(BLOCK):
            total = at(k, 0) * wide[0]
            for i in range(1, BLOCK):
                total = total + at(k, i) * wide[i]
            new_scratch[slot, pl.ds(k, BLOCK, stride=BLOCK), :] = total
        for node in range(NODES):
            new_rows = [
                jnp.broadcast_to(
                    new_scratch[slot, node * BLOCK + k : node * BLOCK + k + 1, :], (BLOCK, 128)
                )
                for k in range(BLOCK)
            ]
            for t in range(count):
                if t == block:
                    continue
                old = tiles[node][t]
                value = jnp.where(inside, 0.0, old)
                for k in range(BLOCK):
                    value = value - lane_of(old, at_lane + k) * new_rows[k]
                tiles[node][t] = value
            tiles[node][block] = new_scratch[slot, node * BLOCK : (node + 1) * BLOCK, :]
    return tiles


def invert_all(matrices, rows_scratch, new_scratch):
    count = KMAX // BLOCK
    lanes = lax.broadcasted_iota(jnp.int32, (BLOCK, 128), 1)
    sublanes = lax.broadcasted_iota(jnp.int32, (BLOCK, 128), 0)
    rows_scratch[...] = jnp.zeros_like(rows_scratch)
    all_tiles, all_down, all_across = [], [], []
    for matrix in matrices:
        wide = jnp.concatenate([matrix, jnp.zeros((KMAX, 128 - KMAX), jnp.float32)], 1)
        tiles = [wide[t * BLOCK : (t + 1) * BLOCK] for t in range(count)]
        on_diagonal = [
            jnp.where(lanes == sublanes + t * BLOCK, tiles[t], 0.0) for t in range(count)
        ]
        down = [lax.rsqrt(jnp.sum(part, axis=1, keepdims=True)) for part in on_diagonal]
        line = functools.reduce(jnp.add, on_diagonal)
        line = jnp.sum(line, axis=0, keepdims=True)
        across = lax.rsqrt(jnp.where(lanes[:1] < KMAX, line, 1.0))
        all_tiles.append([tiles[t] * down[t] * across for t in range(count)])
        all_down.append(down)
        all_across.append(across)
    all_tiles = sweep(all_tiles, rows_scratch, new_scratch)
    inverses = []
    for tiles, down, across in zip(all_tiles, all_down, all_across):
        scaled = [-(tiles[t] * down[t] * across) for t in range(count)]
        inverses.append(jnp.concatenate(scaled, 0)[:, :KMAX])
    return inverses


def select_rows(source, pivots_ref, node, rank, target, target_at):
    for row in range(KMAX):
        picked = source[pl.ds(pivots_ref[node, row], 1), :]
        target[target_at + row : target_at + row + 1, :] = jnp.where(row < rank, picked, 0.0)


def rank_of(info_ref, ranks_ref, level):
    place = info_ref[0] // 2**level
    starts = [0, LEAVES, LEAVES + LEAVES // 2]
    return ranks_ref[starts[level] + place]


def leaf_kernel(info_ref, ranks_ref, pivots_ref, *refs):
    parts, (rows_ref, skeleton_ref) = refs[:-2], refs[-2:]
    rows_ref[...] = functools.reduce(jnp.add, [part[...] for part in parts])
    select_rows(rows_ref, pivots_ref, 0, rank_of(info_ref, ranks_ref, 0), skeleton_ref, 0)


def mid_kernel(info_ref, ranks_ref, pivots_ref, own_ref, other_ref, rows_ref, skeleton_ref):
    own_at = pl.multiple_of((info_ref[0] % 2) * KMAX, KMAX)
    other_at = pl.multiple_of((1 - info_ref[0] % 2) * KMAX, KMAX)
    rows_ref[pl.ds(own_at, KMAX), :] = own_ref[...]
    rows_ref[pl.ds(other_at, KMAX), :] = other_ref[...]
    select_rows(rows_ref, pivots_ref, 1, rank_of(info_ref, ranks_ref, 1), skeleton_ref, 0)


def dot_rows(left, right):
    return lax.dot_general(
        left,
        right,
        (((1,), (1,)), ((), ())),
        precision=lax.Precision.HIGHEST,
        preferred_element_type=jnp.float32,
    )


def lower_kernel(*refs):
    arrays, outs = refs[: 4 * len(WIDTHS)], refs[4 * len(WIDTHS) :]
    for node in range(2):
        pairs = [arrays[4 * chunk + 2 * node :][:2] for chunk in range(len(WIDTHS))]
        grams = [dot_rows(skeleton[...], skeleton[...]) for _, skeleton in pairs]
        crosses = [dot_rows(rows[...], skeleton[...]) for rows, skeleton in pairs]
        outs[2 * node][...] = functools.reduce(jnp.add, grams)
        outs[2 * node + 1][...] = functools.reduce(jnp.add, crosses)


def select_top(info_ref, ranks_ref, pivots_ref, own_ref, cousin_ref, rows, skeleton):
    own_at = pl.multiple_of((info_ref[0] // 2 % 2) * KMAX, KMAX)
    other_at = pl.multiple_of((1 - info_ref[0] // 2 % 2) * KMAX, KMAX)
    rows[pl.ds(own_at, KMAX), :] = own_ref[...]
    rows[pl.ds(other_at, KMAX), :] = cousin_ref[...]
    select_rows(rows, pivots_ref, 2, rank_of(info_ref, ranks_ref, 2), skeleton, 0)
    chosen = skeleton[...]
    return dot_rows(chosen, chosen), dot_rows(rows[...], chosen)


def upper_kernel(
    info_ref, ranks_ref, pivots_ref, own_ref, cousin_ref, skeleton_ref, gram_ref, cross_ref, rows
):
    gram_ref[...], cross_ref[...] = select_top(
        info_ref, ranks_ref, pivots_ref, own_ref, cousin_ref, rows, skeleton_ref
    )


def top_kernel(
    info_ref, ranks_ref, pivots_ref, leaf_gram, leaf_cross, mid_gram, mid_cross, first_skeleton,
    top_gram, top_cross, own_ref, cousin_ref, leaf_out, mid_out, top_out, rows_out, rows, skeleton,
    rows_scratch, new_scratch,
):
    gram, cross = select_top(
        info_ref, ranks_ref, pivots_ref, own_ref, cousin_ref, rows, skeleton
    )
    rows_out[:, : WIDTHS[0]] = first_skeleton[...]
    rows_out[:, WIDTHS[0] :] = skeleton[...]
    row_ids = lax.broadcasted_iota(jnp.int32, (KMAX, KMAX), 0)
    column_ids = lax.broadcasted_iota(jnp.int32, (KMAX, KMAX), 1)
    grams = []
    sums = (leaf_gram[...], mid_gram[...], top_gram[...] + gram)
    for node, total in enumerate(sums):
        empty = (row_ids == column_ids) & (row_ids >= rank_of(info_ref, ranks_ref, node))
        grams.append(total * (1.0 / SAMPLES) + jnp.where(empty, 1.0, 0.0))
    inverses = invert_all(grams, rows_scratch, new_scratch)
    crosses = (leaf_cross[...], mid_cross[...], top_cross[...] + cross)
    for inverse, total, out in zip(inverses, crosses, (leaf_out, mid_out, top_out)):
        out[...] = dot_rows(inverse, total * (1.0 / SAMPLES))


def vmem_call(kernel, outs, scratch, name):
    in_vmem = pl.BlockSpec(memory_space=pltpu.VMEM)

    def call(tables, *arrays):
        return pl.pallas_call(
            kernel,
            out_shape=[jax.ShapeDtypeStruct(shape, jnp.float32) for shape in outs],
            in_specs=[pl.BlockSpec(memory_space=pltpu.SMEM)] * len(tables) + [in_vmem] * len(arrays),
            out_specs=[in_vmem] * len(outs),
            scratch_shapes=scratch,
            compiler_params=pltpu.CompilerParams(vmem_limit_bytes=6 * 2**20),
            name=name,
        )(*tables, *arrays)

    return call


def on_device(
    frontal, sketch, leaf_ranks, leaf_pivots, mid_ranks, mid_pivots, top_ranks, top_pivots
):
    col_count = lax.axis_size("col")
    col_index = lax.axis_index("col")
    row_index = lax.axis_index("row")
    leaf_index = row_index * col_count + col_index
    place = jnp.stack([row_index, col_index // 2, col_index % 2]).astype(jnp.int32)
    nodes = (leaf_index, leaf_index // 2, leaf_index // 4)

    def prepare(*tables):
        ranks = jnp.concatenate(tables[:3])
        pivots = [pick_entry(table, node)[:KMAX] for table, node in zip(tables[3:], nodes)]
        return ranks, jnp.stack(pivots)

    tables = (leaf_ranks, mid_ranks, top_ranks, leaf_pivots, mid_pivots, top_pivots)
    chunks, (ranks, pivots), frontal = gather_parts(sketch, frontal, tables, prepare)
    info = jnp.stack([leaf_index]).astype(jnp.int32)
    halves = [part.reshape(SIDE, 2, LEAF, -1) for part in split(frontal)]
    parts = len(ORDERS)
    own = [piece for pieces in chunks for piece in pieces[:parts]]
    own, halves = lax.optimization_barrier((own, halves))
    early = convert_early(own, halves[0].shape[-1], place)
    chunks = [
        [*pieces[parts:], *early[2 * chunk : 2 * chunk + 2]] for chunk, pieces in enumerate(chunks)
    ]
    groups, core_sum, ready = [], None, ()
    for chunk, pieces in enumerate(chunks):
        last = chunk == len(chunks) - 1
        if core_sum is not None:
            place, core_sum = lax.optimization_barrier((place, core_sum))
            group, ready = sum_over_x(core_sum)
            groups.append(group)
        other, *converted = product_other(halves, pieces, place, last)
        received = from_partner(other, "col", 0)
        place, ready = lax.optimization_barrier((place, ready))
        core_sum = product_own(halves, converted, place, last) + received
    groups.append(sum_over_x(core_sum)[0])
    tables = (info, ranks, pivots)
    arrays, tops = [], []
    for group, width in zip(groups, WIDTHS):
        skeleton_shape, pair_shape = (KMAX, width), (2 * KMAX, width)
        rows, skeleton = vmem_call(
            leaf_kernel, [(LEAF, width), skeleton_shape], [], "leaf_rows"
        )(tables, *group)
        mid_rows, mid_skeleton = vmem_call(
            mid_kernel, [pair_shape, skeleton_shape], [], "mid_rows"
        )(tables, skeleton, from_partner(skeleton, "col", 0))
        arrays += [rows, skeleton, mid_rows, mid_skeleton]
        tops.append((mid_skeleton, from_partner(mid_skeleton, "col", 1)))
    square, leaf_cross, pair_cross = (KMAX, KMAX), (LEAF, KMAX), (2 * KMAX, KMAX)
    lower = vmem_call(
        lower_kernel, [square, leaf_cross, square, pair_cross], [], "lower_sums"
    )((), *arrays)
    tops[0], lower = lax.optimization_barrier((tops[0], lower))
    first = vmem_call(
        upper_kernel,
        [(KMAX, WIDTHS[0]), square, pair_cross],
        [pltpu.VMEM((2 * KMAX, WIDTHS[0]), jnp.float32)],
        "upper_sums",
    )(tables, *tops[0])
    scratch = [pltpu.VMEM((rows, WIDTHS[1]), jnp.float32) for rows in (2 * KMAX, KMAX)]
    scratch += [pltpu.VMEM((2, BLOCK * BLOCK, 128), jnp.float32)] * 2
    outs = vmem_call(
        top_kernel,
        [(KMAX, LEAF), (KMAX, 2 * KMAX), (KMAX, 2 * KMAX), (KMAX, SAMPLES)],
        scratch,
        "interpolation",
    )(tables, *lower, *first, *tops[1])
    return tuple(out[None] for out in outs)


def solution(mesh):
    return jax.shard_map(
        on_device,
        mesh=mesh,
        in_specs=(P("row", "col"), P(("col", "row"), None), P(), P(), P(), P(), P(), P()),
        out_specs=(
            P(("row", "col"), None, None),
            P(("row", "col"), None, None),
            P(("row", "col"), None, None),
            P(("row", "col"), None, None),
        ),
        check_vma=False,
    )
```
